32 devices in a mesh: dp: 4 (over x, core), seq: 8 (over z, y).
Axes of the slice: x: 2, y: 2, z: 4, core: 2. Of those that a mesh axis runs over, the one named last changes fastest.
Arguments:
- tokens_in: bfloat16 [8, 2048, 1024], P('dp', 'seq'), may hold values from -6 to 6
- lead_hours: int32 [8], P('dp'), may hold values from 6 to 168
- cotangent: bfloat16 [8, 2048, 1024], P('dp', 'seq'), may hold values from -6 to 6
- w_qkv: bfloat16 [1024, 3072], P(('dp', 'seq')), may hold values from -0.1875 to 0.1875
- w_out: bfloat16 [1024, 1024], P(('dp', 'seq')), may hold values from -6 to 6
- w_fc1: bfloat16 [1024, 4096], P(('dp', 'seq')), may hold values from -0.1875 to 0.1875
- w_fc2: bfloat16 [4096, 1024], P(('dp', 'seq')), may hold values from -0.09375 to 0.09375
- ln1_gain: bfloat16 [1024], P(('dp', 'seq')), may hold values from 0.25 to 1.75
- ln1_bias: bfloat16 [1024], P(('dp', 'seq')), may hold values from -3 to 3
- q_bias: bfloat16 [1024], P(('dp', 'seq')), may hold values from -3 to 3
- v_bias: bfloat16 [1024], P(('dp', 'seq')), may hold values from -3 to 3
- out_bias: bfloat16 [1024], P(('dp', 'seq')), may hold values from -3 to 3
- ln2_gain: bfloat16 [1024], P(('dp', 'seq')), may hold values from 0.25 to 1.75
- ln2_bias: bfloat16 [1024], P(('dp', 'seq')), may hold values from -3 to 3
- fc1_bias: bfloat16 [4096], P(('dp', 'seq')), may hold values from -3 to 3
- fc2_bias: bfloat16 [1024], P(('dp', 'seq')), may hold values from -3 to 3
- lead_weight: bfloat16 [1024], P(('dp', 'seq')), may hold values from -4 to 4
- lead_bias: bfloat16 [1024], P(('dp', 'seq')), may hold values from -3 to 3
Outputs:
- block_output: bfloat16 [8, 2048, 1024], P('dp', 'seq')
- input_grad: float32 [8, 2048, 1024], P('dp', 'seq')
- grad_qkv: float32 [1024, 3072], P(('dp', 'seq'))
- grad_out: float32 [1024, 1024], P(('dp', 'seq'))
- grad_fc1: float32 [1024, 4096], P(('dp', 'seq'))
- grad_fc2: float32 [4096, 1024], P(('dp', 'seq'))
- grad_ln1_gain: float32 [1024], P(('dp', 'seq'))
- grad_ln1_bias: float32 [1024], P(('dp', 'seq'))
- grad_q_bias: float32 [1024], P(('dp', 'seq'))
- grad_v_bias: float32 [1024], P(('dp', 'seq'))
- grad_out_bias: float32 [1024], P(('dp', 'seq'))
- grad_ln2_gain: float32 [1024], P(('dp', 'seq'))
- grad_ln2_bias: float32 [1024], P(('dp', 'seq'))
- grad_fc1_bias: float32 [4096], P(('dp', 'seq'))
- grad_fc2_bias: float32 [1024], P(('dp', 'seq'))
- grad_lead_weight: float32 [1024], P(('dp', 'seq'))
- grad_lead_bias: float32 [1024], P(('dp', 'seq'))
The draws below stay inside these ranges and needn't reach their ends.
All inputs are finite; a program needn't handle non-finite values.
Results may differ from the reference program's by a relative error of at most 0.009.
Values may be sent and summed in bfloat16 or wider, within the bound.
A program may use at most 256 MiB of HBM per device.

```python
import jax
import jax.numpy as jnp
from jax import lax

D = 1024
HEADS = 16
FF = 4096
PATCHES = 2048
ITEMS = 8


def with_ends(array, stream_key, smallest, high):
    longest = array.shape.index(max(array.shape))
    spots = []
    for shift in (0, 1):
        where = [jax.random.randint(jax.random.fold_in(stream_key, axis), (), 0, length) for axis, length in enumerate(array.shape)]
        where[longest] = (where[longest] + shift) % array.shape[longest]
        spots.append(tuple(where))
    return array.at[spots[0]].set(smallest).at[spots[1]].set(high)


def block_scale(key, extent, cuts, low, high):
    def one(position, shards_of):
        heights = jax.random.uniform(jax.random.fold_in(jax.random.fold_in(key, 6), position), (shards_of,), jnp.float32, low / len(cuts), high / len(cuts))
        return jnp.repeat(jnp.exp(heights), extent[position] // shards_of).reshape((-1,) + (1,) * (len(extent) - position - 1))

    level = one(*cuts[0])
    for cut in cuts[1:]:
        level = level * one(*cut)
    return level


def normal_values(rng, dims, scale, most, shards=(), dtype=jnp.bfloat16):
    level = block_scale(rng, dims, shards, -0.22, 0.18) if shards else 1.0
    result = jax.random.normal(rng, dims, jnp.float32) * scale * level
    return jnp.minimum(jnp.maximum(result, -most), most).astype(dtype)


def setup_inputs(seed: int = 0) -> dict:
    key_of = jax.random.split(jax.random.key(seed), 19)
    tokens_in = normal_values(key_of[0], (ITEMS, PATCHES, D), 1.0, 6.0, ((0, 4), (1, 8)))
    lead_hours = with_ends(jax.random.randint(key_of[1], (ITEMS,), 6, 169), jax.random.fold_in(key_of[1], 1), 6, 168).astype(jnp.int32)
    cotangent = normal_values(key_of[2], (ITEMS, PATCHES, D), 1.0, 6.0, ((0, 4), (1, 8)))
    w_qkv = normal_values(key_of[3], (D, 3 * D), D ** -0.5, 0.1875, ((0, 32),))
    w_out = normal_values(key_of[4], (D, D), (max(1, 3 * D // PATCHES)) ** -0.5, 6.0, ((0, 32),))
    w_fc1 = normal_values(key_of[5], (D, FF), D ** -0.5, 0.1875, ((0, 32),))
    w_fc2 = normal_values(key_of[6], (FF, D), FF ** -0.5, 0.09375, ((0, 32),))
    ln1_gain = jnp.clip(1.0 + 0.15 * jax.random.normal(key_of[7], (D,), jnp.float32), 0.25, 1.75).astype(jnp.bfloat16)
    ln1_bias = normal_values(key_of[8], (D,), 0.3, 3.0, ((0, 32),))
    q_bias = normal_values(key_of[9], (D,), 0.3, 3.0, ((0, 32),))
    v_bias = normal_values(key_of[10], (D,), 0.5, 3.0, ((0, 32),))
    out_bias = normal_values(key_of[11], (D,), 0.3, 3.0, ((0, 32),))
    ln2_gain = jnp.clip(1.0 + 0.15 * jax.random.normal(key_of[12], (D,), jnp.float32), 0.25, 1.75).astype(jnp.bfloat16)
    ln2_bias = normal_values(key_of[13], (D,), 0.3, 3.0, ((0, 32),))
    fc1_bias = normal_values(key_of[14], (FF,), 0.3, 3.0, ((0, 32),))
    fc2_bias = normal_values(key_of[15], (D,), 0.3, 3.0, ((0, 32),))
    lead_weight = normal_values(key_of[16], (D,), 1.0, 4.0, ((0, 32),))
    lead_bias = normal_values(key_of[17], (D,), 0.5, 3.0, ((0, 32),))
    return {"tokens_in": tokens_in, "lead_hours": lead_hours, "cotangent": cotangent, "w_qkv": w_qkv, "w_out": w_out, "w_fc1": w_fc1, "w_fc2": w_fc2, "ln1_gain": ln1_gain, "ln1_bias": ln1_bias, "q_bias": q_bias, "v_bias": v_bias, "out_bias": out_bias, "ln2_gain": ln2_gain, "ln2_bias": ln2_bias, "fc1_bias": fc1_bias, "fc2_bias": fc2_bias, "lead_weight": lead_weight, "lead_bias": lead_bias}


@jax.custom_vjp
def low(v):
    return lax.optimization_barrier(v.astype(jnp.bfloat16)).astype(jnp.float32)

@jax.custom_vjp
def low_back(v):
    return v

def low_keep(v):
    return (low(v), None)

def low_pass(kept, grad):
    return (grad,)

def back_keep(v):
    return (v, None)

def back_low(kept, grad):
    return (low(grad),)
low.defvjp(low_keep, low_pass)
low_back.defvjp(back_keep, back_low)
epsilon = 1e-06

def norm_rows(values, gain, shift):
    center = values - lax.optimization_barrier(jnp.mean(values, axis=-1, keepdims=True))
    spread = lax.optimization_barrier(jnp.mean(center * center, axis=-1, keepdims=True))
    return center * lax.rsqrt(spread + epsilon) * gain + shift

def high_product(left, right):
    return jnp.dot(left, right, precision=lax.Precision.HIGHEST, preferred_element_type=jnp.float32)

def layer_item(weights, tokens_item, hours_item):
    w_qkv, w_out, w_fc1, w_fc2, ln1_gain, ln1_bias, q_bias, v_bias, out_bias, ln2_gain, ln2_bias, fc1_bias, fc2_bias, lead_weight, lead_bias = weights
    width = tokens_item.shape[-1]
    head_size = width // HEADS
    leading = tokens_item + hours_item.astype(jnp.float32) / 100.0 * lead_weight + lead_bias
    normed = low(norm_rows(leading, ln1_gain, ln1_bias))
    projected = high_product(normed, w_qkv)
    queries = low_back(low(projected[:, :width] + q_bias))
    keys_all = low_back(low(projected[:, width:2 * width]))
    values_all = low_back(low(projected[:, 2 * width:] + v_bias))
    query_heads = queries.reshape(-1, HEADS, head_size)
    key_heads = keys_all.reshape(-1, HEADS, head_size)
    value_heads = values_all.reshape(-1, HEADS, head_size)
    raw = low_back(jnp.einsum('qhd,khd->hqk', query_heads, key_heads, precision=lax.Precision.HIGHEST))
    probs = jax.nn.softmax(raw * head_size ** (-0.5), axis=-1)
    blended = jnp.einsum('hqk,khd->qhd', low(probs), value_heads, precision=lax.Precision.HIGHEST)
    blended = low_back(low(blended.reshape(-1, width)))
    attended = low_back(high_product(blended, w_out) + out_bias)
    middle = leading + attended
    normed2 = low(norm_rows(middle, ln2_gain, ln2_bias))
    hidden = low_back(high_product(normed2, w_fc1) + fc1_bias)
    activated = low(jax.nn.gelu(hidden, approximate=False))
    branch = low_back(high_product(activated, w_fc2) + fc2_bias)
    return middle + branch

def reference(tokens_in, lead_hours, cotangent, w_qkv, w_out, w_fc1, w_fc2, ln1_gain, ln1_bias, q_bias, v_bias, out_bias, ln2_gain, ln2_bias, fc1_bias, fc2_bias, lead_weight, lead_bias):
    weights = tuple((w.astype(jnp.float32) for w in (w_qkv, w_out, w_fc1, w_fc2, ln1_gain, ln1_bias, q_bias, v_bias, out_bias, ln2_gain, ln2_bias, fc1_bias, fc2_bias, lead_weight, lead_bias)))
    tokens_float = tokens_in.astype(jnp.float32)

    def forward(tokens_all, params):
        checked = jax.checkpoint(layer_item)

        def one_item(operands):
            return checked(params, operands[0], operands[1])
        return lax.map(one_item, (tokens_all, lead_hours))
    output, pullback = jax.vjp(forward, tokens_float, weights)
    input_grad, weight_grads = pullback(cotangent.astype(jnp.float32))
    return (output.astype(jnp.bfloat16), input_grad) + tuple(weight_grads)
```

```python
import functools
from functools import partial
import jax, jax.numpy as jnp
from jax import lax
from jax.experimental import pallas as pl
from jax.experimental.pallas import tpu as pltpu
from jax.sharding import PartitionSpec as P

MESH = pl.DeviceIdType.MESH
f32, bf16 = jnp.float32, jnp.bfloat16
LOG2E = 1.4426950408889634
EPS = 1e-06


def dot_nn(a, b):
    return lax.dot_general(a, b, (((1,), (0,)), ((), ())), preferred_element_type=f32)


def dot_nt(a, b):
    return lax.dot_general(a, b, (((1,), (1,)), ((), ())), preferred_element_type=f32)


def rcopy(src, dst, ssem, rsem, dev):
    return pltpu.make_async_remote_copy(src_ref=src, dst_ref=dst, send_sem=ssem, recv_sem=rsem, device_id=dev, device_id_type=MESH)


def place():
    dp, seq = lax.axis_index("dp"), lax.axis_index("seq")
    return lax.div(dp, 2), lax.rem(dp, 2), lax.div(seq, 2), lax.rem(seq, 2)


def dev(x, c, z, y):
    return (x * 2 + c, z * 2 + y)


def greet(partners):
    bar = pltpu.get_barrier_semaphore()
    for p in partners:
        pl.semaphore_signal(bar, inc=1, device_id=p, device_id_type=MESH)
    pl.semaphore_wait(bar, len(partners))


def fwd_kernel(hd, heads, tok, wp, normed, qkvT, oT, lse, own, vec, fb1, wT, bt,
               T, Ws, k_s, o_s, st, rt, lt, sy, ry, sc, rc, scy, rcy, sa, ra, la, sz, rz, sx, rx, so, ro, lo):
    x, c, z, y = place()
    hg = c * 2 + y
    W = heads * hd
    D = T.shape[2]
    R = T.shape[1]
    N = qkvT.shape[1]
    zoff = [lax.rem(z + k, 4) for k in (1, 2, 3)]
    greet([dev(x, c, zz, y) for zz in zoff] + [dev(x, 1 - c, zz, y) for zz in zoff]
          + [dev(x, 1 - c, z, y), dev(x, c, z, 1 - y), dev(x, 1 - c, z, 1 - y), dev(1 - x, c, z, y)])
    sib, yp, diag, xp = dev(x, 1 - c, z, y), dev(x, c, z, 1 - y), dev(x, 1 - c, z, 1 - y), dev(1 - x, c, z, y)
    pos = (lax.div(z, 2) * 2 + y) * 2 + lax.rem(z, 2)
    tcp = []
    for i in range(2):
        zt = 2 * c + i
        cp = rcopy(tok.at[i], T.at[pos], st.at[i], rt.at[lax.rem(z, 2)], dev(x, lax.div(z, 2), zt, y))
        loc = pltpu.make_async_copy(tok.at[i], T.at[pos], lt)
        @pl.when(zt != z)
        def _():
            cp.start()
        @pl.when(zt == z)
        def _():
            loc.start()
        tcp.append((zt, cp, loc))
    xz = x * 4 + z
    wloc = pltpu.make_async_copy(wp.at[hg], Ws.at[xz, hg], la)
    wloc.start()
    wa = []
    for k, (d, g) in enumerate(((yp, c * 2 + 1 - y), (sib, (1 - c) * 2 + y), (diag, (1 - c) * 2 + 1 - y))):
        cp = rcopy(wp.at[g], Ws.at[xz, hg], sa.at[k], ra.at[k], d)
        cp.start()
        wa.append(cp)
    wloc.wait()
    for cp in wa:
        cp.wait()
    wz = []
    for k in range(3):
        cp = rcopy(Ws.at[xz], Ws.at[xz], sz.at[k], rz.at[k], dev(x, c, zoff[k], y))
        cp.start()
        wz.append(cp)
    wx = [rcopy(Ws.at[xz], Ws.at[xz], sx.at[3], rx.at[3], xp)]
    wx[0].start()
    ycp, ccp, cycp = [], [], []
    for j in range(2):
        src_z = 2 * c + j
        p = hg * 2 + j
        arr = rcopy(tok.at[0], T.at[p], st.at[0], rt.at[j], sib)
        @pl.when(src_z != z)
        def _():
            arr.wait_recv()
        @pl.when(src_z == z)
        def _():
            pltpu.make_async_copy(tok.at[0], T.at[p], lt).wait()
        a = rcopy(T.at[p], T.at[p], sy.at[j], ry.at[j], yp)
        b = rcopy(T.at[p], T.at[p], sc.at[j], rc.at[j], sib)
        a.start()
        b.start()
        ycp.append(a)
        ccp.append(b)
    for k in range(3):
        wz[k].wait()
        zs = lax.rem(z + 3 - k, 4)
        cp = rcopy(Ws.at[x * 4 + zs], Ws.at[x * 4 + zs], sx.at[k], rx.at[k], xp)
        cp.start()
        wx.append(cp)
    for j in range(2):
        ycp[j].wait()
        p = (c * 2 + 1 - y) * 2 + j
        cp = rcopy(T.at[p], T.at[p], scy.at[j], rcy.at[j], sib)
        cp.start()
        cycp.append(cp)
    for cp in wx:
        cp.wait()
    for xx in range(2):
        for zz in range(4):
            for cc in range(2):
                for yy in range(2):
                    r = (xx * 2 + cc) * 8 + zz * 2 + yy
                    blk = Ws[xx * 4 + zz, cc * 2 + yy, 0:16, 3 * W:3 * W + 128].astype(f32)
                    vec[:, r * 32:(r + 1) * 32] = blk[:, 0:32]
                    fb1[:, r * 128:(r + 1) * 128] = blk[8:16, :]
                c0 = (xx * 2 + cc) * 256 + zz * 64
                wT[:, c0:c0 + 64] = Ws[xx * 4 + zz, cc * 2:cc * 2 + 2, :, 0:3 * W].reshape(64, 3 * W).T
    hours = jnp.zeros((1, 1), f32)
    for zz in range(4):
        hz = Ws[x * 4, (zz // 2) * 2, 0:16, 3 * W:3 * W + 128].astype(f32)[11:12, zz % 2:zz % 2 + 1]
        hours = jnp.where(z == zz, hz, hours)
    t = hours / 100.0
    for j in range(2):
        ccp[j].wait()
        cycp[j].wait()
    shift = t * vec[0:1, :] + vec[1:2, :]
    vec[14:15, :] = jnp.broadcast_to(t, (1, D))
    vec[15:16, :] = shift
    gain, bias = vec[2:3, :], vec[3:4, :]
    qb = vec[:, pl.ds(hg * W, W)].T
    def blk(p, carry):
        v = T[p].astype(f32) + shift
        cen = v - jnp.mean(v, axis=-1, keepdims=True)
        r = lax.rsqrt(jnp.mean(cen * cen, axis=-1, keepdims=True) + EPS)
        nb = (cen * r * gain + bias).astype(bf16)
        normed[p] = nb
        pr = dot_nt(wT[...], nb)
        cols = pl.ds(p * R, R)
        qkvT[0:W, cols] = (pr[0:W] + qb[:, 4:5]).astype(bf16)
        qkvT[W:2 * W, cols] = pr[W:2 * W].astype(bf16)
        qkvT[2 * W:3 * W, cols] = (pr[2 * W:] + qb[:, 5:6]).astype(bf16)
        return carry
    lax.fori_loop(0, T.shape[0], blk, 0)
    own[...] = T[pl.ds(hg * 2, 2)]
    for h in range(heads):
        k_s[h] = qkvT[W + h * hd:W + (h + 1) * hd, :].T
    QB, KB = 2 * R, 512
    cs = LOG2E * hd ** -0.5
    nk = N // KB
    def group(k, carry):
        cc = jnp.where((k == 1) | (k == 2), 1 - c, c)
        yy = jnp.where(k < 2, 1 - y, y)
        g = cc * 2 + yy
        qcols = pl.ds(g * QB, QB)
        def head(h, carry):
            qt = qkvT[pl.ds(h * hd, hd), qcols]
            def scores(i):
                return dot_nn(k_s[h, i * KB:(i + 1) * KB, :], qt)
            m = None
            s = scores(0)
            for i in range(nk):
                nxt = scores(i + 1) if i + 1 < nk else None
                cm = jnp.max(s, axis=0, keepdims=True)
                mn = cm if m is None else jnp.maximum(m, cm)
                p = jnp.exp2(s * cs - mn * cs)
                ps = jnp.sum(p, axis=0, keepdims=True)
                vt = qkvT[pl.ds(2 * W + h * hd, hd), i * KB:(i + 1) * KB]
                ov = dot_nn(vt, p.astype(bf16))
                if m is None:
                    l, o = ps, ov
                else:
                    a = jnp.exp2((m - mn) * cs)
                    l = l * a + ps
                    o = o * a + ov
                m = mn
                s = nxt
            o = o / l
            o_s[g, pl.ds(h * hd, hd), :] = o.astype(bf16)
            oT[pl.ds(h * hd, hd), qcols] = o
            lse[pl.ds(h, 1), qcols] = m * cs + jnp.log2(l)
            return carry
        lax.fori_loop(0, heads, head, 0)
        @pl.when(k < 3)
        def _():
            rcopy(o_s.at[g], bt.at[hg], so.at[k], ro.at[k], dev(x, cc, z, yy)).start()
        @pl.when(k == 3)
        def _():
            pltpu.make_async_copy(o_s.at[g], bt.at[hg], lo).start()
        return carry
    lax.fori_loop(0, 4, group, 0)
    for k, d in enumerate((yp, diag, sib)):
        rcopy(o_s.at[0], bt.at[hg], so.at[k], ro.at[k], d).wait()
    pltpu.make_async_copy(o_s.at[0], bt.at[hg], lo).wait()
    for i in range(2):
        zt, cp, loc = tcp[i]
        @pl.when(zt != z)
        def _():
            cp.wait_send()


def forward_kernel(tok, wp, heads, hd, FF):
    n_it, R, D = tok.shape
    W = heads * hd
    N = 8 * R
    S = pltpu.SemaphoreType.DMA
    vm = pl.BlockSpec(memory_space=pltpu.VMEM)
    hbm = pl.BlockSpec(memory_space=pl.ANY)
    return pl.pallas_call(
        functools.partial(fwd_kernel, hd, heads),
        in_specs=[hbm, hbm],
        out_specs=[vm, vm, vm, vm, vm, vm, vm, vm, hbm],
        out_shape=[
            jax.ShapeDtypeStruct((8, R, D), bf16),
            jax.ShapeDtypeStruct((3 * W, N), bf16),
            jax.ShapeDtypeStruct((W, N), f32),
            jax.ShapeDtypeStruct((heads, N), f32),
            jax.ShapeDtypeStruct((2, R, D), bf16),
            jax.ShapeDtypeStruct((16, D), f32),
            jax.ShapeDtypeStruct((8, FF), f32),
            jax.ShapeDtypeStruct((3 * W, D), bf16),
            jax.ShapeDtypeStruct((4, W, 2 * R), bf16),
        ],
        scratch_shapes=[
            pltpu.VMEM((8, R, D), bf16),
            pltpu.VMEM((8, 4, 32, 3 * W + 128), bf16),
            pltpu.VMEM((heads, N, hd), bf16),
            pltpu.VMEM((4, W, 2 * R), bf16),
            S((2,)), S((2,)), S, S((2,)), S((2,)), S((2,)), S((2,)), S((2,)), S((2,)),
            S((3,)), S((3,)), S, S((3,)), S((3,)), S((4,)), S((4,)), S((3,)), S((3,)), S,
        ],
        compiler_params=pltpu.CompilerParams(collective_id=0, has_side_effects=True, vmem_limit_bytes=56 << 20),
        name="forward",
    )(tok, wp)


def put_sum(dst, pieces):
    total = pieces[0].astype(f32)
    for p in pieces[1:]:
        total = total + p.astype(f32)
    dst[...] = total.astype(dst.dtype)


def tail_kernel(hd, heads, dob, qkvT, oT, lse, a1, a2, a3, normed, wT, own, rows, mgrad, sums0,
                o1, o2, o3, gq, home, sums,
                do_s, dq_s, k1, r11, r12, r13, k2, r21, r22, r23, k3, r31, r32, r33,
                Gb, gx, gz, go, ds_s, dr_c, dy_s, dr_y, ig, hm, vs, vr,
                sd, rd, ld, s1, q1, s2, q2, s3, q3, lk, sg, qg, sgz, qgz, sga, qga, sdc, qdc, sdy, qdy, sh, qh, lh, sv, qv, ll):
    x, c, z, y = place()
    hg = c * 2 + y
    W = heads * hd
    N = qkvT.shape[1]
    zoff = [lax.rem(z + k, 4) for k in (1, 2, 3)]
    sib, yp, diag, xp = dev(x, 1 - c, z, y), dev(x, c, z, 1 - y), dev(x, 1 - c, z, 1 - y), dev(1 - x, c, z, y)
    zp = [dev(x, c, zz, y) for zz in zoff]
    greet(zp + [dev(x, 1 - c, zz, y) for zz in zoff] + [sib, yp, diag, xp])
    peers = ((sib, (1 - c) * 2 + y), (yp, c * 2 + 1 - y), (diag, (1 - c) * 2 + 1 - y))
    for k, (d, g) in enumerate(peers):
        rcopy(dob.at[g], do_s.at[hg], sd.at[k], rd.at[k], d).start()
    loc = pltpu.make_async_copy(dob.at[hg], do_s.at[hg], ld)
    loc.start()

    def part(ref, h, n):
        return ref if n is None else ref.at[..., pl.ds(h * n, n), :]
    n1, n2 = k1.shape[2] // 2, k2.shape[2] // 2

    class Piece:
        def __init__(self, i, h, n, a, k, r1, r2, r3, out, s, q, lsem, yfirst):
            self.a, self.k, self.r1, self.r2, self.r3, self.out = [part(v, h, n) for v in (a, k, r1, r2, r3, out)]
            self.s, self.q, self.lsem, self.yfirst, self.b = s, q, lsem, yfirst, h * 5
            self.i = i
        def copies(self):
            b, s, q = self.b, self.s, self.q
            if self.yfirst:
                first = rcopy(self.a.at[:, :, 1 - y], self.r1, s.at[b], q.at[b], yp)
                second = rcopy(self.k.at[1 - x], self.r2, s.at[b + 1], q.at[b + 1], xp)
                kept = self.a.at[:, :, y]
                mine = lambda zz: self.k.at[x, zz]
            else:
                first = rcopy(self.a.at[1 - x], self.r1, s.at[b], q.at[b], xp)
                second = rcopy(self.k.at[:, 1 - y], self.r2, s.at[b + 1], q.at[b + 1], yp)
                kept = self.a.at[x]
                mine = lambda zz: self.k.at[zz, y]
            zs = [rcopy(mine(zoff[j]), self.r3.at[j], s.at[b + 2 + j], q.at[b + 2 + j], zp[j]) for j in range(3)]
            return first, second, zs, pltpu.make_async_copy(kept, self.k, self.lsem.at[self.i]), mine
        def start(self):
            first, _, _, keep, _ = self.copies()
            keep.start()
            first.start()
        def second(self):
            first, second, _, keep, _ = self.copies()
            keep.wait()
            first.wait()
            n0, n1_ = self.k.shape[0], self.k.shape[1]
            def add(j, carry):
                p, q_ = lax.div(j, n1_), lax.rem(j, n1_)
                put_sum(self.k.at[p, q_], [self.k[p, q_], self.r1[p, q_]])
                return carry
            lax.fori_loop(0, n0 * n1_, add, 0)
            second.start()
        def third(self):
            _, second, zs, _, mine = self.copies()
            second.wait()
            def add(zz, carry):
                put_sum(mine(zz), [mine(zz)[...], self.r2[zz]])
                return carry
            lax.fori_loop(0, 4, add, 0)
            for cp in zs:
                cp.start()
        def finish(self):
            _, _, zs, _, mine = self.copies()
            for cp in zs:
                cp.wait()
            put_sum(self.out, [mine(z)[...]] + [self.r3[j] for j in range(3)])

    f1 = [Piece(h, h, n1, a1, k1, r11, r12, r13, o1, s1, q1, lk, True) for h in range(2)]
    f2 = [Piece(2 + h, h, n2, a2, k2, r21, r22, r23, o2, s2, q2, lk, False) for h in range(2)]
    f3 = Piece(4, 0, None, a3, k3, r31, r32, r33, o3, s3, q3, lk, False)
    f2[0].start()
    f1[0].start()

    QB, KB = N // 4, 512
    cs = LOG2E * hd ** -0.5
    sc = hd ** -0.5
    nk = N // KB

    def attention(k_s, v_s, dk_s, dv_s):
        for h in range(heads):
            k_s[h] = qkvT[W + h * hd:W + (h + 1) * hd, :].T
            v_s[h] = qkvT[2 * W + h * hd:2 * W + (h + 1) * hd, :].T
        dk_s[...] = jnp.zeros_like(dk_s)
        dv_s[...] = jnp.zeros_like(dv_s)
        loc.wait()
        def group(k, carry):
            @pl.when(k > 0)
            def _():
                rcopy(dob.at[0], do_s.at[0], sd.at[k - 1], rd.at[k - 1], sib).wait()
            cc = jnp.where((k == 1) | (k == 3), 1 - c, c)
            yy = jnp.where(k >= 2, 1 - y, y)
            g = cc * 2 + yy
            qcols = pl.ds(g * QB, QB)
            def head(h, carry):
                @pl.when((k == 1) & (h == 1))
                def _():
                    f2[1].start()
                    f1[1].start()
                @pl.when((k == 2) & (h == 1))
                def _():
                    f2[0].second()
                @pl.when((k == 2) & (h == 3))
                def _():
                    f1[0].second()
                    f3.start()
                hr = pl.ds(h * hd, hd)
                qt = qkvT[hr, qcols]
                dt = do_s[g, hr, :]
                delta = jnp.sum(dt.astype(f32) * oT[hr, qcols], axis=0, keepdims=True)
                ls = lse[pl.ds(h, 1), qcols]
                def first(i):
                    ks = slice(i * KB, (i + 1) * KB)
                    return dot_nn(k_s[h, ks, :], qt), dot_nn(v_s[h, ks, :], dt)
                dq = None
                cur = first(0)
                for i in range(nk):
                    nxt = first(i + 1) if i + 1 < nk else None
                    s, dp = cur
                    ks = slice(i * KB, (i + 1) * KB)
                    p = jnp.exp2(s * cs - ls)
                    ds = (p * (dp - delta)).astype(bf16)
                    prt = dot_nn(qkvT[pl.ds(W + h * hd, hd), ks], ds)
                    dq = prt if dq is None else dq + prt
                    dk_s[h, :, ks] += dot_nt(qt, ds)
                    dv_s[h, :, ks] += dot_nt(dt, p.astype(bf16))
                    cur = nxt
                dq_s[hr, qcols] = (dq * sc).astype(bf16)
                return carry
            lax.fori_loop(0, heads, head, 0)
            return carry
        lax.fori_loop(0, 4, group, 0)
        for h in range(heads):
            dq_s[W + h * hd:W + (h + 1) * hd, :] = (dk_s[h] * sc).astype(bf16)
            dq_s[2 * W + h * hd:2 * W + (h + 1) * hd, :] = dv_s[h].astype(bf16)

    pl.run_scoped(attention, pltpu.VMEM((heads, N, hd), bf16), pltpu.VMEM((heads, N, hd), bf16),
                  pltpu.VMEM((heads, hd, N), f32), pltpu.VMEM((heads, hd, N), f32))

    def after(nm, w_s, tok_s, mg_s, dn, lsem):
        R = tok_s.shape[1]
        loads = [pltpu.make_async_copy(a, b, lsem.at[i]) for i, (a, b) in enumerate(((normed, nm), (wT, w_s), (own, tok_s), (mgrad, mg_s)))]
        for cp in loads:
            cp.start()
        loads[1].wait()
        def proj(g, j):
            cols = pl.ds(g * QB + j * R, R)
            return dot_nn(dq_s[:, cols].T, w_s[...])
        g_sy, g_s, g_oy = (1 - c) * 2 + 1 - y, (1 - c) * 2 + y, c * 2 + 1 - y
        def to_sib(a, j):
            return rcopy(ds_s.at[a, j], dr_c.at[a, j], sdc.at[a * 2 + j], qdc.at[a * 2 + j], sib)
        def to_y(j):
            return rcopy(dy_s.at[j], dr_y.at[j], sdy.at[j], qdy.at[j], yp)
        for j in range(2):
            ds_s[0, j] = proj(g_sy, j).astype(bf16)
            to_sib(0, j).start()
        for j in range(2):
            mine = proj(g_oy, j)
            to_sib(0, j).wait()
            dy_s[j] = (mine + dr_c[0, j].astype(f32)).astype(bf16)
            to_y(j).start()
        f2[1].second()
        f1[1].second()
        loads[0].wait()
        nm2 = nm[...].reshape(N, nm.shape[2])
        for q in range(3):
            t = dot_nn(dq_s[q * W:(q + 1) * W, :], nm2).astype(bf16).T
            Gb[..., q * W:(q + 1) * W] = t.reshape(2, 2, 4, 2, Gb.shape[4], W)
        gxc = rcopy(Gb.at[1 - x], gx, sg, qg, xp)
        gxc.start()
        for j in range(2):
            ds_s[1, j] = proj(g_s, j).astype(bf16)
            to_sib(1, j).start()
        for j in range(2):
            dn[j] = proj(hg, j)
        f2[0].third()
        f1[0].third()
        f3.second()
        ones = jnp.ones((8, N), bf16)
        vs[...] = sums0[...]
        for row, q in ((12, 0), (13, 2)):
            tot = dot_nt(ones, dq_s[q * W:(q + 1) * W, :])
            vs[row:row + 1, :] = jnp.zeros((1, vs.shape[1]), f32)
            vs[row:row + 1, pl.ds(pl.multiple_of(hg * W, W), W)] = tot[0:1]
        gxc.wait()
        for cc in range(2):
            for zz in range(4):
                put_sum(Gb.at[x, cc, zz], [Gb[x, cc, zz], gx[cc, zz]])
        gzs = [rcopy(Gb.at[x, :, zoff[j]], gz.at[j], sgz.at[j], qgz.at[j], zp[j]) for j in range(3)]
        for cp in gzs:
            cp.start()
        f2[1].third()
        f1[1].third()
        gain = rows[2:3, :]
        shift = rows[15:16, :]
        acc = [jnp.zeros((1, dn.shape[2]), f32) for _ in range(3)]
        loads[2].wait()
        loads[3].wait()
        homes = []
        for j in range(2):
            to_sib(1, j).wait()
            to_y(j).wait()
            u = dn[j] + dr_c[1, j].astype(f32) + dr_y[j].astype(f32)
            v = tok_s[j].astype(f32) + shift
            cen = v - jnp.mean(v, axis=-1, keepdims=True)
            r = lax.rsqrt(jnp.mean(cen * cen, axis=-1, keepdims=True) + EPS)
            xh = cen * r
            e = u * gain
            res = mg_s[j] + r * (e - jnp.mean(e, axis=-1, keepdims=True) - xh * jnp.mean(e * xh, axis=-1, keepdims=True))
            ig[j] = res.astype(bf16)
            for n, val in enumerate((u * xh, u, res)):
                acc[n] = acc[n] + jnp.sum(val, axis=0, keepdims=True)
            zt = 2 * c + j
            cp = rcopy(ig.at[j], hm.at[lax.rem(z, 2)], sh.at[j], qh.at[lax.rem(z, 2)], dev(x, lax.div(z, 2), zt, y))
            lc = pltpu.make_async_copy(ig.at[j], hm.at[lax.rem(z, 2)], lh)
            @pl.when(zt != z)
            def _():
                cp.start()
            @pl.when(zt == z)
            def _():
                lc.start()
            homes.append((zt, cp, lc))
        vs[8:9, :] = acc[0]
        vs[9:10, :] = acc[1]
        vs[10:11, :] = acc[2] * rows[14:15, :]
        vs[11:12, :] = acc[2]
        for k, d in enumerate((sib, yp, xp)):
            cp = rcopy(vs, vr.at[k], sv.at[k], qv.at[k], d)
            cp.start()
            cp.wait()
            vs[...] = vs[...] + vr[k]
        zv = [rcopy(vs, vr.at[3 + k], sv.at[3 + k], qv.at[3 + k], zp[k]) for k in range(3)]
        for cp in zv:
            cp.start()
        f3.third()
        for cp in gzs:
            cp.wait()
        for cc in range(2):
            for yy in range(2):
                put_sum(Gb.at[x, cc, z, yy], [Gb[x, cc, z, yy]] + [gz[k, cc, yy] for k in range(3)])
        gas = []
        for k, (d, cc, yy) in enumerate(((sib, 1 - c, y), (yp, c, 1 - y), (diag, 1 - c, 1 - y))):
            cp = rcopy(Gb.at[x, cc, z, yy], go.at[hg], sga.at[k], qga.at[k], d)
            cp.start()
            gas.append(cp)
        lcl = pltpu.make_async_copy(Gb.at[x, c, z, y], go.at[hg], ll)
        lcl.start()
        for cp in zv:
            cp.wait()
        sums[...] = vs[...] + vr[3] + vr[4] + vr[5]
        f2[0].finish()
        f1[0].finish()
        f2[1].finish()
        f1[1].finish()
        f3.finish()
        lcl.wait()
        for cp in gas:
            cp.wait()
        D = gq.shape[1] // 3
        for g in range(4):
            for q in range(3):
                gq[:, q * D + g * W:q * D + (g + 1) * W] = go[g, :, q * W:(q + 1) * W].astype(f32)
        for i in range(2):
            src = 2 * c + i
            arr = rcopy(ig.at[0], hm.at[i], sh.at[0], qh.at[i], sib)
            @pl.when(src != z)
            def _():
                arr.wait_recv()
            @pl.when(src == z)
            def _():
                pltpu.make_async_copy(ig.at[0], hm.at[i], lh).wait()
            home[i] = hm[i].astype(f32)
        for zt, cp, lc in homes:
            @pl.when(zt != z)
            def _():
                cp.wait_send()

    R = own.shape[1]
    D = own.shape[2]
    pl.run_scoped(after, pltpu.VMEM(normed.shape, bf16), pltpu.VMEM(wT.shape, bf16), pltpu.VMEM((2, R, D), bf16),
                  pltpu.VMEM((2, R, D), f32), pltpu.VMEM((2, R, D), f32), pltpu.SemaphoreType.DMA((4,)))


def backward_kernel(dob, qkvT, oT, lse, a1, a2, a3, normed, wT, own, rows, mgrad, sums0, heads, hd):
    W3, N = qkvT.shape
    W = heads * hd
    _, R, D = own.shape
    S = pltpu.SemaphoreType.DMA
    V = pltpu.VMEM
    vm = pl.BlockSpec(memory_space=pltpu.VMEM)
    hbm = pl.BlockSpec(memory_space=pl.ANY)
    b1, b2, b3 = a1.shape[3:], a2.shape[3:], a3.shape[3:]
    def bufs(b, yfirst):
        k = (2, 4) if yfirst else (4, 2)
        return [V(k + b, bf16), V(k + b, bf16), V((4,) + b, bf16), V((3,) + b, bf16)]
    rq = D // 32
    return pl.pallas_call(
        functools.partial(tail_kernel, hd, heads),
        in_specs=[hbm, vm, vm, vm, hbm, hbm, hbm, hbm, hbm, hbm, vm, hbm, vm],
        out_specs=[vm] * 6,
        out_shape=[
            jax.ShapeDtypeStruct(b1, f32), jax.ShapeDtypeStruct(b2, f32), jax.ShapeDtypeStruct(b3, f32),
            jax.ShapeDtypeStruct((rq, 3 * D), f32), jax.ShapeDtypeStruct((2, R, D), f32), jax.ShapeDtypeStruct((16, D), f32),
        ],
        scratch_shapes=[V((4, W, N // 4), bf16), V((W3, N), bf16)] + bufs(b1, True) + bufs(b2, False) + bufs(b3, False) + [
            V((2, 2, 4, 2, rq, W3), bf16), V((2, 4, 2, rq, W3), bf16), V((3, 2, 2, rq, W3), bf16), V((4, rq, W3), bf16),
            V((2, 2, R, D), bf16), V((2, 2, R, D), bf16), V((2, R, D), bf16), V((2, R, D), bf16), V((2, R, D), bf16), V((2, R, D), bf16),
            V((16, D), f32), V((6, 16, D), f32),
            S((3,)), S((3,)), S, S((10,)), S((10,)), S((10,)), S((10,)), S((5,)), S((5,)), S((5,)),
            S, S, S((3,)), S((3,)), S((3,)), S((3,)), S((4,)), S((4,)), S((2,)), S((2,)), S((2,)), S((2,)), S, S((6,)), S((6,)), S,
        ],
        compiler_params=pltpu.CompilerParams(collective_id=1, has_side_effects=True, vmem_limit_bytes=60 << 20),
        name="backward",
    )(dob, qkvT, oT, lse, a1, a2, a3, normed, wT, own, rows, mgrad, sums0)


HEADS = 16


epsilon = EPS


def norm_rows_s(values, gain, shift):
    center = values - jnp.mean(values, axis=-1, keepdims=True)
    spread = jnp.mean(center * center, axis=-1, keepdims=True)
    return center * lax.rsqrt(spread + epsilon) * gain + shift


def gelu_exact_s(values):
    return jax.nn.gelu(values, approximate=False)


def product(left, right):
    return jnp.dot(left, right, preferred_element_type=jnp.float32)


def product_tleft(left, right):
    return lax.dot_general(
        left, right, (((0,), (0,)), ((), ())), preferred_element_type=jnp.float32
    )


def product_tright(left, right):
    return lax.dot_general(
        left, right, (((1,), (1,)), ((), ())), preferred_element_type=jnp.float32
    )


def split_heads(values):
    return values.reshape(values.shape[0], HEADS, values.shape[1] // HEADS)


def attend(operands):
    queries, keys_all, values_all = operands
    scale = (queries.shape[1] // HEADS) ** (-0.5)
    scores = (
        jnp.einsum(
            "qhd,khd->hqk",
            split_heads(queries),
            split_heads(keys_all),
            preferred_element_type=jnp.float32,
        )
        * scale
    )
    highest = jnp.max(scores, axis=-1, keepdims=True)
    exps = jnp.exp(scores - highest)
    totals = jnp.sum(exps, axis=-1, keepdims=True)
    probs_low = (exps / totals).astype(jnp.bfloat16)
    blended = jnp.einsum(
        "hqk,khd->qhd", probs_low, split_heads(values_all), preferred_element_type=jnp.float32
    ).reshape(queries.shape)
    return (blended, (highest + jnp.log(totals))[:, :, 0])


def recompute_probs(queries, keys_all, values_all, grads_in, log_totals):
    scale = (queries.shape[1] // HEADS) ** (-0.5)
    scores = (
        jnp.einsum(
            "qhd,khd->hqk",
            split_heads(queries),
            split_heads(keys_all),
            preferred_element_type=jnp.float32,
        )
        * scale
    )
    probs = jnp.exp(scores - log_totals[:, :, None])
    prob_grads = jnp.einsum(
        "qhd,khd->hqk",
        split_heads(grads_in),
        split_heads(values_all),
        preferred_element_type=jnp.float32,
    )
    return (probs, prob_grads, scale)


def key_side_grads(score_grads, probs, queries, grads_in, row_count):
    key_grads = jnp.einsum(
        "hqk,qhd->khd", score_grads, split_heads(queries), preferred_element_type=jnp.float32
    )
    value_grads = jnp.einsum(
        "hqk,qhd->khd",
        probs.astype(jnp.bfloat16),
        split_heads(grads_in),
        preferred_element_type=jnp.float32,
    )
    width = queries.shape[1]
    return (key_grads.reshape(row_count, width), value_grads.reshape(row_count, width))


def query_side(with_keys, operands):
    queries, keys_all, values_all, grads_in, log_totals = operands
    probs, prob_grads, scale = recompute_probs(queries, keys_all, values_all, grads_in, log_totals)
    row_delta = jnp.sum(probs * prob_grads, axis=-1)
    score_grads = (probs * (prob_grads - row_delta[:, :, None]) * scale).astype(jnp.bfloat16)
    query_grads = jnp.einsum(
        "hqk,khd->qhd", score_grads, split_heads(keys_all), preferred_element_type=jnp.float32
    ).reshape(queries.shape)
    key_grads, value_grads = key_side_grads(
        score_grads, probs, queries, grads_in, keys_all.shape[0]
    )
    return (query_grads, row_delta, key_grads, value_grads)


def spread_on_device(
    tokens_in,
    lead_hours,
    cotangent,
    w_qkv,
    w_out,
    w_fc1,
    w_fc2,
    ln1_gain,
    ln1_bias,
    q_bias,
    v_bias,
    out_bias,
    ln2_gain,
    ln2_bias,
    fc1_bias,
    fc2_bias,
    lead_weight,
    lead_bias,
):
    gathered = (
        lax.all_gather(w_qkv, ("dp", "seq"), axis=0, tiled=True),
        lax.all_gather(w_out, ("dp", "seq"), axis=0, tiled=True),
        lax.all_gather(w_fc1, ("dp", "seq"), axis=0, tiled=True),
        lax.all_gather(w_fc2, ("dp", "seq"), axis=0, tiled=True),
        lax.all_gather(ln1_gain, ("dp", "seq"), axis=0, tiled=True),
        lax.all_gather(ln1_bias, ("dp", "seq"), axis=0, tiled=True),
        lax.all_gather(q_bias, ("dp", "seq"), axis=0, tiled=True),
        lax.all_gather(v_bias, ("dp", "seq"), axis=0, tiled=True),
        lax.all_gather(out_bias, ("dp", "seq"), axis=0, tiled=True),
        lax.all_gather(ln2_gain, ("dp", "seq"), axis=0, tiled=True),
        lax.all_gather(ln2_bias, ("dp", "seq"), axis=0, tiled=True),
        lax.all_gather(fc1_bias, ("dp", "seq"), axis=0, tiled=True),
        lax.all_gather(fc2_bias, ("dp", "seq"), axis=0, tiled=True),
        lax.all_gather(lead_weight, ("dp", "seq"), axis=0, tiled=True),
        lax.all_gather(lead_bias, ("dp", "seq"), axis=0, tiled=True),
    )
    (
        full_qkv,
        full_out,
        full_fc1,
        full_fc2,
        gain_one,
        shift_one,
        bias_query,
        bias_value,
        bias_out,
        gain_two,
        shift_two,
        bias_fc1,
        bias_fc2,
        lead_scale,
        lead_shift,
    ) = gathered
    items, rows, width = tokens_in.shape
    count = items * rows
    lead_times = lead_hours.astype(jnp.float32) / 100.0
    leading = (
        tokens_in.astype(jnp.float32)
        + lead_times[:, None, None] * lead_scale.astype(jnp.float32)
        + lead_shift.astype(jnp.float32)
    ).reshape(count, width)
    normed, norm_one_back = jax.vjp(
        norm_rows_s, leading, gain_one.astype(jnp.float32), shift_one.astype(jnp.float32)
    )
    normed_low = normed.astype(jnp.bfloat16)
    projected = product(normed_low, full_qkv)
    queries = (projected[:, :width] + bias_query.astype(jnp.float32)).astype(jnp.bfloat16)
    keys_own = projected[:, width : 2 * width].astype(jnp.bfloat16)
    values_own = (projected[:, 2 * width :] + bias_value.astype(jnp.float32)).astype(jnp.bfloat16)
    queries3 = queries.reshape(items, rows, width)
    keys_all, values_all = (
        lax.all_gather(keys_own.reshape(items, rows, width), "seq", axis=1, tiled=True),
        lax.all_gather(values_own.reshape(items, rows, width), "seq", axis=1, tiled=True),
    )
    blended, log_totals = lax.map(attend, (queries3, keys_all, values_all))
    blended_low = blended.reshape(count, width).astype(jnp.bfloat16)
    middle = leading + product(blended_low, full_out) + bias_out.astype(jnp.float32)
    normed_two, norm_two_back = jax.vjp(
        norm_rows_s, middle, gain_two.astype(jnp.float32), shift_two.astype(jnp.float32)
    )
    normed_two_low = normed_two.astype(jnp.bfloat16)
    hidden = product(normed_two_low, full_fc1) + bias_fc1.astype(jnp.float32)
    activated, gelu_back = jax.vjp(gelu_exact_s, hidden)
    activated_low = activated.astype(jnp.bfloat16)
    output = middle + product(activated_low, full_fc2) + bias_fc2.astype(jnp.float32)
    block_output = output.reshape(items, rows, width).astype(jnp.bfloat16)
    back_qkv, back_out, back_fc1, back_fc2 = (
        lax.all_gather(w_qkv, ("dp", "seq"), axis=0, tiled=True),
        lax.all_gather(w_out, ("dp", "seq"), axis=0, tiled=True),
        lax.all_gather(w_fc1, ("dp", "seq"), axis=0, tiled=True),
        lax.all_gather(w_fc2, ("dp", "seq"), axis=0, tiled=True),
    )
    out_grad = cotangent.reshape(count, width)
    upstream = out_grad.astype(jnp.float32)
    grad_fc2 = product_tleft(activated_low, out_grad)
    grad_fc2_bias = jnp.sum(upstream, axis=0)
    hidden_grad = gelu_back(product_tright(out_grad, back_fc2))[0].astype(jnp.bfloat16)
    grad_fc1 = product_tleft(normed_two_low, hidden_grad)
    grad_fc1_bias = jnp.sum(hidden_grad.astype(jnp.float32), axis=0)
    middle_part, grad_ln2_gain, grad_ln2_bias = norm_two_back(product_tright(hidden_grad, back_fc1))
    middle_grad = upstream + middle_part
    attn_grad = middle_grad.astype(jnp.bfloat16)
    grad_out = product_tleft(blended_low, attn_grad)
    grad_out_bias = jnp.sum(attn_grad.astype(jnp.float32), axis=0)
    blended_grad = (
        product_tright(attn_grad, back_out).astype(jnp.bfloat16).reshape(items, rows, width)
    )
    query_grads, row_delta, key_parts, value_parts = lax.map(
        partial(query_side, True), (queries3, keys_all, values_all, blended_grad, log_totals)
    )
    key_grads, value_grads = (
        lax.psum_scatter(
            key_parts.astype(jnp.bfloat16), "seq", scatter_dimension=1, tiled=True
        ).astype(jnp.float32),
        lax.psum_scatter(
            value_parts.astype(jnp.bfloat16), "seq", scatter_dimension=1, tiled=True
        ).astype(jnp.float32),
    )
    query_low = query_grads.reshape(count, width).astype(jnp.bfloat16)
    key_low = key_grads.reshape(count, width).astype(jnp.bfloat16)
    value_low = value_grads.reshape(count, width).astype(jnp.bfloat16)
    qkv_grad = jnp.concatenate([query_low, key_low, value_low], axis=1)
    grad_qkv = product_tleft(normed_low, qkv_grad)
    grad_q_bias = jnp.sum(query_low.astype(jnp.float32), axis=0)
    grad_v_bias = jnp.sum(value_low.astype(jnp.float32), axis=0)
    leading_part, grad_ln1_gain, grad_ln1_bias = norm_one_back(product_tright(qkv_grad, back_qkv))
    input_grad = (middle_grad + leading_part).reshape(items, rows, width)
    grad_lead_weight = jnp.sum(jnp.sum(input_grad, axis=1) * lead_times[:, None], axis=0)
    grad_lead_bias = jnp.sum(input_grad, axis=(0, 1))
    summed = (
        lax.psum_scatter(grad_qkv, ("dp", "seq"), scatter_dimension=0, tiled=True),
        lax.psum_scatter(grad_out, ("dp", "seq"), scatter_dimension=0, tiled=True),
        lax.psum_scatter(grad_fc1, ("dp", "seq"), scatter_dimension=0, tiled=True),
        lax.psum_scatter(grad_fc2, ("dp", "seq"), scatter_dimension=0, tiled=True),
        lax.psum_scatter(grad_ln1_gain, ("dp", "seq"), scatter_dimension=0, tiled=True),
        lax.psum_scatter(grad_ln1_bias, ("dp", "seq"), scatter_dimension=0, tiled=True),
        lax.psum_scatter(grad_q_bias, ("dp", "seq"), scatter_dimension=0, tiled=True),
        lax.psum_scatter(grad_v_bias, ("dp", "seq"), scatter_dimension=0, tiled=True),
        lax.psum_scatter(grad_out_bias, ("dp", "seq"), scatter_dimension=0, tiled=True),
        lax.psum_scatter(grad_ln2_gain, ("dp", "seq"), scatter_dimension=0, tiled=True),
        lax.psum_scatter(grad_ln2_bias, ("dp", "seq"), scatter_dimension=0, tiled=True),
        lax.psum_scatter(grad_fc1_bias, ("dp", "seq"), scatter_dimension=0, tiled=True),
        lax.psum_scatter(grad_fc2_bias, ("dp", "seq"), scatter_dimension=0, tiled=True),
        lax.psum_scatter(grad_lead_weight, ("dp", "seq"), scatter_dimension=0, tiled=True),
        lax.psum_scatter(grad_lead_bias, ("dp", "seq"), scatter_dimension=0, tiled=True),
    )
    return (block_output, input_grad) + tuple(summed)


def moves(mesh_shape, back):
    seq_n = mesh_shape["seq"]
    out = []
    for p in range(2):
        pairs = []
        for dp in range(mesh_shape["dp"]):
            for seq in range(seq_n):
                x, c, z, y = dp // 2, dp % 2, seq // 2, seq % 2
                i = p ^ (z % 2)
                t = (x * 2 + z // 2) * seq_n + (2 * c + i) * 2 + y
                s = dp * seq_n + seq
                pairs.append((t, s) if back else (s, t))
        out.append(pairs)
    return out


def pick(bit, first, second):
    return jnp.where(bit == 0, first, second)


def carry_out(mesh_shape, values):
    x, c, z, y = place()
    b = lax.rem(z, 2)
    got = [lax.ppermute(pick(b, values[p], values[1 - p]), ("dp", "seq"), m) for p, m in enumerate(moves(mesh_shape, False))]
    return jnp.stack([pick(b, got[0], got[1]), pick(b, got[1], got[0])])


def carry_home(mesh_shape, values):
    x, c, z, y = place()
    b = lax.rem(z, 2)
    got = [lax.ppermute(pick(b, values[p], values[1 - p]), ("dp", "seq"), m) for p, m in enumerate(moves(mesh_shape, True))]
    return jnp.stack([pick(b, got[0], got[1]), pick(b, got[1], got[0])])


def partner(mesh_shape, kind):
    seq_n = mesh_shape["seq"]
    n = seq_n * mesh_shape["dp"]
    if kind == "core":
        return [(s, s ^ seq_n) for s in range(n)]
    return [(s, s ^ 1) for s in range(n)]


def norm_rows(values, gain, shift):
    center = values - jnp.mean(values, axis=-1, keepdims=True)
    spread = jnp.mean(center * center, axis=-1, keepdims=True)
    return center * lax.rsqrt(spread + EPS) * gain + shift


def gelu_exact(values):
    return jax.nn.gelu(values, approximate=False)


def mm(a, b, ca, cb):
    return lax.dot_general(a, b, (((ca,), (cb,)), ((), ())), preferred_element_type=f32)


def on_device(mesh_shape, tokens_in, lead_hours, cotangent, w_qkv, w_out, w_fc1, w_fc2, ln1_gain, ln1_bias, q_bias, v_bias,
              out_bias, ln2_gain, ln2_bias, fc1_bias, fc2_bias, lead_weight, lead_bias):
    AX = ("dp", "seq")
    x, c, z, y = place()
    hg = c * 2 + y
    _, R, D = tokens_in.shape
    FF = w_fc1.shape[1]
    hd = D // HEADS
    heads = HEADS // 4
    W = heads * hd
    rows = w_qkv.shape[0]
    small = jnp.zeros((32, 128), bf16)
    for k, v in enumerate((lead_weight, lead_bias, ln1_gain, ln1_bias, q_bias, v_bias, out_bias, ln2_gain, ln2_bias, fc2_bias)):
        small = small.at[k, :rows].set(v)
    small = small.at[10].set(fc1_bias).at[11, :2].set(lead_hours.astype(bf16))
    slices = w_qkv.reshape(rows, 3, 4, W).transpose(2, 0, 1, 3).reshape(4, rows, 3 * W)
    wp = jnp.concatenate([slices, jnp.broadcast_to(small, (4, 32, 128))], axis=2)
    normed, qkvT, oT, lse, own, vec, fb1, wfull, bt = forward_kernel(tokens_in, wp, heads, hd, FF)
    full_out = lax.all_gather(w_out, AX, axis=0, tiled=True)
    full_fc1 = lax.all_gather(w_fc1, AX, axis=0, tiled=True)
    full_fc2 = lax.all_gather(w_fc2, AX, axis=0, tiled=True)
    upstream_low = carry_out(mesh_shape, cotangent).reshape(2 * R, D)
    bias_fc1 = fb1[2:3]
    leading = own.reshape(2 * R, D).astype(f32) + vec[15:16]
    blendedT = bt.reshape(D, 2 * R)
    middle = leading + mm(blendedT, full_out, 0, 0) + vec[6:7]
    normed2, norm2_back = jax.vjp(norm_rows, middle, vec[7:8], vec[8:9])
    normed2 = normed2.astype(bf16)
    hidden = mm(normed2, full_fc1, 1, 0) + bias_fc1
    activated, gelu_back = jax.vjp(gelu_exact, hidden)
    activated = activated.astype(bf16)
    output = middle + mm(activated, full_fc2, 1, 0) + vec[9:10]
    block_output = carry_home(mesh_shape, output.astype(bf16).reshape(2, R, D))
    upstream = upstream_low.astype(f32)
    core = partner(mesh_shape, "core")
    def chip_sum(left, right, rows):
        cut = left.reshape(2 * R, 2, 2, -1)
        def half(which):
            return mm(lax.dynamic_index_in_dim(cut, which, 2, keepdims=False).reshape(2 * R, -1), right, 0, 0)
        there = lax.ppermute(half(1 - c).astype(bf16), AX, core)
        both = (half(c) + there.astype(f32)).astype(bf16)
        return both.reshape(2, 4, 2, rows, -1)
    a2 = chip_sum(activated, upstream_low, w_fc2.shape[0])
    grad_fc2_bias = jnp.sum(upstream, axis=0)
    hidden_grad = gelu_back(mm(upstream_low, full_fc2, 1, 1))[0].astype(bf16)
    a1 = chip_sum(normed2, hidden_grad, rows)
    grad_fc1_bias = jnp.sum(hidden_grad.astype(f32), axis=0)
    middle_part, g_ln2_gain, g_ln2_bias = norm2_back(mm(hidden_grad, full_fc1, 1, 1))
    middle_grad = upstream + middle_part
    attn_grad = middle_grad.astype(bf16)
    dob = mm(full_out, attn_grad, 1, 1).astype(bf16).reshape(4, W, 2 * R)
    a3 = chip_sum(blendedT.T, attn_grad, rows)
    grad_out_bias = jnp.sum(attn_grad.astype(f32), axis=0)
    sums0 = jnp.concatenate([grad_out_bias[None], g_ln2_gain.reshape(1, D), g_ln2_bias.reshape(1, D), grad_fc2_bias[None],
                             grad_fc1_bias.reshape(-1, D), jnp.zeros((12 - FF // D, D), f32)])
    grad_fc1, grad_fc2, grad_out, grad_qkv, home, sums = backward_kernel(
        dob, qkvT, oT, lse, a1, a2, a3, normed, wfull, own, vec, middle_grad.reshape(2, R, D), sums0, heads, hd)
    index = (x * 2 + c) * 8 + z * 2 + y
    mine = lax.dynamic_slice(sums, (0, index * rows), (16, rows))
    g_fc1_bias = lax.dynamic_slice(sums[4:4 + FF // D].reshape(FF), (index * fc1_bias.shape[0],), (fc1_bias.shape[0],))
    return (block_output, home, grad_qkv, grad_out, grad_fc1, grad_fc2, mine[8], mine[9], mine[12], mine[13], mine[0],
            mine[1], mine[2], g_fc1_bias, mine[3], mine[10], mine[11])


def choose(mesh_shape, *args):
    items, rows = args[0].shape[0], args[3].shape[0]
    planes = mesh_shape["seq"] // 2
    if items == 2 and planes == 2 * items and mesh_shape["dp"] == 4 and rows % 16 == 0:
        return on_device(mesh_shape, *args)
    return spread_on_device(*args)


def solution(mesh):
    big, rows, vec = P("dp", "seq", None), P(("dp", "seq"), None), P(("dp", "seq"))
    in_specs = (big, P("dp"), big) + (rows,) * 4 + (vec,) * 11
    out_specs = (big, big) + (rows,) * 4 + (vec,) * 11
    body = functools.partial(choose, dict(mesh.shape))
    return jax.shard_map(body, mesh=mesh, in_specs=in_specs, out_specs=out_specs, check_vma=False)
```

```python
import functools
from functools import partial
import jax, jax.numpy as jnp
from jax import lax
from jax.experimental import pallas as pl
from jax.experimental.pallas import tpu as pltpu
from jax.sharding import PartitionSpec as P

MESH = pl.DeviceIdType.MESH
f32, bf16 = jnp.float32, jnp.bfloat16
LOG2E = 1.4426950408889634
EPS = 1e-06


def dot_nn(a, b):
    return lax.dot_general(a, b, (((1,), (0,)), ((), ())), preferred_element_type=f32)


def dot_nt(a, b):
    return lax.dot_general(a, b, (((1,), (1,)), ((), ())), preferred_element_type=f32)


def rcopy(src, dst, ssem, rsem, dev):
    return pltpu.make_async_remote_copy(src_ref=src, dst_ref=dst, send_sem=ssem, recv_sem=rsem, device_id=dev, device_id_type=MESH)


def place():
    dp, seq = lax.axis_index("dp"), lax.axis_index("seq")
    return lax.div(dp, 2), lax.rem(dp, 2), lax.div(seq, 2), lax.rem(seq, 2)


def dev(x, c, z, y):
    return (x * 2 + c, z * 2 + y)


def greet(partners):
    bar = pltpu.get_barrier_semaphore()
    for p in partners:
        pl.semaphore_signal(bar, inc=1, device_id=p, device_id_type=MESH)
    pl.semaphore_wait(bar, len(partners))


def fwd_kernel(hd, heads, tok, cot, wp, fa, fb, fc, normed, qkvT, oT, lse, own, vec, wT, a1, a2, a3, dob, mgrad, bout, sums, ga, gb, gc,
               T, Ws, fb1, bt, up, r2, k1, r3, st, rt, lt, sy, ry, sc, rc, scy, rcy, sa, ra, la, sz, rz, sx, rx, so, ro, lo, ln,
               su, ru, lu, gss, grs, gsz, grz, gs1, gr1, gs2, gr2, gsc, grc, sf1, rf1, sf2, rf2, sf3, rf3, la1, la2, la3):
    x, c, z, y = place()
    hg = c * 2 + y
    W = heads * hd
    D = T.shape[2]
    R = T.shape[1]
    N = qkvT.shape[1]
    zoff = [lax.rem(z + k, 4) for k in (1, 2, 3)]
    sums[...] = jnp.zeros_like(sums)
    greet([dev(x, c, zz, y) for zz in zoff] + [dev(x, 1 - c, zz, y) for zz in zoff]
          + [dev(x, 1 - c, z, y), dev(x, c, z, 1 - y), dev(x, 1 - c, z, 1 - y), dev(1 - x, c, z, y)])
    sib, yp, diag, xp = dev(x, 1 - c, z, y), dev(x, c, z, 1 - y), dev(x, 1 - c, z, 1 - y), dev(1 - x, c, z, y)
    pos = (lax.div(z, 2) * 2 + y) * 2 + lax.rem(z, 2)
    tcp = []
    for i in range(2):
        zt = 2 * c + i
        cp = rcopy(tok.at[i], T.at[pos], st.at[i], rt.at[lax.rem(z, 2)], dev(x, lax.div(z, 2), zt, y))
        loc = pltpu.make_async_copy(tok.at[i], T.at[pos], lt)
        @pl.when(zt != z)
        def _():
            cp.start()
        @pl.when(zt == z)
        def _():
            loc.start()
        tcp.append((zt, cp, loc))
    xz = x * 4 + z
    wloc = pltpu.make_async_copy(wp.at[hg], Ws.at[xz, hg], la)
    wloc.start()
    wa = []
    for k, (d, g) in enumerate(((yp, c * 2 + 1 - y), (sib, (1 - c) * 2 + y), (diag, (1 - c) * 2 + 1 - y))):
        cp = rcopy(wp.at[g], Ws.at[xz, hg], sa.at[k], ra.at[k], d)
        cp.start()
        wa.append(cp)
    wloc.wait()
    for cp in wa:
        cp.wait()
    wz = []
    for k in range(3):
        cp = rcopy(Ws.at[xz], Ws.at[xz], sz.at[k], rz.at[k], dev(x, c, zoff[k], y))
        cp.start()
        wz.append(cp)
    wx = [rcopy(Ws.at[xz], Ws.at[xz], sx.at[3], rx.at[3], xp)]
    wx[0].start()
    ca = 1 - c
    gat = ((fa, ga, True), (fb, gb, False), (fc, gc, False))

    def zz_of(u):
        return z if u == 0 else (z - u if u <= 3 else z + (u - 3))

    def ok(u):
        return True if u == 0 else (z >= u if u <= 3 else z + (u - 3) <= 3)

    def guard(cond, f):
        if cond is True:
            f()
        else:
            pl.when(cond)(f)

    def g_start(p):
        f, g, _ = gat[p]
        return rcopy(f, g.at[x, c, z, y], gss.at[p], grs.at[p], sib)

    def g_z(p, u, down):
        g = gat[p][1]
        v = g.at[x, ca, zz_of(u), y]
        d = u if u <= 3 else u - 3
        k = d + (3 if down else 0)
        return rcopy(v, v, gsz.at[p, k], grz.at[p, k], dev(x, c, z - 1 if down else z + 1, y))

    def g_zarr(p, u):
        g = gat[p][1]
        v = g.at[x, ca, zz_of(u), y]
        return rcopy(v, v, gsz.at[p, u - 1], grz.at[p, u - 1], sib)

    def g_one(p, u):
        g, xfirst = gat[p][1:]
        v = g.at[x, ca, zz_of(u), y]
        return rcopy(v, v, gs1.at[p, u], gr1.at[p, u], xp if xfirst else yp)

    def g_two(p, u):
        g, xfirst = gat[p][1:]
        v = g.at[:, ca, zz_of(u), y] if xfirst else g.at[x, ca, zz_of(u)]
        return rcopy(v, v, gs2.at[p, u], gr2.at[p, u], yp if xfirst else xp)

    def g_core(p, u):
        v = gat[p][1].at[:, ca, zz_of(u)]
        return rcopy(v, v, gsc.at[p, u], grc.at[p, u], sib)

    def ag_own(p):
        g_start(p).wait()
        g_one(p, 0).start()

    def ag_z0(p):
        guard(z < 3, lambda: g_z(p, 0, False).start())
        guard(z > 0, lambda: g_z(p, 0, True).start())

    def ag_recv(p, d):
        for u in (d, d + 3):
            def go(u=u):
                g_zarr(p, u).wait_recv()
                if d < 3:
                    guard((z > 0) if u > 3 else (z < 3), lambda: g_z(p, u, u > 3).start())
                g_one(p, u).start()
            guard(ok(u), go)

    def units(d):
        return (0,) if d == 0 else (d, d + 3)

    def ag_two(p, d):
        for u in units(d):
            def go(u=u):
                g_one(p, u).wait()
                g_two(p, u).start()
            guard(ok(u), go)

    def ag_core(p, d):
        for u in units(d):
            def go(u=u):
                g_two(p, u).wait()
                g_core(p, u).start()
            guard(ok(u), go)

    def ag_end(p):
        for u in range(7):
            guard(ok(u), lambda: g_core(p, u).wait())
        for u in (0, 1, 2):
            guard((z >= u) & (z < 3), lambda: g_z(p, u, False).wait_send())
            guard((z + u <= 3) & (z > 0), lambda: g_z(p, u + 3 if u else 0, True).wait_send())

    for p in (2, 0, 1):
        g_start(p).start()
    for p in (2, 0, 1):
        ag_own(p)
    ycp, ccp, cycp = [], [], []
    for j in range(2):
        src_z = 2 * c + j
        p = hg * 2 + j
        arr = rcopy(tok.at[0], T.at[p], st.at[0], rt.at[j], sib)
        @pl.when(src_z != z)
        def _():
            arr.wait_recv()
        @pl.when(src_z == z)
        def _():
            pltpu.make_async_copy(tok.at[0], T.at[p], lt).wait()
        a = rcopy(T.at[p], T.at[p], sy.at[j], ry.at[j], yp)
        b = rcopy(T.at[p], T.at[p], sc.at[j], rc.at[j], sib)
        a.start()
        b.start()
        ycp.append(a)
        ccp.append(b)
    for k in range(3):
        wz[k].wait()
        zs = lax.rem(z + 3 - k, 4)
        cp = rcopy(Ws.at[x * 4 + zs], Ws.at[x * 4 + zs], sx.at[k], rx.at[k], xp)
        cp.start()
        wx.append(cp)
    ag_z0(2)
    ag_z0(0)
    for p in (2, 0, 1):
        ag_two(p, 0)
    for j in range(2):
        ycp[j].wait()
        p = (c * 2 + 1 - y) * 2 + j
        cp = rcopy(T.at[p], T.at[p], scy.at[j], rcy.at[j], sib)
        cp.start()
        cycp.append(cp)
    ag_z0(1)
    for cp in wx:
        cp.wait()
    for xx in range(2):
        for zz in range(4):
            for cc in range(2):
                for yy in range(2):
                    r = (xx * 2 + cc) * 8 + zz * 2 + yy
                    blk = Ws[xx * 4 + zz, cc * 2 + yy, 0:16, 3 * W:3 * W + 128].astype(f32)
                    vec[:, r * 32:(r + 1) * 32] = blk[:, 0:32]
                    fb1[:, r * 128:(r + 1) * 128] = blk[8:16, :]
                c0 = (xx * 2 + cc) * 256 + zz * 64
                wT[:, c0:c0 + 64] = Ws[xx * 4 + zz, cc * 2:cc * 2 + 2, :, 0:3 * W].reshape(64, 3 * W).T
    hours = jnp.zeros((1, 1), f32)
    for zz in range(4):
        hz = Ws[x * 4, (zz // 2) * 2, 0:16, 3 * W:3 * W + 128].astype(f32)[11:12, zz % 2:zz % 2 + 1]
        hours = jnp.where(z == zz, hz, hours)
    t = hours / 100.0
    for j in range(2):
        ccp[j].wait()
        cycp[j].wait()
    shift = t * vec[0:1, :] + vec[1:2, :]
    vec[14:15, :] = jnp.broadcast_to(t, (1, D))
    vec[15:16, :] = shift
    gain, bias = vec[2:3, :], vec[3:4, :]
    qb = vec[:, pl.ds(hg * W, W)].T
    def blk(p, carry):
        v = T[p].astype(f32) + shift
        cen = v - jnp.mean(v, axis=-1, keepdims=True)
        r = lax.rsqrt(jnp.mean(cen * cen, axis=-1, keepdims=True) + EPS)
        nb = (cen * r * gain + bias).astype(bf16)
        T[p] = nb
        pr = dot_nt(wT[...], nb)
        cols = pl.ds(p * R, R)
        qkvT[0:W, cols] = (pr[0:W] + qb[:, 4:5]).astype(bf16)
        qkvT[W:2 * W, cols] = pr[W:2 * W].astype(bf16)
        qkvT[2 * W:3 * W, cols] = (pr[2 * W:] + qb[:, 5:6]).astype(bf16)
        return carry
    own[...] = T[pl.ds(hg * 2, 2)]
    lax.fori_loop(0, T.shape[0], blk, 0)
    keep = pltpu.make_async_copy(T, normed, ln)
    keep.start()
    keep.wait()
    def cot_copy(i):
        zt = 2 * c + i
        return zt, rcopy(cot.at[i], up.at[lax.rem(z, 2)], su.at[i], ru.at[lax.rem(z, 2)], dev(x, lax.div(z, 2), zt, y))
    def cot_start():
        for i in range(2):
            zt, cp = cot_copy(i)
            @pl.when(zt != z)
            def _():
                cp.start()
            @pl.when(zt == z)
            def _():
                pltpu.make_async_copy(cot.at[i], up.at[lax.rem(z, 2)], lu).start()
    def cot_wait():
        for j in range(2):
            @pl.when(2 * c + j != z)
            def _():
                rcopy(cot.at[0], up.at[j], su.at[0], ru.at[j], sib).wait_recv()
            @pl.when(2 * c + j == z)
            def _():
                pltpu.make_async_copy(cot.at[0], up.at[j], lu).wait()
            zt, cp = cot_copy(j)
            @pl.when(zt != z)
            def _():
                cp.wait_send()
    def attention(k_s, o_s):
        for h in range(heads):
            k_s[h] = qkvT[W + h * hd:W + (h + 1) * hd, :].T
        QB, KB = 2 * R, 512
        cs = LOG2E * hd ** -0.5
        nk = N // KB
        PLAN = {0: [(ag_recv, 2, 1), (ag_recv, 0, 1), (ag_core, 2, 0), (ag_core, 0, 0)], 1: [(ag_recv, 1, 1), (ag_core, 1, 0)],
                2: [(ag_two, 2, 1), (ag_two, 0, 1)], 3: [(ag_recv, 2, 2), (ag_recv, 0, 2)], 4: [(ag_recv, 1, 2)], 5: [(ag_two, 1, 1)],
                6: [(ag_two, 2, 2), (ag_two, 0, 2), (ag_core, 2, 1), (ag_core, 0, 1)], 7: [(ag_recv, 2, 3), (ag_recv, 0, 3)],
                8: [(ag_recv, 1, 3)], 9: [(ag_two, 1, 2), (ag_core, 1, 1)], 10: [(ag_two, 2, 3), (ag_two, 0, 3), (ag_core, 2, 2), (ag_core, 0, 2)],
                12: [(ag_two, 1, 3), (ag_core, 1, 2)], 14: [(ag_core, 2, 3), (ag_core, 0, 3)]}
        def group(k, carry):
            cc = jnp.where((k == 1) | (k == 2), 1 - c, c)
            yy = jnp.where(k < 2, 1 - y, y)
            g = cc * 2 + yy
            qcols = pl.ds(g * QB, QB)
            def head(h, carry):
                step = k * heads + h
                for when, work in PLAN.items():
                    @pl.when(step == when)
                    def _():
                        for f, p, d in work:
                            f(p, d)
                @pl.when(step == 9)
                def _():
                    cot_start()
                qt = qkvT[pl.ds(h * hd, hd), qcols]
                def scores(i):
                    return dot_nn(k_s[h, i * KB:(i + 1) * KB, :], qt)
                m = None
                s = scores(0)
                for i in range(nk):
                    nxt = scores(i + 1) if i + 1 < nk else None
                    cm = jnp.max(s, axis=0, keepdims=True)
                    mn = cm if m is None else jnp.maximum(m, cm)
                    p = jnp.exp2(s * cs - mn * cs)
                    ps = jnp.sum(p, axis=0, keepdims=True)
                    vt = qkvT[pl.ds(2 * W + h * hd, hd), i * KB:(i + 1) * KB]
                    ov = dot_nn(vt, p.astype(bf16))
                    if m is None:
                        l, o = ps, ov
                    else:
                        a = jnp.exp2((m - mn) * cs)
                        l = l * a + ps
                        o = o * a + ov
                    m = mn
                    s = nxt
                o = o / l
                o_s[g, pl.ds(h * hd, hd), :] = o.astype(bf16)
                oT[pl.ds(h * hd, hd), qcols] = o
                lse[pl.ds(h, 1), qcols] = m * cs + jnp.log2(l)
                return carry
            lax.fori_loop(0, heads, head, 0)
            @pl.when(k < 3)
            def _():
                rcopy(o_s.at[g], bt.at[hg], so.at[k], ro.at[k], dev(x, cc, z, yy)).start()
            @pl.when(k == 3)
            def _():
                pltpu.make_async_copy(o_s.at[g], bt.at[hg], lo).start()
            return carry
        lax.fori_loop(0, 4, group, 0)
        for k, d in enumerate((yp, diag, sib)):
            rcopy(o_s.at[0], bt.at[hg], so.at[k], ro.at[k], d).wait()
        pltpu.make_async_copy(o_s.at[0], bt.at[hg], lo).wait()
    pl.run_scoped(attention, pltpu.VMEM((heads, N, hd), bf16), pltpu.VMEM((4, W, 2 * R), bf16))
    for i in range(2):
        zt, cp, loc = tcp[i]
        @pl.when(zt != z)
        def _():
            cp.wait_send()


    FF = fb1.shape[1]
    C = 2 * R

    def middle_part(Wo, mid_s, n2, n2T, oacc, dacc, f1b, f2b, sb1, sb2, sb3, lw, l1, l2):
        ag_core(1, 3)
        ag_end(2)
        cpw = pltpu.make_async_copy(gc, Wo, lw)
        cpw.start()
        bT = bt[...].reshape(4 * W, C).T
        cpw.wait()
        w_o = Wo[...].reshape(D, D)
        def norm(v):
            cen = v - jnp.mean(v, axis=-1, keepdims=True)
            return cen, lax.rsqrt(jnp.mean(cen * cen, axis=-1, keepdims=True) + EPS)
        for j in range(2):
            v = own[j].astype(f32) + vec[15:16, :] + dot_nn(bT[j * R:(j + 1) * R], w_o) + vec[6:7, :]
            mid_s[j] = v
            cen, r = norm(v)
            nb = (cen * r * vec[7:8, :] + vec[8:9, :]).astype(bf16)
            n2[j] = nb
            n2T[:, :, j * R:(j + 1) * R] = nb.T.reshape(4, D // 4, R)
        ag_end(0)
        ag_end(1)
        cot_wait()

        def order(s):
            cc = jnp.where(s < 4, 1 - c, c)
            xx = jnp.where(lax.rem(lax.div(s, 2), 2) == 0, x, 1 - x)
            zp = lax.rem(s, 2)
            return xx, cc, zp, (xx * 2 + cc) * 2 + zp
        def loads(s):
            xx, cc, zp, j = order(s)
            slot = lax.rem(s, 2)
            return (pltpu.make_async_copy(ga.at[:, :, :, :, :, pl.ds(pl.multiple_of(j * C, C), C)], f1b.at[slot], l1.at[slot]),
                    pltpu.make_async_copy(gb.at[xx, cc, pl.ds(zp * 2, 2)], f2b.at[slot], l2.at[slot]))
        for cp in loads(0):
            cp.start()
        oacc[...] = jnp.zeros_like(oacc)
        dacc[...] = jnp.zeros_like(dacc)
        def sends(s):
            slot = lax.rem(s, 2)
            return (rcopy(sb1.at[slot], T.at[lax.rem(s + 4, 8)], sf1.at[s], rf1.at[lax.rem(s + 4, 8)], sib),
                    rcopy(sb2.at[slot], r2.at[lax.rem(s, 4)], sf2.at[lax.rem(s, 4)], rf2.at[lax.rem(s, 4)], sib))
        def out1(s):
            j = order(s)[3]
            return [pltpu.make_async_copy(T.at[s, :, pl.ds(q * C, C)], a1.at[q, :, pl.ds(pl.multiple_of(j * C, C), C)], la1.at[s, q]) for q in range(2)]
        def out2(s):
            xx, cc, zp, j = order(s)
            return pltpu.make_async_copy(r2.at[s - 4], a2.at[xx, zp], la2.at[s - 4])
        def chunk(s, carry):
            slot = lax.rem(s, 2)
            xx, cc, zp, j = order(s)
            for cp in loads(s):
                cp.wait()
            @pl.when(s < 7)
            def _():
                for cp in loads(s + 1):
                    cp.start()
            @pl.when(s >= 2)
            def _():
                sends(s - 2)[0].wait_send()
            @pl.when((s >= 2) & (s < 6))
            def _():
                sends(s - 2)[1].wait_send()
            f1c = f1b[slot].reshape(D, C)
            f2c = f2b[slot].reshape(C, D)
            u2 = up[...].reshape(C, D)
            h = dot_nn(n2[...].reshape(C, D), f1c) + fb1[2:3, pl.ds(pl.multiple_of(j * C, C), C)]
            da = dot_nt(u2, f2c)
            ph = 0.5 + 0.5 * lax.erf(h * 0.7071067811865476)
            act = (h * ph).astype(bf16)
            hgr = (da * (ph + h * (jnp.exp(-0.5 * h * h) * 0.3989422804014327))).astype(bf16)
            oacc[...] += dot_nn(act, f2c).reshape(2, R, D)
            sums[pl.ds(4 + lax.div(j, 2), 1), pl.ds(pl.multiple_of(lax.rem(j, 2) * C, C), C)] = jnp.sum(hgr.astype(f32), axis=0, keepdims=True)
            g2 = dot_nn(act.T, u2)
            dacc[...] += dot_nt(hgr, f1c).reshape(2, R, D)
            for q in range(2):
                sb1[slot, :, q * C:(q + 1) * C] = dot_nn(n2T[q * 2 + 1 - c], hgr).astype(bf16)
            @pl.when(s < 4)
            def _():
                sb2[slot] = g2.astype(bf16)
                sends(s)[1].start()
                for q in range(2):
                    k1[s, :, q * C:(q + 1) * C] = dot_nn(n2T[q * 2 + c], hgr).astype(bf16)
            sends(s)[0].start()
            @pl.when(s >= 4)
            def _():
                sends(s)[1].wait_recv()
                r2[s - 4] = (r2[s - 4].astype(f32) + g2).astype(bf16)
                out2(s).start()
                rcopy(sb1.at[0], T.at[s], sf1.at[0], rf1.at[s], sib).wait_recv()
                for q in range(2):
                    cols = slice(q * C, (q + 1) * C)
                    T[s, :, cols] = (T[s, :, cols].astype(f32) + dot_nn(n2T[q * 2 + c], hgr)).astype(bf16)
                for cp in out1(s):
                    cp.start()
            return carry
        lax.fori_loop(0, 8, chunk, 0)

        tot = [jnp.zeros((1, D), f32) for _ in range(4)]
        ags = []
        for j in range(2):
            v = mid_s[j]
            bout[j] = (v + oacc[j] + vec[9:10, :]).astype(bf16)
            cen, r = norm(v)
            xh = cen * r
            u = dacc[j]
            e = u * vec[7:8, :]
            g = up[j].astype(f32) + r * (e - jnp.mean(e, axis=-1, keepdims=True) - xh * jnp.mean(e * xh, axis=-1, keepdims=True))
            mgrad[j] = g
            ag = g.astype(bf16)
            ags.append(ag)
            for n, val in enumerate((ag.astype(f32), u * xh, u, up[j].astype(f32))):
                tot[n] = tot[n] + jnp.sum(val, axis=0, keepdims=True)
        for n in range(4):
            sums[n:n + 1, :] = tot[n]
        ag = jnp.concatenate(ags, axis=0)
        for q in range(2):
            sb3[q] = dot_nn(bt[q * 2 + 1 - c], ag).astype(bf16)
            rcopy(sb3.at[q], r3.at[q], sf3.at[q], rf3.at[q], sib).start()
        for q in range(4):
            dob[q] = dot_nt(Wo[q // 2, q % 2].reshape(D // 4, D), ag).astype(bf16)
        for s in range(4):
            rcopy(sb1.at[0], T.at[s], sf1.at[0], rf1.at[s], sib).wait_recv()
            T[s] = (T[s].astype(f32) + k1[s].astype(f32)).astype(bf16)
            for cp in out1(s):
                cp.start()
        for q in range(2):
            rcopy(sb3.at[q], r3.at[q], sf3.at[q], rf3.at[q], sib).wait()
            r3[q] = (r3[q].astype(f32) + dot_nn(bt[q * 2 + c], ag)).astype(bf16)
        cp3 = pltpu.make_async_copy(r3, a3, la3)
        cp3.start()
        for s in (6, 7):
            sends(s)[0].wait_send()
        for s in range(8):
            for cp in out1(s):
                cp.wait()
        for s in range(4, 8):
            out2(s).wait()
        cp3.wait()

    SD = pltpu.SemaphoreType.DMA
    V = pltpu.VMEM
    pl.run_scoped(middle_part, V(gc.shape, bf16), V((2, R, D), f32), V((2, R, D), bf16), V((4, D // 4, C), bf16), V((2, R, D), f32),
                  V((2, R, D), f32), V((2,) + ga.shape[:5] + (C,), bf16), V((2, 2) + gb.shape[3:], bf16),
                  V((2, D // 4, 2 * C), bf16), V((2, C, D), bf16), V((2, D // 4, D), bf16), SD, SD((2,)), SD((2,)))


def forward_kernel(tok, cot, wp, fa, fb, fc, heads, hd):
    n_it, R, D = tok.shape
    FF = fa.shape[1]
    W = heads * hd
    N = 8 * R
    C = 2 * R
    S = pltpu.SemaphoreType.DMA
    V = pltpu.VMEM
    vm = pl.BlockSpec(memory_space=pltpu.VMEM)
    hbm = pl.BlockSpec(memory_space=pl.ANY)
    sd = jax.ShapeDtypeStruct
    full = lambda a: sd((2, 2, 4, 2) + a.shape, bf16)
    return pl.pallas_call(
        functools.partial(fwd_kernel, hd, heads),
        in_specs=[hbm] * 6,
        out_specs=[hbm] + [vm] * 6 + [hbm] * 3 + [vm] * 4 + [hbm] * 3,
        out_shape=[
            sd((8, R, D), bf16), sd((3 * W, N), bf16), sd((W, N), f32), sd((heads, N), f32), sd((2, R, D), bf16), sd((16, D), f32),
            sd((3 * W, D), bf16), sd((2, D // 4, FF), bf16), sd((2, 2, C, D), bf16), sd((2, D // 4, D), bf16), sd((4, W, C), bf16),
            sd((2, R, D), f32), sd((2, R, D), bf16), sd((16, D), f32), full(fa), full(fb), full(fc),
        ],
        scratch_shapes=[
            V((8, R, D), bf16), V((8, 4, 32, 3 * W + 128), bf16), V((8, FF), f32), V((4, W, C), bf16), V((2, R, D), bf16),
            V((4, C, D), bf16), V((4, D // 4, D), bf16), V((2, D // 4, D), bf16),
            S((2,)), S((2,)), S, S((2,)), S((2,)), S((2,)), S((2,)), S((2,)), S((2,)),
            S((3,)), S((3,)), S, S((3,)), S((3,)), S((4,)), S((4,)), S((3,)), S((3,)), S, S,
            S((2,)), S((2,)), S, S((3,)), S((3,)), S((3, 6)), S((3, 6)), S((3, 7)), S((3, 7)), S((3, 7)), S((3, 7)), S((3, 7)), S((3, 7)),
            S((8,)), S((8,)), S((4,)), S((4,)), S((2,)), S((2,)), S((8, 2)), S((4,)), S,
        ],
        compiler_params=pltpu.CompilerParams(collective_id=0, has_side_effects=True, vmem_limit_bytes=60 << 20),
        name="forward",
    )(tok, cot, wp, fa, fb, fc)


def put_sum(dst, pieces):
    total = pieces[0].astype(f32)
    for p in pieces[1:]:
        total = total + p.astype(f32)
    dst[...] = total.astype(dst.dtype)


def tail_kernel(hd, heads, dob, qkvT, oT, lse, a1, a2, a3, normed, wT, own, rows, mgrad, sums0, bout,
                o1, o2, o3, gq, home, sums, bo,
                do_s, dq_s, k1, r11, r12, r13, k2, r21, r22, r23, k3, r31, r32, r33,
                Gb, gx, gz, go, ds_s, dr_c, dy_s, dr_y, ig, hm, vs, vr,
                sd, rd, ld, s1, q1, s2, q2, s3, q3, lk, sg, qg, sgz, qgz, sga, qga, sdc, qdc, sdy, qdy, sh, qh, lh, sv, qv, ll, sb, qb, lb):
    x, c, z, y = place()
    hg = c * 2 + y
    W = heads * hd
    N = qkvT.shape[1]
    zoff = [lax.rem(z + k, 4) for k in (1, 2, 3)]
    sib, yp, diag, xp = dev(x, 1 - c, z, y), dev(x, c, z, 1 - y), dev(x, 1 - c, z, 1 - y), dev(1 - x, c, z, y)
    zp = [dev(x, c, zz, y) for zz in zoff]
    greet(zp + [dev(x, 1 - c, zz, y) for zz in zoff] + [sib, yp, diag, xp])
    peers = ((sib, (1 - c) * 2 + y), (yp, c * 2 + 1 - y), (diag, (1 - c) * 2 + 1 - y))
    for k, (d, g) in enumerate(peers):
        rcopy(dob.at[g], do_s.at[hg], sd.at[k], rd.at[k], d).start()
    loc = pltpu.make_async_copy(dob.at[hg], do_s.at[hg], ld)
    loc.start()

    def part(ref, h, n):
        return ref if n is None else ref.at[..., pl.ds(h * n, n), :]
    n1, n2 = k1.shape[2] // 2, k2.shape[2] // 2

    class Piece:
        def __init__(self, i, h, n, a, k, r1, r2, r3, out, s, q, lsem, yfirst):
            self.a, self.k, self.r1, self.r2, self.r3, self.out = [part(v, h, n) for v in (a, k, r1, r2, r3, out)]
            self.s, self.q, self.lsem, self.yfirst, self.b = s, q, lsem, yfirst, h * 5
            self.i = i
        def copies(self):
            b, s, q = self.b, self.s, self.q
            if self.yfirst:
                first = rcopy(self.a.at[:, :, 1 - y], self.r1, s.at[b], q.at[b], yp)
                second = rcopy(self.k.at[1 - x], self.r2, s.at[b + 1], q.at[b + 1], xp)
                kept = self.a.at[:, :, y]
                mine = lambda zz: self.k.at[x, zz]
            else:
                first = rcopy(self.a.at[1 - x], self.r1, s.at[b], q.at[b], xp)
                second = rcopy(self.k.at[:, 1 - y], self.r2, s.at[b + 1], q.at[b + 1], yp)
                kept = self.a.at[x]
                mine = lambda zz: self.k.at[zz, y]
            zs = [rcopy(mine(zoff[j]), self.r3.at[j], s.at[b + 2 + j], q.at[b + 2 + j], zp[j]) for j in range(3)]
            return first, second, zs, pltpu.make_async_copy(kept, self.k, self.lsem.at[self.i]), mine
        def start(self):
            first, _, _, keep, _ = self.copies()
            keep.start()
            first.start()
        def second(self):
            first, second, _, keep, _ = self.copies()
            keep.wait()
            first.wait()
            n0, n1_ = self.k.shape[0], self.k.shape[1]
            def add(j, carry):
                p, q_ = lax.div(j, n1_), lax.rem(j, n1_)
                put_sum(self.k.at[p, q_], [self.k[p, q_], self.r1[p, q_]])
                return carry
            lax.fori_loop(0, n0 * n1_, add, 0)
            second.start()
        def third(self):
            _, second, zs, _, mine = self.copies()
            second.wait()
            def add(zz, carry):
                put_sum(mine(zz), [mine(zz)[...], self.r2[zz]])
                return carry
            lax.fori_loop(0, 4, add, 0)
            for cp in zs:
                cp.start()
        def finish(self):
            _, _, zs, _, mine = self.copies()
            for cp in zs:
                cp.wait()
            put_sum(self.out, [mine(z)[...]] + [self.r3[j] for j in range(3)])

    f1 = [Piece(h, h, n1, a1, k1, r11, r12, r13, o1, s1, q1, lk, True) for h in range(2)]
    f2 = [Piece(2 + h, h, n2, a2, k2, r21, r22, r23, o2, s2, q2, lk, False) for h in range(2)]
    f3 = Piece(4, 0, None, a3, k3, r31, r32, r33, o3, s3, q3, lk, False)
    f2[0].start()
    f1[0].start()

    def out_copy(j):
        zt = 2 * c + j
        return zt, rcopy(bout.at[j], bo.at[lax.rem(z, 2)], sb.at[j], qb.at[lax.rem(z, 2)], dev(x, lax.div(z, 2), zt, y))
    def out_start():
        for j in range(2):
            zt, cp = out_copy(j)
            @pl.when(zt != z)
            def _():
                cp.start()
            @pl.when(zt == z)
            def _():
                pltpu.make_async_copy(bout.at[j], bo.at[lax.rem(z, 2)], lb).start()
    def out_wait():
        for i in range(2):
            @pl.when(2 * c + i != z)
            def _():
                rcopy(bout.at[0], bo.at[i], sb.at[0], qb.at[i], sib).wait_recv()
            @pl.when(2 * c + i == z)
            def _():
                pltpu.make_async_copy(bout.at[0], bo.at[i], lb).wait()
            zt, cp = out_copy(i)
            @pl.when(zt != z)
            def _():
                cp.wait_send()
    out_start()

    QB, KB = N // 4, 512
    cs = LOG2E * hd ** -0.5
    sc = hd ** -0.5
    nk = N // KB

    def attention(k_s, v_s, dk_s, dv_s):
        for h in range(heads):
            k_s[h] = qkvT[W + h * hd:W + (h + 1) * hd, :].T
            v_s[h] = qkvT[2 * W + h * hd:2 * W + (h + 1) * hd, :].T
        dk_s[...] = jnp.zeros_like(dk_s)
        dv_s[...] = jnp.zeros_like(dv_s)
        loc.wait()
        def group(k, carry):
            @pl.when(k > 0)
            def _():
                rcopy(dob.at[0], do_s.at[0], sd.at[k - 1], rd.at[k - 1], sib).wait()
            cc = jnp.where((k == 1) | (k == 3), 1 - c, c)
            yy = jnp.where(k >= 2, 1 - y, y)
            g = cc * 2 + yy
            qcols = pl.ds(g * QB, QB)
            def head(h, carry):
                @pl.when((k == 1) & (h == 1))
                def _():
                    f2[1].start()
                    f1[1].start()
                @pl.when((k == 2) & (h == 1))
                def _():
                    f2[0].second()
                @pl.when((k == 2) & (h == 3))
                def _():
                    f1[0].second()
                    f3.start()
                hr = pl.ds(h * hd, hd)
                qt = qkvT[hr, qcols]
                dt = do_s[g, hr, :]
                delta = jnp.sum(dt.astype(f32) * oT[hr, qcols], axis=0, keepdims=True)
                ls = lse[pl.ds(h, 1), qcols]
                def first(i):
                    ks = slice(i * KB, (i + 1) * KB)
                    return dot_nn(k_s[h, ks, :], qt), dot_nn(v_s[h, ks, :], dt)
                dq = None
                cur = first(0)
                for i in range(nk):
                    nxt = first(i + 1) if i + 1 < nk else None
                    s, dp = cur
                    ks = slice(i * KB, (i + 1) * KB)
                    p = jnp.exp2(s * cs - ls)
                    ds = (p * (dp - delta)).astype(bf16)
                    prt = dot_nn(qkvT[pl.ds(W + h * hd, hd), ks], ds)
                    dq = prt if dq is None else dq + prt
                    dk_s[h, :, ks] += dot_nt(qt, ds)
                    dv_s[h, :, ks] += dot_nt(dt, p.astype(bf16))
                    cur = nxt
                dq_s[hr, qcols] = (dq * sc).astype(bf16)
                return carry
            lax.fori_loop(0, heads, head, 0)
            return carry
        lax.fori_loop(0, 4, group, 0)
        for h in range(heads):
            dq_s[W + h * hd:W + (h + 1) * hd, :] = (dk_s[h] * sc).astype(bf16)
            dq_s[2 * W + h * hd:2 * W + (h + 1) * hd, :] = dv_s[h].astype(bf16)

    pl.run_scoped(attention, pltpu.VMEM((heads, N, hd), bf16), pltpu.VMEM((heads, N, hd), bf16),
                  pltpu.VMEM((heads, hd, N), f32), pltpu.VMEM((heads, hd, N), f32))

    def after(nm, w_s, tok_s, mg_s, dn, lsem):
        R = tok_s.shape[1]
        loads = [pltpu.make_async_copy(a, b, lsem.at[i]) for i, (a, b) in enumerate(((normed, nm), (wT, w_s), (own, tok_s), (mgrad, mg_s)))]
        for cp in loads:
            cp.start()
        loads[1].wait()
        def proj(g, j):
            cols = pl.ds(g * QB + j * R, R)
            return dot_nn(dq_s[:, cols].T, w_s[...])
        g_sy, g_s, g_oy = (1 - c) * 2 + 1 - y, (1 - c) * 2 + y, c * 2 + 1 - y
        def to_sib(a, j):
            return rcopy(ds_s.at[a, j], dr_c.at[a, j], sdc.at[a * 2 + j], qdc.at[a * 2 + j], sib)
        def to_y(j):
            return rcopy(dy_s.at[j], dr_y.at[j], sdy.at[j], qdy.at[j], yp)
        for j in range(2):
            ds_s[0, j] = proj(g_sy, j).astype(bf16)
            to_sib(0, j).start()
        for j in range(2):
            mine = proj(g_oy, j)
            to_sib(0, j).wait()
            dy_s[j] = (mine + dr_c[0, j].astype(f32)).astype(bf16)
            to_y(j).start()
        f2[1].second()
        f1[1].second()
        loads[0].wait()
        nm2 = nm[...].reshape(N, nm.shape[2])
        for q in range(3):
            t = dot_nn(dq_s[q * W:(q + 1) * W, :], nm2).astype(bf16).T
            Gb[..., q * W:(q + 1) * W] = t.reshape(2, 2, 4, 2, Gb.shape[4], W)
        gxc = rcopy(Gb.at[1 - x], gx, sg, qg, xp)
        gxc.start()
        for j in range(2):
            ds_s[1, j] = proj(g_s, j).astype(bf16)
            to_sib(1, j).start()
        for j in range(2):
            dn[j] = proj(hg, j)
        f2[0].third()
        f1[0].third()
        f3.second()
        ones = jnp.ones((8, N), bf16)
        vs[...] = sums0[...]
        for row, q in ((12, 0), (13, 2)):
            tot = dot_nt(ones, dq_s[q * W:(q + 1) * W, :])
            vs[row:row + 1, :] = jnp.zeros((1, vs.shape[1]), f32)
            vs[row:row + 1, pl.ds(pl.multiple_of(hg * W, W), W)] = tot[0:1]
        gxc.wait()
        for cc in range(2):
            for zz in range(4):
                put_sum(Gb.at[x, cc, zz], [Gb[x, cc, zz], gx[cc, zz]])
        gzs = [rcopy(Gb.at[x, :, zoff[j]], gz.at[j], sgz.at[j], qgz.at[j], zp[j]) for j in range(3)]
        for cp in gzs:
            cp.start()
        f2[1].third()
        f1[1].third()
        gain = rows[2:3, :]
        shift = rows[15:16, :]
        acc = [jnp.zeros((1, dn.shape[2]), f32) for _ in range(3)]
        loads[2].wait()
        loads[3].wait()
        homes = []
        for j in range(2):
            to_sib(1, j).wait()
            to_y(j).wait()
            u = dn[j] + dr_c[1, j].astype(f32) + dr_y[j].astype(f32)
            v = tok_s[j].astype(f32) + shift
            cen = v - jnp.mean(v, axis=-1, keepdims=True)
            r = lax.rsqrt(jnp.mean(cen * cen, axis=-1, keepdims=True) + EPS)
            xh = cen * r
            e = u * gain
            res = mg_s[j] + r * (e - jnp.mean(e, axis=-1, keepdims=True) - xh * jnp.mean(e * xh, axis=-1, keepdims=True))
            ig[j] = res.astype(bf16)
            for n, val in enumerate((u * xh, u, res)):
                acc[n] = acc[n] + jnp.sum(val, axis=0, keepdims=True)
            zt = 2 * c + j
            cp = rcopy(ig.at[j], hm.at[lax.rem(z, 2)], sh.at[j], qh.at[lax.rem(z, 2)], dev(x, lax.div(z, 2), zt, y))
            lc = pltpu.make_async_copy(ig.at[j], hm.at[lax.rem(z, 2)], lh)
            @pl.when(zt != z)
            def _():
                cp.start()
            @pl.when(zt == z)
            def _():
                lc.start()
            homes.append((zt, cp, lc))
        vs[8:9, :] = acc[0]
        vs[9:10, :] = acc[1]
        vs[10:11, :] = acc[2] * rows[14:15, :]
        vs[11:12, :] = acc[2]
        for k, d in enumerate((sib, yp, xp)):
            cp = rcopy(vs, vr.at[k], sv.at[k], qv.at[k], d)
            cp.start()
            cp.wait()
            vs[...] = vs[...] + vr[k]
        zv = [rcopy(vs, vr.at[3 + k], sv.at[3 + k], qv.at[3 + k], zp[k]) for k in range(3)]
        for cp in zv:
            cp.start()
        f3.third()
        for cp in gzs:
            cp.wait()
        for cc in range(2):
            for yy in range(2):
                put_sum(Gb.at[x, cc, z, yy], [Gb[x, cc, z, yy]] + [gz[k, cc, yy] for k in range(3)])
        gas = []
        for k, (d, cc, yy) in enumerate(((sib, 1 - c, y), (yp, c, 1 - y), (diag, 1 - c, 1 - y))):
            cp = rcopy(Gb.at[x, cc, z, yy], go.at[hg], sga.at[k], qga.at[k], d)
            cp.start()
            gas.append(cp)
        lcl = pltpu.make_async_copy(Gb.at[x, c, z, y], go.at[hg], ll)
        lcl.start()
        for cp in zv:
            cp.wait()
        sums[...] = vs[...] + vr[3] + vr[4] + vr[5]
        f2[0].finish()
        f1[0].finish()
        f2[1].finish()
        f1[1].finish()
        f3.finish()
        lcl.wait()
        for cp in gas:
            cp.wait()
        D = gq.shape[1] // 3
        for g in range(4):
            for q in range(3):
                gq[:, q * D + g * W:q * D + (g + 1) * W] = go[g, :, q * W:(q + 1) * W].astype(f32)
        for i in range(2):
            src = 2 * c + i
            arr = rcopy(ig.at[0], hm.at[i], sh.at[0], qh.at[i], sib)
            @pl.when(src != z)
            def _():
                arr.wait_recv()
            @pl.when(src == z)
            def _():
                pltpu.make_async_copy(ig.at[0], hm.at[i], lh).wait()
            home[i] = hm[i].astype(f32)
        out_wait()
        for zt, cp, lc in homes:
            @pl.when(zt != z)
            def _():
                cp.wait_send()

    R = own.shape[1]
    D = own.shape[2]
    pl.run_scoped(after, pltpu.VMEM(normed.shape, bf16), pltpu.VMEM(wT.shape, bf16), pltpu.VMEM((2, R, D), bf16),
                  pltpu.VMEM((2, R, D), f32), pltpu.VMEM((2, R, D), f32), pltpu.SemaphoreType.DMA((4,)))


def backward_kernel(dob, qkvT, oT, lse, a1, a2, a3, normed, wT, own, rows, mgrad, sums0, bout, heads, hd):
    W3, N = qkvT.shape
    W = heads * hd
    _, R, D = own.shape
    S = pltpu.SemaphoreType.DMA
    V = pltpu.VMEM
    vm = pl.BlockSpec(memory_space=pltpu.VMEM)
    hbm = pl.BlockSpec(memory_space=pl.ANY)
    b1, b2, b3 = a1.shape[3:], a2.shape[3:], a3.shape[3:]
    def bufs(b, yfirst):
        k = (2, 4) if yfirst else (4, 2)
        return [V(k + b, bf16), V(k + b, bf16), V((4,) + b, bf16), V((3,) + b, bf16)]
    rq = D // 32
    return pl.pallas_call(
        functools.partial(tail_kernel, hd, heads),
        in_specs=[hbm, vm, vm, vm, hbm, hbm, hbm, hbm, hbm, hbm, vm, hbm, vm, hbm],
        out_specs=[vm] * 6 + [hbm],
        out_shape=[
            jax.ShapeDtypeStruct(b1, f32), jax.ShapeDtypeStruct(b2, f32), jax.ShapeDtypeStruct(b3, f32),
            jax.ShapeDtypeStruct((rq, 3 * D), f32), jax.ShapeDtypeStruct((2, R, D), f32), jax.ShapeDtypeStruct((16, D), f32),
            jax.ShapeDtypeStruct((2, R, D), bf16),
        ],
        scratch_shapes=[V((4, W, N // 4), bf16), V((W3, N), bf16)] + bufs(b1, True) + bufs(b2, False) + bufs(b3, False) + [
            V((2, 2, 4, 2, rq, W3), bf16), V((2, 4, 2, rq, W3), bf16), V((3, 2, 2, rq, W3), bf16), V((4, rq, W3), bf16),
            V((2, 2, R, D), bf16), V((2, 2, R, D), bf16), V((2, R, D), bf16), V((2, R, D), bf16), V((2, R, D), bf16), V((2, R, D), bf16),
            V((16, D), f32), V((6, 16, D), f32),
            S((3,)), S((3,)), S, S((10,)), S((10,)), S((10,)), S((10,)), S((5,)), S((5,)), S((5,)),
            S, S, S((3,)), S((3,)), S((3,)), S((3,)), S((4,)), S((4,)), S((2,)), S((2,)), S((2,)), S((2,)), S, S((6,)), S((6,)), S,
            S((2,)), S((2,)), S,
        ],
        compiler_params=pltpu.CompilerParams(collective_id=1, has_side_effects=True, vmem_limit_bytes=60 << 20),
        name="backward",
    )(dob, qkvT, oT, lse, a1, a2, a3, normed, wT, own, rows, mgrad, sums0, bout)


HEADS = 16


epsilon = EPS


def norm_rows_s(values, gain, shift):
    center = values - jnp.mean(values, axis=-1, keepdims=True)
    spread = jnp.mean(center * center, axis=-1, keepdims=True)
    return center * lax.rsqrt(spread + epsilon) * gain + shift


def gelu_exact_s(values):
    return jax.nn.gelu(values, approximate=False)


def product(left, right):
    return jnp.dot(left, right, preferred_element_type=jnp.float32)


def product_tleft(left, right):
    return lax.dot_general(
        left, right, (((0,), (0,)), ((), ())), preferred_element_type=jnp.float32
    )


def product_tright(left, right):
    return lax.dot_general(
        left, right, (((1,), (1,)), ((), ())), preferred_element_type=jnp.float32
    )


def split_heads(values):
    return values.reshape(values.shape[0], HEADS, values.shape[1] // HEADS)


def attend(operands):
    queries, keys_all, values_all = operands
    scale = (queries.shape[1] // HEADS) ** (-0.5)
    scores = (
        jnp.einsum(
            "qhd,khd->hqk",
            split_heads(queries),
            split_heads(keys_all),
            preferred_element_type=jnp.float32,
        )
        * scale
    )
    highest = jnp.max(scores, axis=-1, keepdims=True)
    exps = jnp.exp(scores - highest)
    totals = jnp.sum(exps, axis=-1, keepdims=True)
    probs_low = (exps / totals).astype(jnp.bfloat16)
    blended = jnp.einsum(
        "hqk,khd->qhd", probs_low, split_heads(values_all), preferred_element_type=jnp.float32
    ).reshape(queries.shape)
    return (blended, (highest + jnp.log(totals))[:, :, 0])


def recompute_probs(queries, keys_all, values_all, grads_in, log_totals):
    scale = (queries.shape[1] // HEADS) ** (-0.5)
    scores = (
        jnp.einsum(
            "qhd,khd->hqk",
            split_heads(queries),
            split_heads(keys_all),
            preferred_element_type=jnp.float32,
        )
        * scale
    )
    probs = jnp.exp(scores - log_totals[:, :, None])
    prob_grads = jnp.einsum(
        "qhd,khd->hqk",
        split_heads(grads_in),
        split_heads(values_all),
        preferred_element_type=jnp.float32,
    )
    return (probs, prob_grads, scale)


def key_side_grads(score_grads, probs, queries, grads_in, row_count):
    key_grads = jnp.einsum(
        "hqk,qhd->khd", score_grads, split_heads(queries), preferred_element_type=jnp.float32
    )
    value_grads = jnp.einsum(
        "hqk,qhd->khd",
        probs.astype(jnp.bfloat16),
        split_heads(grads_in),
        preferred_element_type=jnp.float32,
    )
    width = queries.shape[1]
    return (key_grads.reshape(row_count, width), value_grads.reshape(row_count, width))


def query_side(with_keys, operands):
    queries, keys_all, values_all, grads_in, log_totals = operands
    probs, prob_grads, scale = recompute_probs(queries, keys_all, values_all, grads_in, log_totals)
    row_delta = jnp.sum(probs * prob_grads, axis=-1)
    score_grads = (probs * (prob_grads - row_delta[:, :, None]) * scale).astype(jnp.bfloat16)
    query_grads = jnp.einsum(
        "hqk,khd->qhd", score_grads, split_heads(keys_all), preferred_element_type=jnp.float32
    ).reshape(queries.shape)
    key_grads, value_grads = key_side_grads(
        score_grads, probs, queries, grads_in, keys_all.shape[0]
    )
    return (query_grads, row_delta, key_grads, value_grads)


def spread_on_device(
    tokens_in,
    lead_hours,
    cotangent,
    w_qkv,
    w_out,
    w_fc1,
    w_fc2,
    ln1_gain,
    ln1_bias,
    q_bias,
    v_bias,
    out_bias,
    ln2_gain,
    ln2_bias,
    fc1_bias,
    fc2_bias,
    lead_weight,
    lead_bias,
):
    gathered = (
        lax.all_gather(w_qkv, ("dp", "seq"), axis=0, tiled=True),
        lax.all_gather(w_out, ("dp", "seq"), axis=0, tiled=True),
        lax.all_gather(w_fc1, ("dp", "seq"), axis=0, tiled=True),
        lax.all_gather(w_fc2, ("dp", "seq"), axis=0, tiled=True),
        lax.all_gather(ln1_gain, ("dp", "seq"), axis=0, tiled=True),
        lax.all_gather(ln1_bias, ("dp", "seq"), axis=0, tiled=True),
        lax.all_gather(q_bias, ("dp", "seq"), axis=0, tiled=True),
        lax.all_gather(v_bias, ("dp", "seq"), axis=0, tiled=True),
        lax.all_gather(out_bias, ("dp", "seq"), axis=0, tiled=True),
        lax.all_gather(ln2_gain, ("dp", "seq"), axis=0, tiled=True),
        lax.all_gather(ln2_bias, ("dp", "seq"), axis=0, tiled=True),
        lax.all_gather(fc1_bias, ("dp", "seq"), axis=0, tiled=True),
        lax.all_gather(fc2_bias, ("dp", "seq"), axis=0, tiled=True),
        lax.all_gather(lead_weight, ("dp", "seq"), axis=0, tiled=True),
        lax.all_gather(lead_bias, ("dp", "seq"), axis=0, tiled=True),
    )
    (
        full_qkv,
        full_out,
        full_fc1,
        full_fc2,
        gain_one,
        shift_one,
        bias_query,
        bias_value,
        bias_out,
        gain_two,
        shift_two,
        bias_fc1,
        bias_fc2,
        lead_scale,
        lead_shift,
    ) = gathered
    items, rows, width = tokens_in.shape
    count = items * rows
    lead_times = lead_hours.astype(jnp.float32) / 100.0
    leading = (
        tokens_in.astype(jnp.float32)
        + lead_times[:, None, None] * lead_scale.astype(jnp.float32)
        + lead_shift.astype(jnp.float32)
    ).reshape(count, width)
    normed, norm_one_back = jax.vjp(
        norm_rows_s, leading, gain_one.astype(jnp.float32), shift_one.astype(jnp.float32)
    )
    normed_low = normed.astype(jnp.bfloat16)
    projected = product(normed_low, full_qkv)
    queries = (projected[:, :width] + bias_query.astype(jnp.float32)).astype(jnp.bfloat16)
    keys_own = projected[:, width : 2 * width].astype(jnp.bfloat16)
    values_own = (projected[:, 2 * width :] + bias_value.astype(jnp.float32)).astype(jnp.bfloat16)
    queries3 = queries.reshape(items, rows, width)
    keys_all, values_all = (
        lax.all_gather(keys_own.reshape(items, rows, width), "seq", axis=1, tiled=True),
        lax.all_gather(values_own.reshape(items, rows, width), "seq", axis=1, tiled=True),
    )
    blended, log_totals = lax.map(attend, (queries3, keys_all, values_all))
    blended_low = blended.reshape(count, width).astype(jnp.bfloat16)
    middle = leading + product(blended_low, full_out) + bias_out.astype(jnp.float32)
    normed_two, norm_two_back = jax.vjp(
        norm_rows_s, middle, gain_two.astype(jnp.float32), shift_two.astype(jnp.float32)
    )
    normed_two_low = normed_two.astype(jnp.bfloat16)
    hidden = product(normed_two_low, full_fc1) + bias_fc1.astype(jnp.float32)
    activated, gelu_back = jax.vjp(gelu_exact_s, hidden)
    activated_low = activated.astype(jnp.bfloat16)
    output = middle + product(activated_low, full_fc2) + bias_fc2.astype(jnp.float32)
    block_output = output.reshape(items, rows, width).astype(jnp.bfloat16)
    back_qkv, back_out, back_fc1, back_fc2 = (
        lax.all_gather(w_qkv, ("dp", "seq"), axis=0, tiled=True),
        lax.all_gather(w_out, ("dp", "seq"), axis=0, tiled=True),
        lax.all_gather(w_fc1, ("dp", "seq"), axis=0, tiled=True),
        lax.all_gather(w_fc2, ("dp", "seq"), axis=0, tiled=True),
    )
    out_grad = cotangent.reshape(count, width)
    upstream = out_grad.astype(jnp.float32)
    grad_fc2 = product_tleft(activated_low, out_grad)
    grad_fc2_bias = jnp.sum(upstream, axis=0)
    hidden_grad = gelu_back(product_tright(out_grad, back_fc2))[0].astype(jnp.bfloat16)
    grad_fc1 = product_tleft(normed_two_low, hidden_grad)
    grad_fc1_bias = jnp.sum(hidden_grad.astype(jnp.float32), axis=0)
    middle_part, grad_ln2_gain, grad_ln2_bias = norm_two_back(product_tright(hidden_grad, back_fc1))
    middle_grad = upstream + middle_part
    attn_grad = middle_grad.astype(jnp.bfloat16)
    grad_out = product_tleft(blended_low, attn_grad)
    grad_out_bias = jnp.sum(attn_grad.astype(jnp.float32), axis=0)
    blended_grad = (
        product_tright(attn_grad, back_out).astype(jnp.bfloat16).reshape(items, rows, width)
    )
    query_grads, row_delta, key_parts, value_parts = lax.map(
        partial(query_side, True), (queries3, keys_all, values_all, blended_grad, log_totals)
    )
    key_grads, value_grads = (
        lax.psum_scatter(
            key_parts.astype(jnp.bfloat16), "seq", scatter_dimension=1, tiled=True
        ).astype(jnp.float32),
        lax.psum_scatter(
            value_parts.astype(jnp.bfloat16), "seq", scatter_dimension=1, tiled=True
        ).astype(jnp.float32),
    )
    query_low = query_grads.reshape(count, width).astype(jnp.bfloat16)
    key_low = key_grads.reshape(count, width).astype(jnp.bfloat16)
    value_low = value_grads.reshape(count, width).astype(jnp.bfloat16)
    qkv_grad = jnp.concatenate([query_low, key_low, value_low], axis=1)
    grad_qkv = product_tleft(normed_low, qkv_grad)
    grad_q_bias = jnp.sum(query_low.astype(jnp.float32), axis=0)
    grad_v_bias = jnp.sum(value_low.astype(jnp.float32), axis=0)
    leading_part, grad_ln1_gain, grad_ln1_bias = norm_one_back(product_tright(qkv_grad, back_qkv))
    input_grad = (middle_grad + leading_part).reshape(items, rows, width)
    grad_lead_weight = jnp.sum(jnp.sum(input_grad, axis=1) * lead_times[:, None], axis=0)
    grad_lead_bias = jnp.sum(input_grad, axis=(0, 1))
    summed = (
        lax.psum_scatter(grad_qkv, ("dp", "seq"), scatter_dimension=0, tiled=True),
        lax.psum_scatter(grad_out, ("dp", "seq"), scatter_dimension=0, tiled=True),
        lax.psum_scatter(grad_fc1, ("dp", "seq"), scatter_dimension=0, tiled=True),
        lax.psum_scatter(grad_fc2, ("dp", "seq"), scatter_dimension=0, tiled=True),
        lax.psum_scatter(grad_ln1_gain, ("dp", "seq"), scatter_dimension=0, tiled=True),
        lax.psum_scatter(grad_ln1_bias, ("dp", "seq"), scatter_dimension=0, tiled=True),
        lax.psum_scatter(grad_q_bias, ("dp", "seq"), scatter_dimension=0, tiled=True),
        lax.psum_scatter(grad_v_bias, ("dp", "seq"), scatter_dimension=0, tiled=True),
        lax.psum_scatter(grad_out_bias, ("dp", "seq"), scatter_dimension=0, tiled=True),
        lax.psum_scatter(grad_ln2_gain, ("dp", "seq"), scatter_dimension=0, tiled=True),
        lax.psum_scatter(grad_ln2_bias, ("dp", "seq"), scatter_dimension=0, tiled=True),
        lax.psum_scatter(grad_fc1_bias, ("dp", "seq"), scatter_dimension=0, tiled=True),
        lax.psum_scatter(grad_fc2_bias, ("dp", "seq"), scatter_dimension=0, tiled=True),
        lax.psum_scatter(grad_lead_weight, ("dp", "seq"), scatter_dimension=0, tiled=True),
        lax.psum_scatter(grad_lead_bias, ("dp", "seq"), scatter_dimension=0, tiled=True),
    )
    return (block_output, input_grad) + tuple(summed)


def on_device(mesh_shape, tokens_in, lead_hours, cotangent, w_qkv, w_out, w_fc1, w_fc2, ln1_gain, ln1_bias, q_bias, v_bias,
              out_bias, ln2_gain, ln2_bias, fc1_bias, fc2_bias, lead_weight, lead_bias):
    x, c, z, y = place()
    _, R, D = tokens_in.shape
    FF = w_fc1.shape[1]
    hd = D // HEADS
    heads = HEADS // 4
    W = heads * hd
    rows = w_qkv.shape[0]
    small = jnp.zeros((32, 128), bf16)
    for k, v in enumerate((lead_weight, lead_bias, ln1_gain, ln1_bias, q_bias, v_bias, out_bias, ln2_gain, ln2_bias, fc2_bias)):
        small = small.at[k, :rows].set(v)
    small = small.at[10].set(fc1_bias).at[11, :2].set(lead_hours.astype(bf16))
    slices = w_qkv.reshape(rows, 3, 4, W).transpose(2, 0, 1, 3).reshape(4, rows, 3 * W)
    wp = jnp.concatenate([slices, jnp.broadcast_to(small, (4, 32, 128))], axis=2)
    normed, qkvT, oT, lse, own, vec, wT, a1, a2, a3, dob, mgrad, bout, sums0 = forward_kernel(
        tokens_in, cotangent, wp, w_fc1, w_fc2, w_out, heads, hd)[:14]
    grad_fc1, grad_fc2, grad_out, grad_qkv, home, sums, block_output = backward_kernel(
        dob, qkvT, oT, lse, a1.reshape(2, 4, 2, rows, FF), a2.reshape(2, 4, 2, -1, D), a3.reshape(2, 4, 2, rows, D), normed, wT,
        own, vec, mgrad, sums0, bout, heads, hd)
    index = (x * 2 + c) * 8 + z * 2 + y
    mine = lax.dynamic_slice(sums, (0, index * rows), (16, rows))
    g_fc1_bias = lax.dynamic_slice(sums[4:4 + FF // D].reshape(FF), (index * fc1_bias.shape[0],), (fc1_bias.shape[0],))
    return (block_output, home, grad_qkv, grad_out, grad_fc1, grad_fc2, mine[8], mine[9], mine[12], mine[13], mine[0],
            mine[1], mine[2], g_fc1_bias, mine[3], mine[10], mine[11])


def choose(mesh_shape, *args):
    items, rows = args[0].shape[0], args[3].shape[0]
    planes = mesh_shape["seq"] // 2
    if items == 2 and planes == 2 * items and mesh_shape["dp"] == 4 and rows % 16 == 0 and 4 * args[0].shape[1] == args[0].shape[2]:
        return on_device(mesh_shape, *args)
    return spread_on_device(*args)


def solution(mesh):
    big, rows, vec = P("dp", "seq", None), P(("dp", "seq"), None), P(("dp", "seq"))
    in_specs = (big, P("dp"), big) + (rows,) * 4 + (vec,) * 11
    out_specs = (big, big) + (rows,) * 4 + (vec,) * 11
    body = functools.partial(choose, dict(mesh.shape))
    return jax.shard_map(body, mesh=mesh, in_specs=in_specs, out_specs=out_specs, check_vma=False)
```

```python
import functools
from functools import partial
import jax, jax.numpy as jnp
from jax import lax
from jax.experimental import pallas as pl
from jax.experimental.pallas import tpu as pltpu
from jax.sharding import PartitionSpec as P

MESH = pl.DeviceIdType.MESH
f32, bf16 = jnp.float32, jnp.bfloat16
LOG2E = 1.4426950408889634
EPS = 1e-06


def dot_nn(a, b):
    return lax.dot_general(a, b, (((1,), (0,)), ((), ())), preferred_element_type=f32)


def dot_nt(a, b):
    return lax.dot_general(a, b, (((1,), (1,)), ((), ())), preferred_element_type=f32)


def rcopy(src, dst, ssem, rsem, dev):
    return pltpu.make_async_remote_copy(src_ref=src, dst_ref=dst, send_sem=ssem, recv_sem=rsem, device_id=dev, device_id_type=MESH)


def place():
    dp, seq = lax.axis_index("dp"), lax.axis_index("seq")
    return lax.div(dp, 2), lax.rem(dp, 2), lax.div(seq, 2), lax.rem(seq, 2)


def dev(x, c, z, y):
    return (x * 2 + c, z * 2 + y)


def greet(partners):
    bar = pltpu.get_barrier_semaphore()
    for p in partners:
        pl.semaphore_signal(bar, inc=1, device_id=p, device_id_type=MESH)
    pl.semaphore_wait(bar, len(partners))


def fwd_kernel(hd, heads, tok, cot, wq, small, fa, fb, fc, normed, qkvT, oT, lse, own, vec, wT, a1, h1, a2, h2, a3, dob, mgrad, bo, sums,
               ga, gb, gc, T, Ws, fb1, bt, up, r1, r2, r3, st, rt, lt, sy, ry, sc, rc, scy, rcy, sa, ra, la, sz, rz, sx, rx, so, ro, lo,
               ln, su, ru, lu, gss, grs, gsz, grz, gs1, gr1, gs2, gr2, gsc, grc, sf1, rf1, sf2, rf2, sf3, rf3, la1, la2, la3,
               sh1, qh1, sh2, qh2, sbo, qbo, lbo):
    x, c, z, y = place()
    hg = c * 2 + y
    W = heads * hd
    D = T.shape[2]
    R = T.shape[1]
    N = qkvT.shape[1]
    zoff = [lax.rem(z + k, 4) for k in (1, 2, 3)]
    sums[...] = jnp.zeros_like(sums)
    greet([dev(x, c, zz, y) for zz in zoff] + [dev(x, 1 - c, zz, y) for zz in zoff]
          + [dev(x, 1 - c, z, y), dev(x, c, z, 1 - y), dev(x, 1 - c, z, 1 - y), dev(1 - x, c, z, y)])
    sib, yp, diag, xp = dev(x, 1 - c, z, y), dev(x, c, z, 1 - y), dev(x, 1 - c, z, 1 - y), dev(1 - x, c, z, y)
    pos = (lax.div(z, 2) * 2 + y) * 2 + lax.rem(z, 2)
    tcp = []
    for i in range(2):
        zt = 2 * c + i
        cp = rcopy(tok.at[i], T.at[pos], st.at[i], rt.at[lax.rem(z, 2)], dev(x, lax.div(z, 2), zt, y))
        loc = pltpu.make_async_copy(tok.at[i], T.at[pos], lt)
        @pl.when(zt != z)
        def _():
            cp.start()
        @pl.when(zt == z)
        def _():
            loc.start()
        tcp.append((zt, cp, loc))
    xz = x * 4 + z
    def slices(g):
        dst = Ws.at[xz, hg]
        out = [(wq.at[:, pl.ds(pl.multiple_of(q * D + g * W, W), W)], dst.at[:, q * W:(q + 1) * W]) for q in range(3)]
        return out + [(small, dst.at[:, 3 * W:3 * W + 128])]
    wa = [pltpu.make_async_copy(a, b, la.at[n]) for n, (a, b) in enumerate(slices(hg))]
    for k, (d, g) in enumerate(((yp, c * 2 + 1 - y), (sib, (1 - c) * 2 + y), (diag, (1 - c) * 2 + 1 - y))):
        wa += [rcopy(a, b, sa.at[k, n], ra.at[k, n], d) for n, (a, b) in enumerate(slices(g))]
    for cp in wa:
        cp.start()
    for cp in wa:
        cp.wait()
    def zz_of(u):
        return z if u == 0 else (z - u if u <= 3 else z + (u - 3))

    def ok(u):
        return True if u == 0 else (z >= u if u <= 3 else z + (u - 3) <= 3)

    def guard(cond, f):
        if cond is True:
            f()
        else:
            pl.when(cond)(f)

    def w_z(u, down):
        v = Ws.at[x * 4 + zz_of(u)]
        k = (u if u <= 3 else u - 3) + (3 if down else 0)
        return rcopy(v, v, sz.at[k], rz.at[k], dev(x, c, z - 1 if down else z + 1, y))

    def w_arr(u):
        v = Ws.at[x * 4 + zz_of(u)]
        return rcopy(v, v, sz.at[u - 1], rz.at[u - 1], sib)

    def w_x(u):
        v = Ws.at[x * 4 + zz_of(u)]
        return rcopy(v, v, sx.at[u], rx.at[u], xp)

    def w_recv(d):
        for u in (d, d + 3):
            def go(u=u):
                w_arr(u).wait_recv()
                if d < 3:
                    guard((z > 0) if u > 3 else (z < 3), lambda: w_z(u, u > 3).start())
                w_x(u).start()
            guard(ok(u), go)

    guard(z < 3, lambda: w_z(0, False).start())
    guard(z > 0, lambda: w_z(0, True).start())
    w_x(0).start()
    ca = 1 - c
    gat = ((fa, ga, False), (fb, gb, True), (fc, gc, False))

    def g_start(p):
        f, g, _ = gat[p]
        return rcopy(f, g.at[x, c, z, y], gss.at[p], grs.at[p], sib)

    def g_z(p, u, down):
        g = gat[p][1]
        v = g.at[x, ca, zz_of(u), y]
        d = u if u <= 3 else u - 3
        k = d + (3 if down else 0)
        return rcopy(v, v, gsz.at[p, k], grz.at[p, k], dev(x, c, z - 1 if down else z + 1, y))

    def g_zarr(p, u):
        g = gat[p][1]
        v = g.at[x, ca, zz_of(u), y]
        return rcopy(v, v, gsz.at[p, u - 1], grz.at[p, u - 1], sib)

    def g_one(p, u):
        g, xfirst = gat[p][1:]
        v = g.at[x, ca, zz_of(u), y]
        return rcopy(v, v, gs1.at[p, u], gr1.at[p, u], xp if xfirst else yp)

    def g_two(p, u):
        g, xfirst = gat[p][1:]
        v = g.at[:, ca, zz_of(u), y] if xfirst else g.at[x, ca, zz_of(u)]
        return rcopy(v, v, gs2.at[p, u], gr2.at[p, u], yp if xfirst else xp)

    def g_core(p, u):
        v = gat[p][1].at[:, ca, zz_of(u)]
        return rcopy(v, v, gsc.at[p, u], grc.at[p, u], sib)

    def ag_own(p):
        g_start(p).wait()
        g_one(p, 0).start()

    def ag_z0(p, d):
        guard(z < 3, lambda: g_z(p, 0, False).start())
        guard(z > 0, lambda: g_z(p, 0, True).start())

    def ag_recv(p, d):
        for u in (d, d + 3):
            def go(u=u):
                g_zarr(p, u).wait_recv()
                if d < 3:
                    guard((z > 0) if u > 3 else (z < 3), lambda: g_z(p, u, u > 3).start())
                g_one(p, u).start()
            guard(ok(u), go)

    def units(d):
        return (0,) if d == 0 else (d, d + 3)

    def ag_two(p, d):
        for u in units(d):
            def go(u=u):
                g_one(p, u).wait()
                g_two(p, u).start()
            guard(ok(u), go)

    def ag_core(p, d):
        for u in units(d):
            def go(u=u):
                g_two(p, u).wait()
                g_core(p, u).start()
            guard(ok(u), go)

    def ag_got(p, half):
        own_half = ((0, True), (1, lax.rem(z, 2) == 1), (4, lax.rem(z, 2) == 0))
        rest = ((1, z == 2), (2, z >= 2), (3, z == 3), (4, z == 1), (5, z <= 1), (6, z == 0))
        for u, cond in (own_half if half == 0 else rest):
            guard(cond, lambda: g_core(p, u).wait())

    def ag_sent(p):
        for u in (0, 1, 2):
            guard((z >= u) & (z < 3), lambda: g_z(p, u, False).wait_send())
            guard((z + u <= 3) & (z > 0), lambda: g_z(p, u + 3 if u else 0, True).wait_send())

    PLAN = {
        0: ((ag_z0, 2, 0), (ag_two, 0, 0), (ag_two, 1, 0),),
        1: ((ag_two, 2, 0),),
        2: ((ag_z0, 1, 0),),
        3: ((ag_z0, 0, 0), (ag_core, 0, 0),),
        6: ((ag_recv, 0, 1), (ag_recv, 1, 1),),
        7: ((ag_recv, 0, 2), (ag_recv, 1, 2),),
        8: ((ag_two, 1, 1),),
        10: ((ag_two, 0, 1),),
        12: ((ag_core, 2, 0),),
        13: ((ag_recv, 2, 1), (ag_recv, 2, 2), (ag_recv, 0, 3),),
        14: ((ag_two, 0, 2),),
        16: ((ag_two, 2, 1), (ag_two, 2, 2), (ag_recv, 2, 3),),
        17: ((ag_core, 0, 1),),
        19: ((ag_recv, 1, 3),),
        20: ((ag_two, 2, 3),),
        21: ((ag_two, 1, 2),),
        22: ((ag_core, 2, 2),),
        23: ((ag_two, 0, 3), (ag_core, 1, 0),),
        24: ((ag_core, 2, 1), (ag_core, 2, 3), (ag_core, 0, 2), (ag_core, 1, 1),),
        25: ((ag_core, 0, 3),),
        26: ((ag_two, 1, 3),),
        28: ((ag_core, 1, 2),),
        29: ((ag_core, 1, 3),),
    }

    COT = 9

    def ag_slot(i):
        for f, p, d in PLAN.get(i, ()):
            f(p, d)

    for p in (2, 0, 1):
        g_start(p).start()
    for p in (2, 0, 1):
        ag_own(p)
    ag_slot(0)
    w_recv(1)
    ag_slot(1)
    ycp, ccp, cycp = [], [], []
    j0 = jnp.where(lax.div(z, 2) == c, lax.rem(z, 2), 0)
    for j in (j0, 1 - j0):
        src_z = 2 * c + j
        p = hg * 2 + j
        @pl.when(src_z != z)
        def _():
            rcopy(tok.at[0], T.at[p], st.at[0], rt.at[j], sib).wait_recv()
        @pl.when(src_z == z)
        def _():
            pltpu.make_async_copy(tok.at[0], T.at[p], lt).wait()
        a = rcopy(T.at[p], T.at[p], sy.at[j], ry.at[j], yp)
        b = rcopy(T.at[p], T.at[p], sc.at[j], rc.at[j], sib)
        a.start()
        b.start()
        ycp.append(a)
        ccp.append(b)
    ag_slot(2)
    w_recv(2)
    ag_slot(3)
    w_recv(3)
    ag_slot(4)
    for n, j in enumerate((j0, 1 - j0)):
        ycp[n].wait()
        p = (c * 2 + 1 - y) * 2 + j
        cp = rcopy(T.at[p], T.at[p], scy.at[j], rcy.at[j], sib)
        cp.start()
        cycp.append(cp)
    ag_slot(5)
    for u in range(7):
        guard(ok(u), lambda: w_x(u).wait())
    for u in (0, 1, 2):
        guard((z >= u) & (z < 3), lambda: w_z(u, False).wait_send())
        guard((z + u <= 3) & (z > 0), lambda: w_z(u + 3 if u else 0, True).wait_send())
    for xx in range(2):
        for zz in range(4):
            for cc in range(2):
                for yy in range(2):
                    r = (xx * 2 + cc) * 8 + zz * 2 + yy
                    blk = Ws[xx * 4 + zz, cc * 2 + yy, 0:16, 3 * W:3 * W + 128].astype(f32)
                    vec[:, r * 32:(r + 1) * 32] = blk[:, 0:32]
                    fb1[:, r * 128:(r + 1) * 128] = blk[8:16, :]
                c0 = (xx * 2 + cc) * 256 + zz * 64
                wT[:, c0:c0 + 64] = Ws[xx * 4 + zz, cc * 2:cc * 2 + 2, :, 0:3 * W].reshape(64, 3 * W).T
    hours = jnp.zeros((1, 1), f32)
    for zz in range(4):
        hz = Ws[x * 4, (zz // 2) * 2, 0:16, 3 * W:3 * W + 128].astype(f32)[11:12, zz % 2:zz % 2 + 1]
        hours = jnp.where(z == zz, hz, hours)
    t = hours / 100.0
    for j in range(2):
        ccp[j].wait()
        cycp[j].wait()
    ag_slot(6)
    shift = t * vec[0:1, :] + vec[1:2, :]
    vec[14:15, :] = jnp.broadcast_to(t, (1, D))
    vec[15:16, :] = shift
    gain, bias = vec[2:3, :], vec[3:4, :]
    qb = vec[:, pl.ds(hg * W, W)].T
    def blk(p, carry):
        v = T[p].astype(f32) + shift
        cen = v - jnp.mean(v, axis=-1, keepdims=True)
        r = lax.rsqrt(jnp.mean(cen * cen, axis=-1, keepdims=True) + EPS)
        nb = (cen * r * gain + bias).astype(bf16)
        T[p] = nb
        pr = dot_nt(wT[...], nb)
        cols = pl.ds(p * R, R)
        qkvT[0:W, cols] = (pr[0:W] + qb[:, 4:5]).astype(bf16)
        qkvT[W:2 * W, cols] = pr[W:2 * W].astype(bf16)
        qkvT[2 * W:3 * W, cols] = (pr[2 * W:] + qb[:, 5:6]).astype(bf16)
        return carry
    own[...] = T[pl.ds(hg * 2, 2)]
    lax.fori_loop(0, T.shape[0], blk, 0)
    keep = pltpu.make_async_copy(T, normed, ln)
    keep.start()
    ag_slot(7)
    keep.wait()
    def cot_copy(i):
        zt = 2 * c + i
        return zt, rcopy(cot.at[i], up.at[lax.rem(z, 2)], su.at[i], ru.at[lax.rem(z, 2)], dev(x, lax.div(z, 2), zt, y))
    def cot_start():
        for i in range(2):
            zt, cp = cot_copy(i)
            @pl.when(zt != z)
            def _():
                cp.start()
            @pl.when(zt == z)
            def _():
                pltpu.make_async_copy(cot.at[i], up.at[lax.rem(z, 2)], lu).start()
    def cot_wait():
        for j in range(2):
            @pl.when(2 * c + j != z)
            def _():
                rcopy(cot.at[0], up.at[j], su.at[0], ru.at[j], sib).wait_recv()
            @pl.when(2 * c + j == z)
            def _():
                pltpu.make_async_copy(cot.at[0], up.at[j], lu).wait()
            zt, cp = cot_copy(j)
            @pl.when(zt != z)
            def _():
                cp.wait_send()
    def attention(k_s, o_s):
        for h in range(heads):
            k_s[h] = qkvT[W + h * hd:W + (h + 1) * hd, :].T
        QB, KB = 2 * R, 512
        cs = LOG2E * hd ** -0.5
        nk = N // KB
        def group(k, carry):
            cc = jnp.where((k == 1) | (k == 2), 1 - c, c)
            yy = jnp.where(k < 2, 1 - y, y)
            g = cc * 2 + yy
            qcols = pl.ds(g * QB, QB)
            def head(h, carry):
                step = k * heads + h
                for i in range(16):
                    if 8 + i in PLAN or COT == 8 + i:
                        @pl.when(step == i)
                        def _():
                            ag_slot(8 + i)
                            if COT == 8 + i:
                                cot_start()
                qt = qkvT[pl.ds(h * hd, hd), qcols]
                def scores(i):
                    return dot_nn(k_s[h, i * KB:(i + 1) * KB, :], qt)
                m = None
                s = scores(0)
                for i in range(nk):
                    nxt = scores(i + 1) if i + 1 < nk else None
                    cm = jnp.max(s, axis=0, keepdims=True)
                    mn = cm if m is None else jnp.maximum(m, cm)
                    p = jnp.exp2(s * cs - mn * cs)
                    ps = jnp.sum(p, axis=0, keepdims=True)
                    vt = qkvT[pl.ds(2 * W + h * hd, hd), i * KB:(i + 1) * KB]
                    ov = dot_nn(vt, p.astype(bf16))
                    if m is None:
                        l, o = ps, ov
                    else:
                        a = jnp.exp2((m - mn) * cs)
                        l = l * a + ps
                        o = o * a + ov
                    m = mn
                    s = nxt
                o = o / l
                o_s[g, pl.ds(h * hd, hd), :] = o.astype(bf16)
                oT[pl.ds(h * hd, hd), qcols] = o
                lse[pl.ds(h, 1), qcols] = m * cs + jnp.log2(l)
                return carry
            lax.fori_loop(0, heads, head, 0)
            @pl.when(k < 3)
            def _():
                rcopy(o_s.at[g], bt.at[hg], so.at[k], ro.at[k], dev(x, cc, z, yy)).start()
            @pl.when(k == 3)
            def _():
                pltpu.make_async_copy(o_s.at[g], bt.at[hg], lo).start()
            return carry
        lax.fori_loop(0, 4, group, 0)
        for k, d in enumerate((yp, diag, sib)):
            rcopy(o_s.at[0], bt.at[hg], so.at[k], ro.at[k], d).wait()
        pltpu.make_async_copy(o_s.at[0], bt.at[hg], lo).wait()
    pl.run_scoped(attention, pltpu.VMEM((heads, N, hd), bf16), pltpu.VMEM((4, W, 2 * R), bf16))
    for i in range(2):
        zt, cp, loc = tcp[i]
        @pl.when(zt != z)
        def _():
            cp.wait_send()


    FF = fb1.shape[1]
    C = 2 * R

    def out_copy(bout, j):
        zt = 2 * c + j
        return zt, rcopy(bout.at[j], bo.at[lax.rem(z, 2)], sbo.at[j], qbo.at[lax.rem(z, 2)], dev(x, lax.div(z, 2), zt, y)), \
            pltpu.make_async_copy(bout.at[j], bo.at[lax.rem(z, 2)], lbo)
    def out_wait(bout):
        for i in range(2):
            zt, cp, lc = out_copy(bout, i)
            @pl.when(2 * c + i != z)
            def _():
                rcopy(bout.at[0], bo.at[i], sbo.at[0], qbo.at[i], sib).wait_recv()
            @pl.when(2 * c + i == z)
            def _():
                pltpu.make_async_copy(bout.at[0], bo.at[i], lbo).wait()
            @pl.when(zt != z)
            def _():
                cp.wait_send()

    def middle_part(Wo, mid_s, n2, n2T, oacc, dacc, f1b, f2b, p1, sb1, k1, p2, sb2, k2, sb3, bout, lw, l1, l2):
        ag_slot(24)
        ag_got(2, 0)
        ag_got(2, 1)
        cpw = pltpu.make_async_copy(gc, Wo, lw)
        cpw.start()
        bT = bt[...].reshape(4 * W, C).T
        cpw.wait()
        w_o = Wo[...].reshape(D, D)
        def norm(v):
            cen = v - jnp.mean(v, axis=-1, keepdims=True)
            return cen, lax.rsqrt(jnp.mean(cen * cen, axis=-1, keepdims=True) + EPS)
        for j in range(2):
            v = own[j].astype(f32) + vec[15:16, :] + dot_nn(bT[j * R:(j + 1) * R], w_o) + vec[6:7, :]
            mid_s[j] = v
            cen, r = norm(v)
            nb = (cen * r * vec[7:8, :] + vec[8:9, :]).astype(bf16)
            n2[j] = nb
            n2T[:, :, j * R:(j + 1) * R] = nb.T.reshape(4, D // 4, R)
        ag_slot(25)
        ag_got(0, 0)
        ag_got(0, 1)
        cot_wait()
        ag_got(1, 0)

        def order(s):
            zp = jnp.where(s < 4, lax.div(z, 2), 1 - lax.div(z, 2))
            xx = jnp.where(lax.rem(lax.div(s, 2), 2) == 0, 1 - x, x)
            cc = lax.rem(s, 2)
            return xx, cc, zp, (xx * 2 + cc) * 2 + zp
        def loads(s):
            xx, cc, zp, j = order(s)
            slot = lax.rem(s, 2)
            return (pltpu.make_async_copy(ga.at[:, :, :, :, :, pl.ds(pl.multiple_of(j * C, C), C)], f1b.at[slot], l1.at[slot]),
                    pltpu.make_async_copy(gb.at[xx, cc, pl.ds(zp * 2, 2)], f2b.at[slot], l2.at[slot]))
        for cp in loads(0):
            cp.start()
        oacc[...] = jnp.zeros_like(oacc)
        dacc[...] = jnp.zeros_like(dacc)
        def sends(s):
            slot = lax.rem(s, 2)
            return (rcopy(sb1.at[slot], r1.at[slot], sf1.at[s], rf1.at[s], sib), rcopy(sb2, r2, sf2.at[s], rf2.at[s], sib))
        def cols_of(s):
            return pl.ds(pl.multiple_of(order(s)[3] * C, C), C)
        def go1(s):
            slot = lax.rem(s, 2)
            out = []
            for q in range(2):
                cs_ = pl.ds(q * C, C)
                out.append(rcopy(k1.at[slot, :, 1 - y, :, cs_], h1.at[q, :, :, cols_of(s)], sh1.at[s, q], qh1.at[s, q], yp))
                out.append(pltpu.make_async_copy(k1.at[slot, :, y, :, cs_], a1.at[q, :, :, cols_of(s)], la1.at[s, q]))
            return out
        def go2(s):
            slot, zp = lax.rem(lax.div(s, 2), 2), order(s)[2]
            i = lax.div(s, 4)
            return (rcopy(k2.at[slot], h2.at[pl.ds(zp * 2, 2)], sh2.at[i], qh2.at[i], xp),
                    pltpu.make_async_copy(k2.at[slot], a2.at[pl.ds(zp * 2, 2)], la2.at[i]))
        def keeps(s):
            return lax.rem(s, 2) == c
        def away(s):
            return lax.rem(lax.div(s, 2), 2) == 0
        def finish(s):
            slot = lax.rem(s, 2)
            sends(s)[0].wait_recv()
            @pl.when(s >= 2)
            def _():
                for n, cp in enumerate(go1(s - 2)):
                    cp.wait() if n % 2 else cp.wait_send()
            k1[slot] = (p1[...].astype(f32) + r1[slot].astype(f32)).astype(bf16)
            for cp in go1(s):
                cp.start()
            @pl.when(keeps(s))
            def _():
                sends(s)[1].wait_recv()
                @pl.when(s >= 4)
                def _():
                    @pl.when(away(s))
                    def _():
                        go2(s - 4)[0].wait_send()
                    @pl.when(jnp.logical_not(away(s)))
                    def _():
                        go2(s - 4)[1].wait()
                k2[lax.rem(lax.div(s, 2), 2)] = (p2[...].astype(f32) + r2[...].astype(f32)).astype(bf16).reshape(k2.shape[1:])
                @pl.when(away(s))
                def _():
                    go2(s)[0].start()
                @pl.when(jnp.logical_not(away(s)))
                def _():
                    go2(s)[1].start()
        def chunk(s, carry):
            slot = lax.rem(s, 2)
            xx, cc, zp, j = order(s)
            for cp in loads(s):
                cp.wait()
            for i in range(8):
                if 26 + i in PLAN or i == 3:
                    @pl.when(s == i)
                    def _():
                        ag_slot(26 + i)
                        if i == 3:
                            ag_got(1, 1)
            @pl.when(s < 7)
            def _():
                for cp in loads(s + 1):
                    cp.start()
            f1c = f1b[slot].reshape(D, C)
            f2c = f2b[slot].reshape(C, D)
            u2 = up[...].reshape(C, D)
            h = dot_nn(n2[...].reshape(C, D), f1c) + fb1[2:3, pl.ds(pl.multiple_of(j * C, C), C)]
            da = dot_nt(u2, f2c)
            ph = 0.5 + 0.5 * lax.erf(h * 0.7071067811865476)
            act = (h * ph).astype(bf16)
            hgr = (da * (ph + h * (jnp.exp(-0.5 * h * h) * 0.3989422804014327))).astype(bf16)
            oacc[...] += dot_nn(act, f2c).reshape(2, R, D)
            sums[pl.ds(4 + lax.div(j, 2), 1), pl.ds(pl.multiple_of(lax.rem(j, 2) * C, C), C)] = jnp.sum(hgr.astype(f32), axis=0, keepdims=True)
            dacc[...] += dot_nt(hgr, f1c).reshape(2, R, D)
            @pl.when(s > 0)
            def _():
                finish(s - 1)
            @pl.when(s >= 2)
            def _():
                sends(s - 2)[0].wait_send()
            @pl.when((s >= 2) & jnp.logical_not(keeps(s)))
            def _():
                sends(s - 2)[1].wait_send()
            for q in range(2):
                sb1[slot, :, :, :, q * C:(q + 1) * C] = dot_nn(n2T[q * 2 + 1 - c], hgr).astype(bf16).reshape(4, 2, R // 8, C)
            sends(s)[0].start()
            g2 = dot_nn(act.T, u2).astype(bf16)
            @pl.when(keeps(s))
            def _():
                p2[...] = g2
            @pl.when(jnp.logical_not(keeps(s)))
            def _():
                sb2[...] = g2
                sends(s)[1].start()
            for q in range(2):
                p1[:, :, :, q * C:(q + 1) * C] = dot_nn(n2T[q * 2 + c], hgr).astype(bf16).reshape(4, 2, R // 8, C)
            return carry
        lax.fori_loop(0, 8, chunk, 0)
        for j in range(2):
            bout[j] = (mid_s[j] + oacc[j] + vec[9:10, :]).astype(bf16)
            zt, cp, lc = out_copy(bout, j)
            @pl.when(zt != z)
            def _():
                cp.start()
            @pl.when(zt == z)
            def _():
                lc.start()
        last = jnp.int32(7)
        finish(last)

        tot = [jnp.zeros((1, D), f32) for _ in range(4)]
        ags = []
        for j in range(2):
            v = mid_s[j]
            cen, r = norm(v)
            xh = cen * r
            u = dacc[j]
            e = u * vec[7:8, :]
            g = up[j].astype(f32) + r * (e - jnp.mean(e, axis=-1, keepdims=True) - xh * jnp.mean(e * xh, axis=-1, keepdims=True))
            mgrad[j] = g
            ag = g.astype(bf16)
            ags.append(ag)
            for n, val in enumerate((ag.astype(f32), u * xh, u, up[j].astype(f32))):
                tot[n] = tot[n] + jnp.sum(val, axis=0, keepdims=True)
        for n in range(4):
            sums[n:n + 1, :] = tot[n]
        ag = jnp.concatenate(ags, axis=0)
        for q in range(2):
            sb3[q] = dot_nn(bt[q * 2 + 1 - c], ag).astype(bf16)
            rcopy(sb3.at[q], r3.at[q], sf3.at[q], rf3.at[q], sib).start()
        for q in range(4):
            dob[q] = dot_nt(Wo[q // 2, q % 2].reshape(D // 4, D), ag).astype(bf16)
        for q in range(2):
            rcopy(sb3.at[q], r3.at[q], sf3.at[q], rf3.at[q], sib).wait()
            r3[q] = (r3[q].astype(f32) + dot_nn(bt[q * 2 + c], ag)).astype(bf16)
        cp3 = pltpu.make_async_copy(r3, a3, la3)
        cp3.start()
        for s in (6, 7):
            sends(s)[0].wait_send()
            @pl.when(c != s % 2)
            def _():
                sends(s)[1].wait_send()
            for n, cp in enumerate(go1(jnp.int32(s))):
                cp.wait() if n % 2 else cp.wait_send()
        for s in range(8):
            for cp in go1(jnp.int32(s))[::2]:
                cp.wait_recv()
        go2(4 + c)[0].wait_send()
        go2(6 + c)[1].wait()
        for i in range(2):
            go2(i * 4 + c)[0].wait_recv()
        cp3.wait()
        out_wait(bout)
        for p in range(3):
            ag_sent(p)

    SD = pltpu.SemaphoreType.DMA
    V = pltpu.VMEM
    blk1 = (4, 2, R // 8, 2 * C)
    pl.run_scoped(middle_part, V(gc.shape, bf16), V((2, R, D), f32), V((2, R, D), bf16), V((4, D // 4, C), bf16), V((2, R, D), f32),
                  V((2, R, D), f32), V((2,) + ga.shape[:5] + (C,), bf16), V((2, 2) + gb.shape[3:], bf16),
                  V(blk1, bf16), V((2,) + blk1, bf16), V((2,) + blk1, bf16), V((C, D), bf16), V((C, D), bf16), V((2, 2) + gb.shape[3:], bf16),
                  V((2, D // 4, D), bf16), V((2, R, D), bf16), SD, SD((2,)), SD((2,)))


def forward_kernel(tok, cot, wq, small, fa, fb, fc, heads, hd):
    n_it, R, D = tok.shape
    FF = fa.shape[1]
    W = heads * hd
    N = 8 * R
    C = 2 * R
    S = pltpu.SemaphoreType.DMA
    V = pltpu.VMEM
    vm = pl.BlockSpec(memory_space=pltpu.VMEM)
    hbm = pl.BlockSpec(memory_space=pl.ANY)
    sd = jax.ShapeDtypeStruct
    full = lambda a: sd((2, 2, 4, 2) + a.shape, bf16)
    return pl.pallas_call(
        functools.partial(fwd_kernel, hd, heads),
        in_specs=[hbm] * 7,
        out_specs=[hbm] + [vm] * 6 + [hbm] * 5 + [vm] * 2 + [hbm, vm] + [hbm] * 3,
        out_shape=[
            sd((8, R, D), bf16), sd((3 * W, N), bf16), sd((W, N), f32), sd((heads, N), f32), sd((2, R, D), bf16), sd((16, D), f32),
            sd((3 * W, D), bf16), sd((2, 4) + fa.shape, bf16), sd((2, 4) + fa.shape, bf16), sd((4, 2) + fb.shape, bf16),
            sd((4, 2) + fb.shape, bf16), sd((2, D // 4, D), bf16), sd((4, W, C), bf16),
            sd((2, R, D), f32), sd((2, R, D), bf16), sd((16, D), f32), full(fa), full(fb), full(fc),
        ],
        scratch_shapes=[
            V((8, R, D), bf16), V((8, 4, 32, 3 * W + 128), bf16), V((8, FF), f32), V((4, W, C), bf16), V((2, R, D), bf16),
            V((2, 4, 2, R // 8, 2 * C), bf16), V((C, D), bf16), V((2, D // 4, D), bf16),
            S((2,)), S((2,)), S, S((2,)), S((2,)), S((2,)), S((2,)), S((2,)), S((2,)),
            S((3, 4)), S((3, 4)), S((4,)), S((6,)), S((6,)), S((7,)), S((7,)), S((3,)), S((3,)), S, S,
            S((2,)), S((2,)), S, S((3,)), S((3,)), S((3, 6)), S((3, 6)), S((3, 7)), S((3, 7)), S((3, 7)), S((3, 7)), S((3, 7)), S((3, 7)),
            S((8,)), S((8,)), S((8,)), S((8,)), S((2,)), S((2,)), S((8, 2)), S((2,)), S,
            S((8, 2)), S((8, 2)), S((2,)), S((2,)), S((2,)), S((2,)), S,
        ],
        compiler_params=pltpu.CompilerParams(collective_id=0, has_side_effects=True, vmem_limit_bytes=60 << 20),
        name="forward",
    )(tok, cot, wq, small, fa, fb, fc)


def put_sum(dst, pieces):
    total = pieces[0].astype(f32)
    for p in pieces[1:]:
        total = total + p.astype(f32)
    dst[...] = total.astype(dst.dtype)


def tail_kernel(hd, heads, dob, qkvT, oT, lse, a1, h1, a2, h2, a3, normed, wT, own, rows, mgrad, sums0,
                o1, o2, o3, gq, home, sums,
                do_s, dq_s, k1, r11, r12, r13, k2, r21, r22, r23, k3, r31, r32, r33,
                nm, w_s, Gb, gx, gz, go, ds_s, dr_c, dy_s, dr_y, ig, hm, vs, vr,
                sd, rd, ld, s1, q1, s2, q2, s3, q3, lk, sg, qg, sgz, qgz, sga, qga, sdc, qdc, sdy, qdy, sh, qh, lh, sv, qv, ll, lnm):
    x, c, z, y = place()
    hg = c * 2 + y
    W = heads * hd
    N = qkvT.shape[1]
    zoff = [lax.rem(z + k, 4) for k in (1, 2, 3)]
    sib, yp, diag, xp = dev(x, 1 - c, z, y), dev(x, c, z, 1 - y), dev(x, 1 - c, z, 1 - y), dev(1 - x, c, z, y)
    zp = [dev(x, c, zz, y) for zz in zoff]
    greet(zp + [dev(x, 1 - c, zz, y) for zz in zoff] + [sib, yp, diag, xp])
    peers = ((sib, (1 - c) * 2 + y), (yp, c * 2 + 1 - y), (diag, (1 - c) * 2 + 1 - y))
    for k, (d, g) in enumerate(peers):
        rcopy(dob.at[g], do_s.at[hg], sd.at[k], rd.at[k], d).start()
    loc = pltpu.make_async_copy(dob.at[hg], do_s.at[hg], ld)
    loc.start()

    def part(ref, h, n):
        return ref if n is None else ref.at[..., pl.ds(h * n, n), :]
    n1, n2 = k1.shape[2] // 2, k2.shape[2] // 2

    class Piece:
        def __init__(self, i, h, n, a, first, k, r1, r2, r3, out, s, q, lsem, yfirst):
            self.h = None if first is None else part(first, h, n)
            self.a, self.k, self.r1, self.r2, self.r3, self.out = [part(v, h, n) for v in (a, k, r1, r2, r3, out)]
            self.s, self.q, self.lsem, self.yfirst, self.b = s, q, lsem, yfirst, h * 5
            self.i = i
        def copies(self):
            b, s, q = self.b, self.s, self.q
            if self.yfirst:
                second = rcopy(self.k.at[1 - x], self.r2, s.at[b + 1], q.at[b + 1], xp)
                mine = lambda zz: self.k.at[x, zz]
            else:
                second = rcopy(self.k.at[:, 1 - y], self.r2, s.at[b + 1], q.at[b + 1], yp)
                mine = lambda zz: self.k.at[zz, y]
            if self.h is None:
                first = rcopy(self.a.at[1 - x], self.r1, s.at[b], q.at[b], xp)
                kept = self.a.at[x]
            else:
                first = pltpu.make_async_copy(self.h, self.r1, s.at[b])
                kept = self.a
            zs = [rcopy(mine(zoff[j]), self.r3.at[j], s.at[b + 2 + j], q.at[b + 2 + j], zp[j]) for j in range(3)]
            return first, second, zs, pltpu.make_async_copy(kept, self.k, self.lsem.at[self.i]), mine
        def start(self):
            first, _, _, keep, _ = self.copies()
            keep.start()
            first.start()
        def second(self):
            first, second, _, keep, _ = self.copies()
            keep.wait()
            first.wait()
            n0, n1_ = self.k.shape[0], self.k.shape[1]
            def add(j, carry):
                p, q_ = lax.div(j, n1_), lax.rem(j, n1_)
                put_sum(self.k.at[p, q_], [self.k[p, q_], self.r1[p, q_]])
                return carry
            lax.fori_loop(0, n0 * n1_, add, 0)
            second.start()
        def third(self):
            _, second, zs, _, mine = self.copies()
            second.wait()
            def add(zz, carry):
                put_sum(mine(zz), [mine(zz)[...], self.r2[zz]])
                return carry
            lax.fori_loop(0, 4, add, 0)
            for cp in zs:
                cp.start()
        def finish(self):
            _, _, zs, _, mine = self.copies()
            for cp in zs:
                cp.wait()
            put_sum(self.out, [mine(z)[...]] + [self.r3[j] for j in range(3)])

    f1 = [Piece(h, h, n1, a1, h1, k1, r11, r12, r13, o1, s1, q1, lk, True) for h in range(2)]
    f2 = [Piece(2 + h, h, n2, a2, h2, k2, r21, r22, r23, o2, s2, q2, lk, False) for h in range(2)]
    f3 = Piece(4, 0, None, a3, None, k3, r31, r32, r33, o3, s3, q3, lk, False)
    for piece in (f2[0], f1[0], f2[1], f1[1], f3):
        piece.start()

    QB, KB = N // 4, 512
    cs = LOG2E * hd ** -0.5
    sc = hd ** -0.5
    nk = N // KB

    ld_n = pltpu.make_async_copy(normed, nm, lnm.at[0])
    ld_w = pltpu.make_async_copy(wT, w_s, lnm.at[1])
    ld_n.start()
    ld_w.start()

    def G_first(pr):
        rows_ = [dq_s[q * W + pr * 2 * hd:q * W + (pr + 1) * 2 * hd, :] for q in range(3)]
        g = dot_nn(jnp.concatenate(rows_, axis=0), nm[...].reshape(N, nm.shape[2])).astype(bf16).T
        Gb[pr] = g.reshape(Gb.shape[1:])
        G_x(pr).start()
    def G_x(pr):
        return rcopy(Gb.at[pr, 1 - x], gx.at[pr], sg.at[pr], qg.at[pr], xp)
    def G_z(pr):
        return [rcopy(Gb.at[pr, x, :, zoff[j]], gz.at[pr, j], sgz.at[pr, j], qgz.at[pr, j], zp[j]) for j in range(3)]
    def G_second(pr):
        G_x(pr).wait()
        def add(i, carry):
            cc, zz = lax.div(i, 4), lax.rem(i, 4)
            put_sum(Gb.at[pr, x, cc, zz], [Gb[pr, x, cc, zz], gx[pr, cc, zz]])
            return carry
        lax.fori_loop(0, 8, add, 0)
        for cp in G_z(pr):
            cp.start()
    def G_own(pr):
        cps = [rcopy(Gb.at[pr, x, cc, z, yy], go.at[pr, hg], sga.at[pr, k], qga.at[pr, k], d)
               for k, (d, cc, yy) in enumerate(((sib, 1 - c, y), (yp, c, 1 - y), (diag, 1 - c, 1 - y)))]
        return cps, pltpu.make_async_copy(Gb.at[pr, x, c, z, y], go.at[pr, hg], ll.at[pr])
    def G_third(pr):
        for cp in G_z(pr):
            cp.wait()
        def add(i, carry):
            cc, yy = lax.div(i, 2), lax.rem(i, 2)
            put_sum(Gb.at[pr, x, cc, z, yy], [Gb[pr, x, cc, z, yy]] + [gz[pr, k, cc, yy] for k in range(3)])
            return carry
        lax.fori_loop(0, 4, add, 0)
        cps, own_ = G_own(pr)
        for cp in cps:
            cp.start()
        own_.start()
    def G_done(pr):
        cps, own_ = G_own(pr)
        own_.wait()
        for cp in cps:
            cp.wait()
        D_ = gq.shape[1] // 3
        for g in range(4):
            for q in range(3):
                at = q * D_ + g * W + pr * 2 * hd
                gq[:, at:at + 2 * hd] = go[pr, g, :, q * 2 * hd:(q + 1) * 2 * hd].astype(f32)

    PLAN = {
        1: ((Piece.second, f1[1]),),
        2: ((Piece.second, f2[0]),),
        5: ((Piece.second, f2[1]), (Piece.third, f1[1]),),
        6: ((Piece.second, f1[0]),),
        7: ((Piece.third, f2[0]),),
        8: ((Piece.second, f3),),
        11: ((Piece.third, f2[1]), (Piece.third, f3),),
        13: ((G_second, 0),),
        15: ((Piece.third, f1[0]),),
        17: ((G_second, 1),),
        19: ((G_third, 0),),
        21: ((G_third, 1), (G_done, 0),),
        22: ((Piece.finish, f2[0]),),
        24: ((Piece.finish, f3), (G_done, 1),),
        25: ((Piece.finish, f1[0]), (Piece.finish, f1[1]), (Piece.finish, f2[1]),),
    }

    def slot(i):
        for f, a in PLAN.get(i, ()):
            f(a)

    def attention(k_s, v_s, dk_s, dv_s):
        loc.wait()
        def head(h, carry):
            hr = pl.ds(h * hd, hd)
            @pl.when(h == 2)
            def _():
                ld_n.wait()
                G_first(0)
            k_s[...] = qkvT[pl.ds(W + h * hd, hd), :].T
            v_s[...] = qkvT[pl.ds(2 * W + h * hd, hd), :].T
            dk_s[...] = jnp.zeros_like(dk_s)
            dv_s[...] = jnp.zeros_like(dv_s)
            def group(k, carry):
                step = h * 4 + k
                @pl.when((step > 0) & (step < 4))
                def _():
                    rcopy(dob.at[0], do_s.at[0], sd.at[k - 1], rd.at[k - 1], sib).wait()
                for i in range(16):
                    if i in PLAN:
                        @pl.when(step == i)
                        def _():
                            slot(i)
                cc = jnp.where((k == 1) | (k == 3), 1 - c, c)
                yy = jnp.where(k >= 2, 1 - y, y)
                g = cc * 2 + yy
                qcols = pl.ds(g * QB, QB)
                qt = qkvT[hr, qcols]
                dt = do_s[g, hr, :]
                delta = jnp.sum(dt.astype(f32) * oT[hr, qcols], axis=0, keepdims=True)
                ls = lse[pl.ds(h, 1), qcols]
                def first(i):
                    ks = slice(i * KB, (i + 1) * KB)
                    return dot_nn(k_s[ks, :], qt), dot_nn(v_s[ks, :], dt)
                dq = None
                cur = first(0)
                for i in range(nk):
                    nxt = first(i + 1) if i + 1 < nk else None
                    s, dp = cur
                    ks = slice(i * KB, (i + 1) * KB)
                    p = jnp.exp2(s * cs - ls)
                    ds = (p * (dp - delta)).astype(bf16)
                    prt = dot_nn(qkvT[pl.ds(W + h * hd, hd), ks], ds)
                    dq = prt if dq is None else dq + prt
                    dk_s[:, ks] += dot_nt(qt, ds)
                    dv_s[:, ks] += dot_nt(dt, p.astype(bf16))
                    cur = nxt
                dq_s[hr, qcols] = (dq * sc).astype(bf16)
                return carry
            lax.fori_loop(0, 4, group, 0)
            dq_s[pl.ds(W + h * hd, hd), :] = (dk_s[...] * sc).astype(bf16)
            dq_s[pl.ds(2 * W + h * hd, hd), :] = dv_s[...].astype(bf16)
            return carry
        lax.fori_loop(0, heads, head, 0)

    pl.run_scoped(attention, pltpu.VMEM((N, hd), bf16), pltpu.VMEM((N, hd), bf16),
                  pltpu.VMEM((hd, N), f32), pltpu.VMEM((hd, N), f32))

    def after(tok_s, mg_s, dn, lsem):
        R = tok_s.shape[1]
        B = R // 2
        loads = [pltpu.make_async_copy(a, b, lsem.at[i]) for i, (a, b) in enumerate(((own, tok_s), (mgrad, mg_s)))]
        for cp in loads:
            cp.start()
        ld_w.wait()
        def proj(g, b):
            return dot_nn(dq_s[:, pl.ds(pl.multiple_of(g * QB + b * B, B), B)].T, w_s[...])
        g_sy, g_s, g_oy = (1 - c) * 2 + 1 - y, (1 - c) * 2 + y, c * 2 + 1 - y
        def rows_of(b):
            return b // 2, pl.ds((b % 2) * B, B)
        def to_sib(a, b):
            j, rw = rows_of(b)
            return rcopy(ds_s.at[a, j, rw], dr_c.at[a, j, rw], sdc.at[a * 4 + b], qdc.at[a * 4 + b], sib)
        def to_y(b):
            j, rw = rows_of(b)
            return rcopy(dy_s.at[j, rw], dr_y.at[j, rw], sdy.at[b], qdy.at[b], yp)
        for b in range(4):
            j, rw = rows_of(b)
            ds_s[0, j, rw, :] = proj(g_sy, b).astype(bf16)
            to_sib(0, b).start()
        for b in range(4):
            j, rw = rows_of(b)
            mine = proj(g_oy, b)
            to_sib(0, b).wait()
            dy_s[j, rw, :] = (mine + dr_c[0, j, rw, :].astype(f32)).astype(bf16)
            to_y(b).start()
        slot(16)
        G_first(1)
        for b in range(4):
            j, rw = rows_of(b)
            ds_s[1, j, rw, :] = proj(g_s, b).astype(bf16)
            to_sib(1, b).start()
        for b in range(4):
            j, rw = rows_of(b)
            dn[j, rw, :] = proj(hg, b)
        ones = jnp.ones((8, N), bf16)
        vs[...] = sums0[...]
        for row, q in ((12, 0), (13, 2)):
            tot = dot_nt(ones, dq_s[q * W:(q + 1) * W, :])
            vs[row:row + 1, :] = jnp.zeros((1, vs.shape[1]), f32)
            vs[row:row + 1, pl.ds(pl.multiple_of(hg * W, W), W)] = tot[0:1]
        slot(17)
        gain = rows[2:3, :]
        shift = rows[15:16, :]
        acc = [jnp.zeros((1, dn.shape[2]), f32) for _ in range(3)]
        for cp in loads:
            cp.wait()
        def home_copy(b):
            j, rw = rows_of(b)
            i = lax.rem(z, 2)
            zt = 2 * c + j
            return zt, rcopy(ig.at[j, rw], hm.at[i, rw], sh.at[b], qh.at[i, b % 2], dev(x, lax.div(z, 2), zt, y)), \
                pltpu.make_async_copy(ig.at[j, rw], hm.at[i, rw], lh.at[b % 2])
        for b in range(4):
            j, rw = rows_of(b)
            to_sib(1, b).wait()
            to_y(b).wait()
            u = dn[j, rw, :] + dr_c[1, j, rw, :].astype(f32) + dr_y[j, rw, :].astype(f32)
            v = tok_s[j, rw, :].astype(f32) + shift
            cen = v - jnp.mean(v, axis=-1, keepdims=True)
            r = lax.rsqrt(jnp.mean(cen * cen, axis=-1, keepdims=True) + EPS)
            xh = cen * r
            e = u * gain
            res = mg_s[j, rw, :] + r * (e - jnp.mean(e, axis=-1, keepdims=True) - xh * jnp.mean(e * xh, axis=-1, keepdims=True))
            ig[j, rw, :] = res.astype(bf16)
            for n, val in enumerate((u * xh, u, res)):
                acc[n] = acc[n] + jnp.sum(val, axis=0, keepdims=True)
            zt, cp, lc = home_copy(b)
            @pl.when(zt != z)
            def _():
                cp.start()
            @pl.when(zt == z)
            def _():
                lc.start()
            slot(18 + b)
        vs[8:9, :] = acc[0]
        vs[9:10, :] = acc[1]
        vs[10:11, :] = acc[2] * rows[14:15, :]
        vs[11:12, :] = acc[2]
        for k, d in enumerate((sib, yp, xp)):
            cp = rcopy(vs, vr.at[k], sv.at[k], qv.at[k], d)
            cp.start()
            slot(22 + k)
            cp.wait()
            vs[...] = vs[...] + vr[k]
        zv = [rcopy(vs, vr.at[3 + k], sv.at[3 + k], qv.at[3 + k], zp[k]) for k in range(3)]
        for cp in zv:
            cp.start()
        slot(25)
        for i in range(2):
            src = 2 * c + i
            for hb in range(2):
                rw = pl.ds(hb * B, B)
                @pl.when(src != z)
                def _():
                    rcopy(ig.at[0, rw], hm.at[i, rw], sh.at[0], qh.at[i, hb], sib).wait_recv()
                @pl.when(src == z)
                def _():
                    pltpu.make_async_copy(ig.at[0, rw], hm.at[i, rw], lh.at[hb]).wait()
                home[i, rw, :] = hm[i, rw, :].astype(f32)
        for cp in zv:
            cp.wait()
        sums[...] = vs[...] + vr[3] + vr[4] + vr[5]
        slot(26)
        for b in range(4):
            zt, cp, lc = home_copy(b)
            @pl.when(zt != z)
            def _():
                cp.wait_send()

    R = own.shape[1]
    D = own.shape[2]
    pl.run_scoped(after, pltpu.VMEM((2, R, D), bf16), pltpu.VMEM((2, R, D), f32), pltpu.VMEM((2, R, D), f32), pltpu.SemaphoreType.DMA((2,)))


def backward_kernel(dob, qkvT, oT, lse, a1, h1, a2, h2, a3, normed, wT, own, rows, mgrad, sums0, heads, hd):
    W3, N = qkvT.shape
    W = heads * hd
    _, R, D = own.shape
    S = pltpu.SemaphoreType.DMA
    V = pltpu.VMEM
    vm = pl.BlockSpec(memory_space=pltpu.VMEM)
    hbm = pl.BlockSpec(memory_space=pl.ANY)
    b1, b2, b3 = a1.shape[2:], a2.shape[2:], a3.shape[3:]
    def bufs(b, yfirst):
        k = (2, 4) if yfirst else (4, 2)
        return [V(k + b, bf16), V(k + b, bf16), V((4,) + b, bf16), V((3,) + b, bf16)]
    rq = D // 32
    return pl.pallas_call(
        functools.partial(tail_kernel, hd, heads),
        in_specs=[hbm, vm, vm, vm, hbm, hbm, hbm, hbm, hbm, hbm, hbm, hbm, vm, hbm, vm],
        out_specs=[vm] * 6,
        out_shape=[
            jax.ShapeDtypeStruct(b1, f32), jax.ShapeDtypeStruct(b2, f32), jax.ShapeDtypeStruct(b3, f32),
            jax.ShapeDtypeStruct((rq, 3 * D), f32), jax.ShapeDtypeStruct((2, R, D), f32), jax.ShapeDtypeStruct((16, D), f32),
        ],
        scratch_shapes=[V((4, W, N // 4), bf16), V((W3, N), bf16)] + bufs(b1, True) + bufs(b2, False) + bufs(b3, False) + [
            V((8, R, D), bf16), V((W3, D), bf16),
            V((2, 2, 2, 4, 2, rq, W3 // 2), bf16), V((2, 2, 4, 2, rq, W3 // 2), bf16), V((2, 3, 2, 2, rq, W3 // 2), bf16), V((2, 4, rq, W3 // 2), bf16),
            V((2, 2, R, D), bf16), V((2, 2, R, D), bf16), V((2, R, D), bf16), V((2, R, D), bf16), V((2, R, D), bf16), V((2, R, D), bf16),
            V((16, D), f32), V((6, 16, D), f32),
            S((3,)), S((3,)), S, S((10,)), S((10,)), S((10,)), S((10,)), S((5,)), S((5,)), S((5,)),
            S((2,)), S((2,)), S((2, 3)), S((2, 3)), S((2, 3)), S((2, 3)), S((8,)), S((8,)), S((4,)), S((4,)),
            S((4,)), S((2, 2)), S((2,)), S((6,)), S((6,)), S((2,)), S((2,)),
        ],
        compiler_params=pltpu.CompilerParams(collective_id=1, has_side_effects=True, vmem_limit_bytes=60 << 20),
        name="backward",
    )(dob, qkvT, oT, lse, a1, h1, a2, h2, a3, normed, wT, own, rows, mgrad, sums0)


HEADS = 16


epsilon = EPS


def norm_rows_s(values, gain, shift):
    center = values - jnp.mean(values, axis=-1, keepdims=True)
    spread = jnp.mean(center * center, axis=-1, keepdims=True)
    return center * lax.rsqrt(spread + epsilon) * gain + shift


def gelu_exact_s(values):
    return jax.nn.gelu(values, approximate=False)


def product(left, right):
    return jnp.dot(left, right, preferred_element_type=jnp.float32)


def product_tleft(left, right):
    return lax.dot_general(
        left, right, (((0,), (0,)), ((), ())), preferred_element_type=jnp.float32
    )


def product_tright(left, right):
    return lax.dot_general(
        left, right, (((1,), (1,)), ((), ())), preferred_element_type=jnp.float32
    )


def split_heads(values):
    return values.reshape(values.shape[0], HEADS, values.shape[1] // HEADS)


def attend(operands):
    queries, keys_all, values_all = operands
    scale = (queries.shape[1] // HEADS) ** (-0.5)
    scores = (
        jnp.einsum(
            "qhd,khd->hqk",
            split_heads(queries),
            split_heads(keys_all),
            preferred_element_type=jnp.float32,
        )
        * scale
    )
    highest = jnp.max(scores, axis=-1, keepdims=True)
    exps = jnp.exp(scores - highest)
    totals = jnp.sum(exps, axis=-1, keepdims=True)
    probs_low = (exps / totals).astype(jnp.bfloat16)
    blended = jnp.einsum(
        "hqk,khd->qhd", probs_low, split_heads(values_all), preferred_element_type=jnp.float32
    ).reshape(queries.shape)
    return (blended, (highest + jnp.log(totals))[:, :, 0])


def recompute_probs(queries, keys_all, values_all, grads_in, log_totals):
    scale = (queries.shape[1] // HEADS) ** (-0.5)
    scores = (
        jnp.einsum(
            "qhd,khd->hqk",
            split_heads(queries),
            split_heads(keys_all),
            preferred_element_type=jnp.float32,
        )
        * scale
    )
    probs = jnp.exp(scores - log_totals[:, :, None])
    prob_grads = jnp.einsum(
        "qhd,khd->hqk",
        split_heads(grads_in),
        split_heads(values_all),
        preferred_element_type=jnp.float32,
    )
    return (probs, prob_grads, scale)


def key_side_grads(score_grads, probs, queries, grads_in, row_count):
    key_grads = jnp.einsum(
        "hqk,qhd->khd", score_grads, split_heads(queries), preferred_element_type=jnp.float32
    )
    value_grads = jnp.einsum(
        "hqk,qhd->khd",
        probs.astype(jnp.bfloat16),
        split_heads(grads_in),
        preferred_element_type=jnp.float32,
    )
    width = queries.shape[1]
    return (key_grads.reshape(row_count, width), value_grads.reshape(row_count, width))


def query_side(with_keys, operands):
    queries, keys_all, values_all, grads_in, log_totals = operands
    probs, prob_grads, scale = recompute_probs(queries, keys_all, values_all, grads_in, log_totals)
    row_delta = jnp.sum(probs * prob_grads, axis=-1)
    score_grads = (probs * (prob_grads - row_delta[:, :, None]) * scale).astype(jnp.bfloat16)
    query_grads = jnp.einsum(
        "hqk,khd->qhd", score_grads, split_heads(keys_all), preferred_element_type=jnp.float32
    ).reshape(queries.shape)
    key_grads, value_grads = key_side_grads(
        score_grads, probs, queries, grads_in, keys_all.shape[0]
    )
    return (query_grads, row_delta, key_grads, value_grads)


def spread_on_device(
    tokens_in,
    lead_hours,
    cotangent,
    w_qkv,
    w_out,
    w_fc1,
    w_fc2,
    ln1_gain,
    ln1_bias,
    q_bias,
    v_bias,
    out_bias,
    ln2_gain,
    ln2_bias,
    fc1_bias,
    fc2_bias,
    lead_weight,
    lead_bias,
):
    gathered = (
        lax.all_gather(w_qkv, ("dp", "seq"), axis=0, tiled=True),
        lax.all_gather(w_out, ("dp", "seq"), axis=0, tiled=True),
        lax.all_gather(w_fc1, ("dp", "seq"), axis=0, tiled=True),
        lax.all_gather(w_fc2, ("dp", "seq"), axis=0, tiled=True),
        lax.all_gather(ln1_gain, ("dp", "seq"), axis=0, tiled=True),
        lax.all_gather(ln1_bias, ("dp", "seq"), axis=0, tiled=True),
        lax.all_gather(q_bias, ("dp", "seq"), axis=0, tiled=True),
        lax.all_gather(v_bias, ("dp", "seq"), axis=0, tiled=True),
        lax.all_gather(out_bias, ("dp", "seq"), axis=0, tiled=True),
        lax.all_gather(ln2_gain, ("dp", "seq"), axis=0, tiled=True),
        lax.all_gather(ln2_bias, ("dp", "seq"), axis=0, tiled=True),
        lax.all_gather(fc1_bias, ("dp", "seq"), axis=0, tiled=True),
        lax.all_gather(fc2_bias, ("dp", "seq"), axis=0, tiled=True),
        lax.all_gather(lead_weight, ("dp", "seq"), axis=0, tiled=True),
        lax.all_gather(lead_bias, ("dp", "seq"), axis=0, tiled=True),
    )
    (
        full_qkv,
        full_out,
        full_fc1,
        full_fc2,
        gain_one,
        shift_one,
        bias_query,
        bias_value,
        bias_out,
        gain_two,
        shift_two,
        bias_fc1,
        bias_fc2,
        lead_scale,
        lead_shift,
    ) = gathered
    items, rows, width = tokens_in.shape
    count = items * rows
    lead_times = lead_hours.astype(jnp.float32) / 100.0
    leading = (
        tokens_in.astype(jnp.float32)
        + lead_times[:, None, None] * lead_scale.astype(jnp.float32)
        + lead_shift.astype(jnp.float32)
    ).reshape(count, width)
    normed, norm_one_back = jax.vjp(
        norm_rows_s, leading, gain_one.astype(jnp.float32), shift_one.astype(jnp.float32)
    )
    normed_low = normed.astype(jnp.bfloat16)
    projected = product(normed_low, full_qkv)
    queries = (projected[:, :width] + bias_query.astype(jnp.float32)).astype(jnp.bfloat16)
    keys_own = projected[:, width : 2 * width].astype(jnp.bfloat16)
    values_own = (projected[:, 2 * width :] + bias_value.astype(jnp.float32)).astype(jnp.bfloat16)
    queries3 = queries.reshape(items, rows, width)
    keys_all, values_all = (
        lax.all_gather(keys_own.reshape(items, rows, width), "seq", axis=1, tiled=True),
        lax.all_gather(values_own.reshape(items, rows, width), "seq", axis=1, tiled=True),
    )
    blended, log_totals = lax.map(attend, (queries3, keys_all, values_all))
    blended_low = blended.reshape(count, width).astype(jnp.bfloat16)
    middle = leading + product(blended_low, full_out) + bias_out.astype(jnp.float32)
    normed_two, norm_two_back = jax.vjp(
        norm_rows_s, middle, gain_two.astype(jnp.float32), shift_two.astype(jnp.float32)
    )
    normed_two_low = normed_two.astype(jnp.bfloat16)
    hidden = product(normed_two_low, full_fc1) + bias_fc1.astype(jnp.float32)
    activated, gelu_back = jax.vjp(gelu_exact_s, hidden)
    activated_low = activated.astype(jnp.bfloat16)
    output = middle + product(activated_low, full_fc2) + bias_fc2.astype(jnp.float32)
    block_output = output.reshape(items, rows, width).astype(jnp.bfloat16)
    back_qkv, back_out, back_fc1, back_fc2 = (
        lax.all_gather(w_qkv, ("dp", "seq"), axis=0, tiled=True),
        lax.all_gather(w_out, ("dp", "seq"), axis=0, tiled=True),
        lax.all_gather(w_fc1, ("dp", "seq"), axis=0, tiled=True),
        lax.all_gather(w_fc2, ("dp", "seq"), axis=0, tiled=True),
    )
    out_grad = cotangent.reshape(count, width)
    upstream = out_grad.astype(jnp.float32)
    grad_fc2 = product_tleft(activated_low, out_grad)
    grad_fc2_bias = jnp.sum(upstream, axis=0)
    hidden_grad = gelu_back(product_tright(out_grad, back_fc2))[0].astype(jnp.bfloat16)
    grad_fc1 = product_tleft(normed_two_low, hidden_grad)
    grad_fc1_bias = jnp.sum(hidden_grad.astype(jnp.float32), axis=0)
    middle_part, grad_ln2_gain, grad_ln2_bias = norm_two_back(product_tright(hidden_grad, back_fc1))
    middle_grad = upstream + middle_part
    attn_grad = middle_grad.astype(jnp.bfloat16)
    grad_out = product_tleft(blended_low, attn_grad)
    grad_out_bias = jnp.sum(attn_grad.astype(jnp.float32), axis=0)
    blended_grad = (
        product_tright(attn_grad, back_out).astype(jnp.bfloat16).reshape(items, rows, width)
    )
    query_grads, row_delta, key_parts, value_parts = lax.map(
        partial(query_side, True), (queries3, keys_all, values_all, blended_grad, log_totals)
    )
    key_grads, value_grads = (
        lax.psum_scatter(
            key_parts.astype(jnp.bfloat16), "seq", scatter_dimension=1, tiled=True
        ).astype(jnp.float32),
        lax.psum_scatter(
            value_parts.astype(jnp.bfloat16), "seq", scatter_dimension=1, tiled=True
        ).astype(jnp.float32),
    )
    query_low = query_grads.reshape(count, width).astype(jnp.bfloat16)
    key_low = key_grads.reshape(count, width).astype(jnp.bfloat16)
    value_low = value_grads.reshape(count, width).astype(jnp.bfloat16)
    qkv_grad = jnp.concatenate([query_low, key_low, value_low], axis=1)
    grad_qkv = product_tleft(normed_low, qkv_grad)
    grad_q_bias = jnp.sum(query_low.astype(jnp.float32), axis=0)
    grad_v_bias = jnp.sum(value_low.astype(jnp.float32), axis=0)
    leading_part, grad_ln1_gain, grad_ln1_bias = norm_one_back(product_tright(qkv_grad, back_qkv))
    input_grad = (middle_grad + leading_part).reshape(items, rows, width)
    grad_lead_weight = jnp.sum(jnp.sum(input_grad, axis=1) * lead_times[:, None], axis=0)
    grad_lead_bias = jnp.sum(input_grad, axis=(0, 1))
    summed = (
        lax.psum_scatter(grad_qkv, ("dp", "seq"), scatter_dimension=0, tiled=True),
        lax.psum_scatter(grad_out, ("dp", "seq"), scatter_dimension=0, tiled=True),
        lax.psum_scatter(grad_fc1, ("dp", "seq"), scatter_dimension=0, tiled=True),
        lax.psum_scatter(grad_fc2, ("dp", "seq"), scatter_dimension=0, tiled=True),
        lax.psum_scatter(grad_ln1_gain, ("dp", "seq"), scatter_dimension=0, tiled=True),
        lax.psum_scatter(grad_ln1_bias, ("dp", "seq"), scatter_dimension=0, tiled=True),
        lax.psum_scatter(grad_q_bias, ("dp", "seq"), scatter_dimension=0, tiled=True),
        lax.psum_scatter(grad_v_bias, ("dp", "seq"), scatter_dimension=0, tiled=True),
        lax.psum_scatter(grad_out_bias, ("dp", "seq"), scatter_dimension=0, tiled=True),
        lax.psum_scatter(grad_ln2_gain, ("dp", "seq"), scatter_dimension=0, tiled=True),
        lax.psum_scatter(grad_ln2_bias, ("dp", "seq"), scatter_dimension=0, tiled=True),
        lax.psum_scatter(grad_fc1_bias, ("dp", "seq"), scatter_dimension=0, tiled=True),
        lax.psum_scatter(grad_fc2_bias, ("dp", "seq"), scatter_dimension=0, tiled=True),
        lax.psum_scatter(grad_lead_weight, ("dp", "seq"), scatter_dimension=0, tiled=True),
        lax.psum_scatter(grad_lead_bias, ("dp", "seq"), scatter_dimension=0, tiled=True),
    )
    return (block_output, input_grad) + tuple(summed)


def on_device(mesh_shape, tokens_in, lead_hours, cotangent, w_qkv, w_out, w_fc1, w_fc2, ln1_gain, ln1_bias, q_bias, v_bias,
              out_bias, ln2_gain, ln2_bias, fc1_bias, fc2_bias, lead_weight, lead_bias):
    x, c, z, y = place()
    _, R, D = tokens_in.shape
    FF = w_fc1.shape[1]
    hd = D // HEADS
    heads = HEADS // 4
    W = heads * hd
    rows = w_qkv.shape[0]
    vectors = (lead_weight, lead_bias, ln1_gain, ln1_bias, q_bias, v_bias, out_bias, ln2_gain, ln2_bias, fc2_bias, fc1_bias,
               lead_hours.astype(bf16))
    small = sum(lax.pad(v[None].astype(f32), f32(0), ((k, 31 - k, 0), (0, 128 - v.shape[0], 0))) for k, v in enumerate(vectors)).astype(bf16)
    normed, qkvT, oT, lse, own, vec, wT, a1, h1, a2, h2, a3, dob, mgrad, block_output, sums0 = forward_kernel(
        tokens_in, cotangent, w_qkv, small, w_fc1, w_fc2, w_out, heads, hd)[:16]
    grad_fc1, grad_fc2, grad_out, grad_qkv, home, sums = backward_kernel(
        dob, qkvT, oT, lse, a1, h1, a2, h2, a3.reshape(2, 4, 2, rows, D), normed, wT,
        own, vec, mgrad, sums0, heads, hd)
    index = (x * 2 + c) * 8 + z * 2 + y
    mine = lax.dynamic_slice(sums, (0, index * rows), (16, rows))
    g_fc1_bias = lax.dynamic_slice(sums[4:4 + FF // D].reshape(FF), (index * fc1_bias.shape[0],), (fc1_bias.shape[0],))
    return (block_output, home, grad_qkv, grad_out, grad_fc1, grad_fc2, mine[8], mine[9], mine[12], mine[13], mine[0],
            mine[1], mine[2], g_fc1_bias, mine[3], mine[10], mine[11])


def choose(mesh_shape, *args):
    items, rows = args[0].shape[0], args[3].shape[0]
    planes = mesh_shape["seq"] // 2
    if items == 2 and planes == 2 * items and mesh_shape["dp"] == 4 and rows % 16 == 0 and 4 * args[0].shape[1] == args[0].shape[2]:
        return on_device(mesh_shape, *args)
    return spread_on_device(*args)


def solution(mesh):
    big, rows, vec = P("dp", "seq", None), P(("dp", "seq"), None), P(("dp", "seq"))
    in_specs = (big, P("dp"), big) + (rows,) * 4 + (vec,) * 11
    out_specs = (big, big) + (rows,) * 4 + (vec,) * 11
    body = functools.partial(choose, dict(mesh.shape))
    return jax.shard_map(body, mesh=mesh, in_specs=in_specs, out_specs=out_specs, check_vma=False)
```

```python
import functools
from functools import partial
import jax, jax.numpy as jnp
from jax import lax
from jax.experimental import pallas as pl
from jax.experimental.pallas import tpu as pltpu
from jax.sharding import PartitionSpec as P

MESH = pl.DeviceIdType.MESH
f32, bf16 = jnp.float32, jnp.bfloat16
LOG2E = 1.4426950408889634
EPS = 1e-06


def dot_nn(a, b):
    return lax.dot_general(a, b, (((1,), (0,)), ((), ())), preferred_element_type=f32)


def dot_nt(a, b):
    return lax.dot_general(a, b, (((1,), (1,)), ((), ())), preferred_element_type=f32)


def rcopy(src, dst, ssem, rsem, dev):
    return pltpu.make_async_remote_copy(src_ref=src, dst_ref=dst, send_sem=ssem, recv_sem=rsem, device_id=dev, device_id_type=MESH)


def place():
    dp, seq = lax.axis_index("dp"), lax.axis_index("seq")
    return lax.div(dp, 2), lax.rem(dp, 2), lax.div(seq, 2), lax.rem(seq, 2)


def dev(x, c, z, y):
    return (x * 2 + c, z * 2 + y)


def greet(partners):
    bar = pltpu.get_barrier_semaphore()
    for p in partners:
        pl.semaphore_signal(bar, inc=1, device_id=p, device_id_type=MESH)
    pl.semaphore_wait(bar, len(partners))


def fwd_kernel(hd, heads, tok, cot, wq, small, fa, fb, fc, normed, qkv_out, o_out, lse, own, vec, w_out_, a1, h1, a2, h2, a3, dob, mgrad, bo, sums,
               ga, gb, gc, qkvT, oT, wT, T, Ws, fb1, bt, up, r1, r2, r3, st, rt, lt, sy, ry, sc, rc, scy, rcy, sa, ra, la, sz, rz, sx, rx, so, ro, lo,
               ln, su, ru, lu, gss, grs, gsz, grz, gs1, gr1, gs2, gr2, gsc, grc, sf1, rf1, sf2, rf2, sf3, rf3, la1, la2, la3,
               sh1, qh1, sh2, qh2, sbo, qbo, lbo, lq):
    x, c, z, y = place()
    hg = c * 2 + y
    W = heads * hd
    D = T.shape[2]
    R = T.shape[1]
    N = qkvT.shape[1]
    zoff = [lax.rem(z + k, 4) for k in (1, 2, 3)]
    sums[...] = jnp.zeros_like(sums)
    greet([dev(x, c, zz, y) for zz in zoff] + [dev(x, 1 - c, zz, y) for zz in zoff]
          + [dev(x, 1 - c, z, y), dev(x, c, z, 1 - y), dev(x, 1 - c, z, 1 - y), dev(1 - x, c, z, y)])
    sib, yp, diag, xp = dev(x, 1 - c, z, y), dev(x, c, z, 1 - y), dev(x, 1 - c, z, 1 - y), dev(1 - x, c, z, y)
    pos = (lax.div(z, 2) * 2 + y) * 2 + lax.rem(z, 2)
    tcp = []
    for i in range(2):
        zt = 2 * c + i
        cp = rcopy(tok.at[i], T.at[pos], st.at[i], rt.at[lax.rem(z, 2)], dev(x, lax.div(z, 2), zt, y))
        loc = pltpu.make_async_copy(tok.at[i], T.at[pos], lt)
        @pl.when(zt != z)
        def _():
            cp.start()
        @pl.when(zt == z)
        def _():
            loc.start()
        tcp.append((zt, cp, loc))
    xz = x * 4 + z
    def slices(g):
        dst = Ws.at[xz, hg]
        out = [(wq.at[:, pl.ds(pl.multiple_of(q * D + g * W, W), W)], dst.at[:, q * W:(q + 1) * W]) for q in range(3)]
        return out + [(small, dst.at[:, 3 * W:3 * W + 128])]
    wa = [pltpu.make_async_copy(a, b, la.at[n]) for n, (a, b) in enumerate(slices(hg))]
    for k, (d, g) in enumerate(((yp, c * 2 + 1 - y), (sib, (1 - c) * 2 + y), (diag, (1 - c) * 2 + 1 - y))):
        wa += [rcopy(a, b, sa.at[k, n], ra.at[k, n], d) for n, (a, b) in enumerate(slices(g))]
    for cp in wa:
        cp.start()
    for cp in wa:
        cp.wait()
    def zz_of(u):
        return z if u == 0 else (z - u if u <= 3 else z + (u - 3))

    def ok(u):
        return True if u == 0 else (z >= u if u <= 3 else z + (u - 3) <= 3)

    def guard(cond, f):
        if cond is True:
            f()
        else:
            pl.when(cond)(f)

    def w_z(u, down):
        v = Ws.at[x * 4 + zz_of(u)]
        k = (u if u <= 3 else u - 3) + (3 if down else 0)
        return rcopy(v, v, sz.at[k], rz.at[k], dev(x, c, z - 1 if down else z + 1, y))

    def w_arr(u):
        v = Ws.at[x * 4 + zz_of(u)]
        return rcopy(v, v, sz.at[u - 1], rz.at[u - 1], sib)

    def w_x(u):
        v = Ws.at[x * 4 + zz_of(u)]
        return rcopy(v, v, sx.at[u], rx.at[u], xp)

    def w_recv(d):
        for u in (d, d + 3):
            def go(u=u):
                w_arr(u).wait_recv()
                if d < 3:
                    guard((z > 0) if u > 3 else (z < 3), lambda: w_z(u, u > 3).start())
                w_x(u).start()
            guard(ok(u), go)

    guard(z < 3, lambda: w_z(0, False).start())
    guard(z > 0, lambda: w_z(0, True).start())
    w_x(0).start()
    ca = 1 - c
    gat = ((fa, ga, False), (fb, gb, True), (fc, gc, False))
    before_z = (False, True, True)
    known = set()

    def g_start(p):
        f, g, _ = gat[p]
        return rcopy(f, g.at[x, c, z, y], gss.at[p], grs.at[p], sib)

    def z_block(p, u):
        g, xfirst = gat[p][1:]
        if not before_z[p]:
            return g.at[x, ca, zz_of(u), y]
        return g.at[:, ca, zz_of(u), y] if xfirst else g.at[x, ca, zz_of(u)]

    def g_z(p, u, down):
        v = z_block(p, u)
        d = u if u <= 3 else u - 3
        k = d + (3 if down else 0)
        return rcopy(v, v, gsz.at[p, k], grz.at[p, k], dev(x, c, z - 1 if down else z + 1, y))

    def g_zarr(p, u):
        v = z_block(p, u)
        return rcopy(v, v, gsz.at[p, u - 1], grz.at[p, u - 1], sib)

    def g_one(p, u):
        g, xfirst = gat[p][1:]
        v = g.at[x, ca, zz_of(u), y]
        return rcopy(v, v, gs1.at[p, u], gr1.at[p, u], xp if xfirst else yp)

    def g_two(p, u):
        g, xfirst = gat[p][1:]
        v = g.at[:, ca, zz_of(u), y] if xfirst else g.at[x, ca, zz_of(u)]
        return rcopy(v, v, gs2.at[p, u], gr2.at[p, u], yp if xfirst else xp)

    def g_core(p, u):
        v = gat[p][1].at[:, ca, zz_of(u)]
        return rcopy(v, v, gsc.at[p, u], grc.at[p, u], sib)

    def ag_own(p):
        g_start(p).wait()
        g_one(p, 0).start()

    def one_own(p):
        if p not in known:
            known.add(p)
            g_one(p, 0).wait()

    def ag_z0(p, d):
        if before_z[p]:
            one_own(p)
        guard(z < 3, lambda: g_z(p, 0, False).start())
        guard(z > 0, lambda: g_z(p, 0, True).start())

    def ag_recv(p, d):
        for u in (d, d + 3):
            def go(u=u):
                g_zarr(p, u).wait_recv()
                if d < 3:
                    guard((z > 0) if u > 3 else (z < 3), lambda: g_z(p, u, u > 3).start())
                (g_two if before_z[p] else g_one)(p, u).start()
            guard(ok(u), go)

    def units(d):
        return (0,) if d == 0 else (d, d + 3)

    def ag_two(p, d):
        if before_z[p] and d > 0:
            return
        for u in units(d):
            def go(u=u):
                if u == 0:
                    one_own(p)
                else:
                    g_one(p, u).wait()
                g_two(p, u).start()
            guard(ok(u), go)

    def ag_core(p, d):
        for u in units(d):
            def go(u=u):
                g_two(p, u).wait()
                g_core(p, u).start()
            guard(ok(u), go)

    def ag_got(p, half):
        own_half = ((0, True), (1, lax.rem(z, 2) == 1), (4, lax.rem(z, 2) == 0))
        rest = ((1, z == 2), (2, z >= 2), (3, z == 3), (4, z == 1), (5, z <= 1), (6, z == 0))
        for u, cond in (own_half if half == 0 else rest):
            guard(cond, lambda: g_core(p, u).wait())

    def ag_sent(p):
        for u in (0, 1, 2):
            guard((z >= u) & (z < 3), lambda: g_z(p, u, False).wait_send())
            guard((z + u <= 3) & (z > 0), lambda: g_z(p, u + 3 if u else 0, True).wait_send())

    PLAN = {
        0: ((ag_two, 1, 0),),
        2: ((ag_z0, 1, 0), (ag_two, 0, 0),),
        3: ((ag_z0, 0, 0),),
        5: ((ag_recv, 0, 1),),
        6: ((ag_two, 2, 0),),
        7: ((ag_recv, 1, 1),),
        9: ((ag_recv, 2, 1),),
        10: ((ag_two, 1, 1),),
        11: ((ag_recv, 2, 2), (ag_recv, 0, 3),),
        12: ((ag_two, 2, 1),),
        13: ((ag_two, 0, 2),),
        14: ((ag_two, 2, 2),),
        15: ((ag_core, 0, 0),),
        17: ((ag_core, 2, 0),),
        19: ((ag_two, 0, 3),),
        20: ((ag_recv, 1, 2),),
        22: ((ag_core, 0, 1), (ag_core, 0, 2), (ag_recv, 2, 3),),
        23: ((ag_core, 2, 2), (ag_core, 1, 1),),
        24: ((ag_two, 2, 3), (ag_two, 1, 2), (ag_core, 2, 1), (ag_core, 2, 3),),
        25: ((ag_two, 1, 3), (ag_core, 0, 3), (ag_recv, 1, 3),),
        26: ((ag_core, 1, 2),),
        28: ((ag_core, 1, 3),),
        34: ((ag_recv, 0, 2),),
        35: ((ag_z0, 2, 0),),
        36: ((ag_core, 1, 0),),
        38: ((ag_two, 0, 1),),
    }

    COT = 14

    def ag_slot(i):
        for f, p, d in PLAN.get(i, ()):
            f(p, d)

    for p in (2, 0, 1):
        g_start(p).start()
    for p in (2, 0, 1):
        ag_own(p)
    ag_slot(0)
    w_recv(1)
    ag_slot(1)
    ycp, ccp, cycp = [], [], []
    j0 = jnp.where(lax.div(z, 2) == c, lax.rem(z, 2), 0)
    for j in (j0, 1 - j0):
        src_z = 2 * c + j
        p = hg * 2 + j
        @pl.when(src_z != z)
        def _():
            rcopy(tok.at[0], T.at[p], st.at[0], rt.at[j], sib).wait_recv()
        @pl.when(src_z == z)
        def _():
            pltpu.make_async_copy(tok.at[0], T.at[p], lt).wait()
        a = rcopy(T.at[p], T.at[p], sy.at[j], ry.at[j], yp)
        b = rcopy(T.at[p], T.at[p], sc.at[j], rc.at[j], sib)
        a.start()
        b.start()
        ycp.append(a)
        ccp.append(b)
    ag_slot(2)
    w_recv(2)
    ag_slot(3)
    w_recv(3)
    ag_slot(4)
    for n, j in enumerate((j0, 1 - j0)):
        ycp[n].wait()
        p = (c * 2 + 1 - y) * 2 + j
        cp = rcopy(T.at[p], T.at[p], scy.at[j], rcy.at[j], sib)
        cp.start()
        cycp.append(cp)
    ag_slot(5)
    for u in range(7):
        guard(ok(u), lambda: w_x(u).wait())
    for u in (0, 1, 2):
        guard((z >= u) & (z < 3), lambda: w_z(u, False).wait_send())
        guard((z + u <= 3) & (z > 0), lambda: w_z(u + 3 if u else 0, True).wait_send())
    for xx in range(2):
        for zz in range(4):
            for cc in range(2):
                for yy in range(2):
                    r = (xx * 2 + cc) * 8 + zz * 2 + yy
                    blk = Ws[xx * 4 + zz, cc * 2 + yy, 0:16, 3 * W:3 * W + 128].astype(f32)
                    vec[:, r * 32:(r + 1) * 32] = blk[:, 0:32]
                    fb1[:, r * 128:(r + 1) * 128] = blk[8:16, :]
                c0 = (xx * 2 + cc) * 256 + zz * 64
                wT[:, c0:c0 + 64] = Ws[xx * 4 + zz, cc * 2:cc * 2 + 2, :, 0:3 * W].reshape(64, 3 * W).T
    hours = jnp.zeros((1, 1), f32)
    for zz in range(4):
        hz = Ws[x * 4, (zz // 2) * 2, 0:16, 3 * W:3 * W + 128].astype(f32)[11:12, zz % 2:zz % 2 + 1]
        hours = jnp.where(z == zz, hz, hours)
    t = hours / 100.0
    for j in range(2):
        ccp[j].wait()
        cycp[j].wait()
    ag_slot(6)
    shift = t * vec[0:1, :] + vec[1:2, :]
    vec[14:15, :] = jnp.broadcast_to(t, (1, D))
    vec[15:16, :] = shift
    gain, bias = vec[2:3, :], vec[3:4, :]
    qb = vec[:, pl.ds(hg * W, W)].T
    def blk(p, carry):
        for i in range(8):
            if 34 + i in PLAN:
                @pl.when(p == i)
                def _():
                    ag_slot(34 + i)
        v = T[p].astype(f32) + shift
        cen = v - jnp.mean(v, axis=-1, keepdims=True)
        r = lax.rsqrt(jnp.mean(cen * cen, axis=-1, keepdims=True) + EPS)
        nb = (cen * r * gain + bias).astype(bf16)
        T[p] = nb
        pr = dot_nt(wT[...], nb)
        cols = pl.ds(p * R, R)
        qkvT[0:W, cols] = (pr[0:W] + qb[:, 4:5]).astype(bf16)
        qkvT[W:2 * W, cols] = pr[W:2 * W].astype(bf16)
        qkvT[2 * W:3 * W, cols] = (pr[2 * W:] + qb[:, 5:6]).astype(bf16)
        return carry
    own[...] = T[pl.ds(hg * 2, 2)]
    lax.fori_loop(0, T.shape[0], blk, 0)
    keep = pltpu.make_async_copy(T, normed, ln)
    keep.start()
    early = [pltpu.make_async_copy(a, b, lq.at[i]) for i, (a, b) in enumerate(((qkvT, qkv_out), (wT, w_out_), (oT, o_out)))]
    early[0].start()
    early[1].start()
    ag_slot(7)
    keep.wait()
    def cot_copy(i):
        zt = 2 * c + i
        return zt, rcopy(cot.at[i], up.at[lax.rem(z, 2)], su.at[i], ru.at[lax.rem(z, 2)], dev(x, lax.div(z, 2), zt, y))
    def cot_start():
        for i in range(2):
            zt, cp = cot_copy(i)
            @pl.when(zt != z)
            def _():
                cp.start()
            @pl.when(zt == z)
            def _():
                pltpu.make_async_copy(cot.at[i], up.at[lax.rem(z, 2)], lu).start()
    def cot_wait():
        for j in range(2):
            @pl.when(2 * c + j != z)
            def _():
                rcopy(cot.at[0], up.at[j], su.at[0], ru.at[j], sib).wait_recv()
            @pl.when(2 * c + j == z)
            def _():
                pltpu.make_async_copy(cot.at[0], up.at[j], lu).wait()
            zt, cp = cot_copy(j)
            @pl.when(zt != z)
            def _():
                cp.wait_send()
    def attention(k_s, o_s):
        for h in range(heads):
            k_s[h] = qkvT[W + h * hd:W + (h + 1) * hd, :].T
        QB, KB = 2 * R, 512
        cs = LOG2E * hd ** -0.5
        nk = N // KB
        def group(k, carry):
            cc = jnp.where((k == 1) | (k == 2), 1 - c, c)
            yy = jnp.where(k < 2, 1 - y, y)
            g = cc * 2 + yy
            qcols = pl.ds(g * QB, QB)
            def head(h, carry):
                step = k * heads + h
                for i in range(16):
                    if 8 + i in PLAN or COT == 8 + i:
                        @pl.when(step == i)
                        def _():
                            ag_slot(8 + i)
                            if COT == 8 + i:
                                cot_start()
                qt = qkvT[pl.ds(h * hd, hd), qcols]
                def scores(i):
                    return dot_nn(k_s[h, i * KB:(i + 1) * KB, :], qt)
                m = None
                s = scores(0)
                for i in range(nk):
                    nxt = scores(i + 1) if i + 1 < nk else None
                    cm = jnp.max(s, axis=0, keepdims=True)
                    mn = cm if m is None else jnp.maximum(m, cm)
                    p = jnp.exp2(s * cs - mn * cs)
                    ps = jnp.sum(p, axis=0, keepdims=True)
                    vt = qkvT[pl.ds(2 * W + h * hd, hd), i * KB:(i + 1) * KB]
                    ov = dot_nn(vt, p.astype(bf16))
                    if m is None:
                        l, o = ps, ov
                    else:
                        a = jnp.exp2((m - mn) * cs)
                        l = l * a + ps
                        o = o * a + ov
                    m = mn
                    s = nxt
                o = o / l
                o_s[g, pl.ds(h * hd, hd), :] = o.astype(bf16)
                oT[pl.ds(h * hd, hd), qcols] = o
                lse[pl.ds(h, 1), qcols] = m * cs + jnp.log2(l)
                return carry
            lax.fori_loop(0, heads, head, 0)
            @pl.when(k < 3)
            def _():
                rcopy(o_s.at[g], bt.at[hg], so.at[k], ro.at[k], dev(x, cc, z, yy)).start()
            @pl.when(k == 3)
            def _():
                pltpu.make_async_copy(o_s.at[g], bt.at[hg], lo).start()
            return carry
        lax.fori_loop(0, 4, group, 0)
        for k, d in enumerate((yp, diag, sib)):
            rcopy(o_s.at[0], bt.at[hg], so.at[k], ro.at[k], d).wait()
        pltpu.make_async_copy(o_s.at[0], bt.at[hg], lo).wait()
    pl.run_scoped(attention, pltpu.VMEM((heads, N, hd), bf16), pltpu.VMEM((4, W, 2 * R), bf16))
    for i in range(2):
        zt, cp, loc = tcp[i]
        @pl.when(zt != z)
        def _():
            cp.wait_send()


    early[2].start()
    FF = fb1.shape[1]
    C = 2 * R

    def out_copy(bout, j):
        zt = 2 * c + j
        return zt, rcopy(bout.at[j], bo.at[lax.rem(z, 2)], sbo.at[j], qbo.at[lax.rem(z, 2)], dev(x, lax.div(z, 2), zt, y)), \
            pltpu.make_async_copy(bout.at[j], bo.at[lax.rem(z, 2)], lbo)
    def out_wait(bout):
        for i in range(2):
            zt, cp, lc = out_copy(bout, i)
            @pl.when(2 * c + i != z)
            def _():
                rcopy(bout.at[0], bo.at[i], sbo.at[0], qbo.at[i], sib).wait_recv()
            @pl.when(2 * c + i == z)
            def _():
                pltpu.make_async_copy(bout.at[0], bo.at[i], lbo).wait()
            @pl.when(zt != z)
            def _():
                cp.wait_send()

    def middle_part(Wo, mid_s, n2, n2T, oacc, dacc, f1b, f2b, p1, sb1, k1, p2, sb2, k2, sb3, bout, lw, l1, l2):
        ag_slot(24)
        ag_got(2, 0)
        ag_got(2, 1)
        cpw = pltpu.make_async_copy(gc, Wo, lw)
        cpw.start()
        bT = bt[...].reshape(4 * W, C).T
        cpw.wait()
        w_o = Wo[...].reshape(D, D)
        def norm(v):
            cen = v - jnp.mean(v, axis=-1, keepdims=True)
            return cen, lax.rsqrt(jnp.mean(cen * cen, axis=-1, keepdims=True) + EPS)
        for j in range(2):
            v = own[j].astype(f32) + vec[15:16, :] + dot_nn(bT[j * R:(j + 1) * R], w_o) + vec[6:7, :]
            mid_s[j] = v
            cen, r = norm(v)
            nb = (cen * r * vec[7:8, :] + vec[8:9, :]).astype(bf16)
            n2[j] = nb
            n2T[:, :, j * R:(j + 1) * R] = nb.T.reshape(4, D // 4, R)
        ag_slot(25)
        ag_got(0, 0)
        ag_got(0, 1)
        cot_wait()
        ag_got(1, 0)

        def order(s):
            zp = jnp.where(s < 4, lax.div(z, 2), 1 - lax.div(z, 2))
            xx = jnp.where(lax.rem(lax.div(s, 2), 2) == 0, 1 - x, x)
            cc = lax.rem(s, 2)
            return xx, cc, zp, (xx * 2 + cc) * 2 + zp
        def loads(s):
            xx, cc, zp, j = order(s)
            slot = lax.rem(s, 2)
            return (pltpu.make_async_copy(ga.at[:, :, :, :, :, pl.ds(pl.multiple_of(j * C, C), C)], f1b.at[slot], l1.at[slot]),
                    pltpu.make_async_copy(gb.at[xx, cc, pl.ds(zp * 2, 2)], f2b.at[slot], l2.at[slot]))
        for cp in loads(0):
            cp.start()
        oacc[...] = jnp.zeros_like(oacc)
        dacc[...] = jnp.zeros_like(dacc)
        def sends(s):
            slot = lax.rem(s, 2)
            return (rcopy(sb1.at[slot], r1.at[slot], sf1.at[s], rf1.at[s], sib), rcopy(sb2, r2, sf2.at[s], rf2.at[s], sib))
        def cols_of(s):
            return pl.ds(pl.multiple_of(order(s)[3] * C, C), C)
        def go1(s):
            slot = lax.rem(s, 2)
            out = []
            for q in range(2):
                cs_ = pl.ds(q * C, C)
                out.append(rcopy(k1.at[slot, :, 1 - y, :, cs_], h1.at[q, :, :, cols_of(s)], sh1.at[s, q], qh1.at[s, q], yp))
                out.append(pltpu.make_async_copy(k1.at[slot, :, y, :, cs_], a1.at[q, :, :, cols_of(s)], la1.at[s, q]))
            return out
        def go2(s):
            slot, zp = lax.rem(lax.div(s, 2), 2), order(s)[2]
            i = lax.div(s, 4)
            return (rcopy(k2.at[slot], h2.at[pl.ds(zp * 2, 2)], sh2.at[i], qh2.at[i], xp),
                    pltpu.make_async_copy(k2.at[slot], a2.at[pl.ds(zp * 2, 2)], la2.at[i]))
        def keeps(s):
            return lax.rem(s, 2) == c
        def away(s):
            return lax.rem(lax.div(s, 2), 2) == 0
        def finish(s):
            slot = lax.rem(s, 2)
            sends(s)[0].wait_recv()
            @pl.when(s >= 2)
            def _():
                for n, cp in enumerate(go1(s - 2)):
                    cp.wait() if n % 2 else cp.wait_send()
            k1[slot] = (p1[...].astype(f32) + r1[slot].astype(f32)).astype(bf16)
            for cp in go1(s):
                cp.start()
            @pl.when(keeps(s))
            def _():
                sends(s)[1].wait_recv()
                @pl.when(s >= 4)
                def _():
                    @pl.when(away(s))
                    def _():
                        go2(s - 4)[0].wait_send()
                    @pl.when(jnp.logical_not(away(s)))
                    def _():
                        go2(s - 4)[1].wait()
                k2[lax.rem(lax.div(s, 2), 2)] = (p2[...].astype(f32) + r2[...].astype(f32)).astype(bf16).reshape(k2.shape[1:])
                @pl.when(away(s))
                def _():
                    go2(s)[0].start()
                @pl.when(jnp.logical_not(away(s)))
                def _():
                    go2(s)[1].start()
        def chunk(s, carry):
            slot = lax.rem(s, 2)
            xx, cc, zp, j = order(s)
            for cp in loads(s):
                cp.wait()
            for i in range(8):
                if 26 + i in PLAN or i == 3:
                    @pl.when(s == i)
                    def _():
                        ag_slot(26 + i)
                        if i == 3:
                            ag_got(1, 1)
            @pl.when(s < 7)
            def _():
                for cp in loads(s + 1):
                    cp.start()
            f1c = f1b[slot].reshape(D, C)
            f2c = f2b[slot].reshape(C, D)
            u2 = up[...].reshape(C, D)
            h = dot_nn(n2[...].reshape(C, D), f1c) + fb1[2:3, pl.ds(pl.multiple_of(j * C, C), C)]
            da = dot_nt(u2, f2c)
            ph = 0.5 + 0.5 * lax.erf(h * 0.7071067811865476)
            act = (h * ph).astype(bf16)
            hgr = (da * (ph + h * (jnp.exp(-0.5 * h * h) * 0.3989422804014327))).astype(bf16)
            oacc[...] += dot_nn(act, f2c).reshape(2, R, D)
            sums[pl.ds(4 + lax.div(j, 2), 1), pl.ds(pl.multiple_of(lax.rem(j, 2) * C, C), C)] = jnp.sum(hgr.astype(f32), axis=0, keepdims=True)
            dacc[...] += dot_nt(hgr, f1c).reshape(2, R, D)
            @pl.when(s > 0)
            def _():
                finish(s - 1)
            @pl.when(s >= 2)
            def _():
                sends(s - 2)[0].wait_send()
            @pl.when((s >= 2) & jnp.logical_not(keeps(s)))
            def _():
                sends(s - 2)[1].wait_send()
            for q in range(2):
                sb1[slot, :, :, :, q * C:(q + 1) * C] = dot_nn(n2T[q * 2 + 1 - c], hgr).astype(bf16).reshape(4, 2, R // 8, C)
            sends(s)[0].start()
            g2 = dot_nn(act.T, u2).astype(bf16)
            @pl.when(keeps(s))
            def _():
                p2[...] = g2
            @pl.when(jnp.logical_not(keeps(s)))
            def _():
                sb2[...] = g2
                sends(s)[1].start()
            for q in range(2):
                p1[:, :, :, q * C:(q + 1) * C] = dot_nn(n2T[q * 2 + c], hgr).astype(bf16).reshape(4, 2, R // 8, C)
            return carry
        lax.fori_loop(0, 8, chunk, 0)
        for j in range(2):
            bout[j] = (mid_s[j] + oacc[j] + vec[9:10, :]).astype(bf16)
            zt, cp, lc = out_copy(bout, j)
            @pl.when(zt != z)
            def _():
                cp.start()
            @pl.when(zt == z)
            def _():
                lc.start()
        last = jnp.int32(7)
        finish(last)

        tot = [jnp.zeros((1, D), f32) for _ in range(4)]
        ags = []
        for j in range(2):
            v = mid_s[j]
            cen, r = norm(v)
            xh = cen * r
            u = dacc[j]
            e = u * vec[7:8, :]
            g = up[j].astype(f32) + r * (e - jnp.mean(e, axis=-1, keepdims=True) - xh * jnp.mean(e * xh, axis=-1, keepdims=True))
            mgrad[j] = g
            ag = g.astype(bf16)
            ags.append(ag)
            for n, val in enumerate((ag.astype(f32), u * xh, u, up[j].astype(f32))):
                tot[n] = tot[n] + jnp.sum(val, axis=0, keepdims=True)
        for n in range(4):
            sums[n:n + 1, :] = tot[n]
        ag = jnp.concatenate(ags, axis=0)
        for q in range(2):
            sb3[q] = dot_nn(bt[q * 2 + 1 - c], ag).astype(bf16)
            rcopy(sb3.at[q], r3.at[q], sf3.at[q], rf3.at[q], sib).start()
        for q in range(4):
            dob[q] = dot_nt(Wo[q // 2, q % 2].reshape(D // 4, D), ag).astype(bf16)
        for q in range(2):
            rcopy(sb3.at[q], r3.at[q], sf3.at[q], rf3.at[q], sib).wait()
            r3[q] = (r3[q].astype(f32) + dot_nn(bt[q * 2 + c], ag)).astype(bf16)
        cp3 = pltpu.make_async_copy(r3, a3, la3)
        cp3.start()
        for s in (6, 7):
            sends(s)[0].wait_send()
            @pl.when(c != s % 2)
            def _():
                sends(s)[1].wait_send()
            for n, cp in enumerate(go1(jnp.int32(s))):
                cp.wait() if n % 2 else cp.wait_send()
        for s in range(8):
            for cp in go1(jnp.int32(s))[::2]:
                cp.wait_recv()
        go2(4 + c)[0].wait_send()
        go2(6 + c)[1].wait()
        for i in range(2):
            go2(i * 4 + c)[0].wait_recv()
        cp3.wait()
        for cp in early:
            cp.wait()
        out_wait(bout)
        for p in range(3):
            ag_sent(p)

    SD = pltpu.SemaphoreType.DMA
    V = pltpu.VMEM
    blk1 = (4, 2, R // 8, 2 * C)
    pl.run_scoped(middle_part, V(gc.shape, bf16), V((2, R, D), f32), V((2, R, D), bf16), V((4, D // 4, C), bf16), V((2, R, D), f32),
                  V((2, R, D), f32), V((2,) + ga.shape[:5] + (C,), bf16), V((2, 2) + gb.shape[3:], bf16),
                  V(blk1, bf16), V((2,) + blk1, bf16), V((2,) + blk1, bf16), V((C, D), bf16), V((C, D), bf16), V((2, 2) + gb.shape[3:], bf16),
                  V((2, D // 4, D), bf16), V((2, R, D), bf16), SD, SD((2,)), SD((2,)))


def forward_kernel(tok, cot, wq, small, fa, fb, fc, heads, hd):
    n_it, R, D = tok.shape
    FF = fa.shape[1]
    W = heads * hd
    N = 8 * R
    C = 2 * R
    S = pltpu.SemaphoreType.DMA
    V = pltpu.VMEM
    vm = pl.BlockSpec(memory_space=pltpu.VMEM)
    hbm = pl.BlockSpec(memory_space=pl.ANY)
    sd = jax.ShapeDtypeStruct
    full = lambda a: sd((2, 2, 4, 2) + a.shape, bf16)
    return pl.pallas_call(
        functools.partial(fwd_kernel, hd, heads),
        in_specs=[hbm] * 7,
        out_specs=[hbm] * 3 + [vm] * 3 + [hbm] * 6 + [vm] * 2 + [hbm, vm] + [hbm] * 3,
        out_shape=[
            sd((8, R, D), bf16), sd((3 * W, N), bf16), sd((W, N), f32), sd((heads, N), f32), sd((2, R, D), bf16), sd((16, D), f32),
            sd((3 * W, D), bf16), sd((2, 4) + fa.shape, bf16), sd((2, 4) + fa.shape, bf16), sd((4, 2) + fb.shape, bf16),
            sd((4, 2) + fb.shape, bf16), sd((2, D // 4, D), bf16), sd((4, W, C), bf16),
            sd((2, R, D), f32), sd((2, R, D), bf16), sd((16, D), f32), full(fa), full(fb), full(fc),
        ],
        scratch_shapes=[
            V((3 * W, N), bf16), V((W, N), f32), V((3 * W, D), bf16),
            V((8, R, D), bf16), V((8, 4, 32, 3 * W + 128), bf16), V((8, FF), f32), V((4, W, C), bf16), V((2, R, D), bf16),
            V((2, 4, 2, R // 8, 2 * C), bf16), V((C, D), bf16), V((2, D // 4, D), bf16),
            S((2,)), S((2,)), S, S((2,)), S((2,)), S((2,)), S((2,)), S((2,)), S((2,)),
            S((3, 4)), S((3, 4)), S((4,)), S((6,)), S((6,)), S((7,)), S((7,)), S((3,)), S((3,)), S, S,
            S((2,)), S((2,)), S, S((3,)), S((3,)), S((3, 6)), S((3, 6)), S((3, 7)), S((3, 7)), S((3, 7)), S((3, 7)), S((3, 7)), S((3, 7)),
            S((8,)), S((8,)), S((8,)), S((8,)), S((2,)), S((2,)), S((8, 2)), S((2,)), S,
            S((8, 2)), S((8, 2)), S((2,)), S((2,)), S((2,)), S((2,)), S, S((3,)),
        ],
        compiler_params=pltpu.CompilerParams(collective_id=0, has_side_effects=True, vmem_limit_bytes=60 << 20),
        name="forward",
    )(tok, cot, wq, small, fa, fb, fc)


def put_sum(dst, pieces):
    total = pieces[0].astype(f32)
    for p in pieces[1:]:
        total = total + p.astype(f32)
    dst[...] = total.astype(dst.dtype)


def tail_kernel(hd, heads, dob, qkvT, oT, lse, a1, h1, a2, h2, a3, normed, wT, own, rows, mgrad, sums0,
                o1, o2, o3, gq, hm, sums,
                do_s, dq_s, k1, r11, r12, r13, k2, r21, r22, r23, k3, r31, r32, r33,
                nm, w_s, Gb, gx, gz, go, ds_s, dr_c, dy_s, dr_y, ig, vs, vr,
                sd, rd, ld, s1, q1, s2, q2, s3, q3, lk, sg, qg, sgz, qgz, sga, qga, sdc, qdc, sdy, qdy, sh, qh, lh, sv, qv, ll, lnm):
    x, c, z, y = place()
    hg = c * 2 + y
    W = heads * hd
    N = qkvT.shape[1]
    zoff = [lax.rem(z + k, 4) for k in (1, 2, 3)]
    sib, yp, diag, xp = dev(x, 1 - c, z, y), dev(x, c, z, 1 - y), dev(x, 1 - c, z, 1 - y), dev(1 - x, c, z, y)
    zp = [dev(x, c, zz, y) for zz in zoff]
    greet(zp + [dev(x, 1 - c, zz, y) for zz in zoff] + [sib, yp, diag, xp])
    peers = ((sib, (1 - c) * 2 + y), (yp, c * 2 + 1 - y), (diag, (1 - c) * 2 + 1 - y))
    for k, (d, g) in enumerate(peers):
        rcopy(dob.at[g], do_s.at[hg], sd.at[k], rd.at[k], d).start()
    loc = pltpu.make_async_copy(dob.at[hg], do_s.at[hg], ld)
    loc.start()

    def part(ref, h, n):
        return ref if n is None else ref.at[..., pl.ds(h * n, n), :]
    n1, n2 = k1.shape[2] // 2, k2.shape[2] // 2

    class Piece:
        def __init__(self, i, h, n, a, first, k, r1, r2, r3, out, s, q, lsem, yfirst):
            self.h = None if first is None else part(first, h, n)
            self.a, self.k, self.r1, self.r2, self.r3, self.out = [part(v, h, n) for v in (a, k, r1, r2, r3, out)]
            self.s, self.q, self.lsem, self.yfirst, self.b = s, q, lsem, yfirst, h * 5
            self.i = i
        def copies(self):
            b, s, q = self.b, self.s, self.q
            if self.yfirst:
                second = rcopy(self.k.at[1 - x], self.r2, s.at[b + 1], q.at[b + 1], xp)
                mine = lambda zz: self.k.at[x, zz]
            else:
                second = rcopy(self.k.at[:, 1 - y], self.r2, s.at[b + 1], q.at[b + 1], yp)
                mine = lambda zz: self.k.at[zz, y]
            if self.h is None:
                first = rcopy(self.a.at[1 - x], self.r1, s.at[b], q.at[b], xp)
                kept = self.a.at[x]
            else:
                first = pltpu.make_async_copy(self.h, self.r1, s.at[b])
                kept = self.a
            zs = [rcopy(mine(zoff[j]), self.r3.at[j], s.at[b + 2 + j], q.at[b + 2 + j], zp[j]) for j in range(3)]
            return first, second, zs, pltpu.make_async_copy(kept, self.k, self.lsem.at[self.i]), mine
        def start(self):
            first, _, _, keep, _ = self.copies()
            keep.start()
            first.start()
        def second(self):
            first, second, _, keep, _ = self.copies()
            keep.wait()
            first.wait()
            n0, n1_ = self.k.shape[0], self.k.shape[1]
            def add(j, carry):
                p, q_ = lax.div(j, n1_), lax.rem(j, n1_)
                self.k[p, q_] = self.k[p, q_] + self.r1[p, q_]
                return carry
            lax.fori_loop(0, n0 * n1_, add, 0)
            second.start()
        def third(self):
            _, second, zs, _, mine = self.copies()
            second.wait()
            def add(zz, carry):
                mine(zz)[...] = mine(zz)[...] + self.r2[zz]
                return carry
            lax.fori_loop(0, 4, add, 0)
            for cp in zs:
                cp.start()
        def finish(self):
            _, _, zs, _, mine = self.copies()
            for cp in zs:
                cp.wait()
            put_sum(self.out, [mine(z)[...]] + [self.r3[j] for j in range(3)])

    f1 = [Piece(h, h, n1, a1, h1, k1, r11, r12, r13, o1, s1, q1, lk, True) for h in range(2)]
    f2 = [Piece(2 + h, h, n2, a2, h2, k2, r21, r22, r23, o2, s2, q2, lk, False) for h in range(2)]
    f3 = Piece(4, 0, None, a3, None, k3, r31, r32, r33, o3, s3, q3, lk, False)
    for piece in (f2[0], f1[0], f2[1], f1[1], f3):
        piece.start()

    QB, KB = N // 4, 512
    cs = LOG2E * hd ** -0.5
    sc = hd ** -0.5
    nk = N // KB

    ld_n = pltpu.make_async_copy(normed, nm, lnm.at[0])
    ld_w = pltpu.make_async_copy(wT, w_s, lnm.at[1])
    ld_n.start()
    ld_w.start()

    def G_first(pr):
        rows_ = [dq_s[q * W + pr * 2 * hd:q * W + (pr + 1) * 2 * hd, :] for q in range(3)]
        g = dot_nn(jnp.concatenate(rows_, axis=0), nm[...].reshape(N, nm.shape[2])).astype(bf16).T
        Gb[pr] = g.reshape(Gb.shape[1:])
        G_x(pr).start()
    def G_x(pr):
        return rcopy(Gb.at[pr, 1 - x], gx.at[pr], sg.at[pr], qg.at[pr], xp)
    def G_z(pr):
        return [rcopy(Gb.at[pr, x, :, zoff[j]], gz.at[pr, j], sgz.at[pr, j], qgz.at[pr, j], zp[j]) for j in range(3)]
    def G_second(pr):
        G_x(pr).wait()
        def add(i, carry):
            cc, zz = lax.div(i, 4), lax.rem(i, 4)
            Gb[pr, x, cc, zz] = Gb[pr, x, cc, zz] + gx[pr, cc, zz]
            return carry
        lax.fori_loop(0, 8, add, 0)
        for cp in G_z(pr):
            cp.start()
    def G_own(pr):
        cps = [rcopy(Gb.at[pr, x, cc, z, yy], go.at[pr, hg], sga.at[pr, k], qga.at[pr, k], d)
               for k, (d, cc, yy) in enumerate(((sib, 1 - c, y), (yp, c, 1 - y), (diag, 1 - c, 1 - y)))]
        return cps, pltpu.make_async_copy(Gb.at[pr, x, c, z, y], go.at[pr, hg], ll.at[pr])
    def G_third(pr):
        for cp in G_z(pr):
            cp.wait()
        def add(i, carry):
            cc, yy = lax.div(i, 2), lax.rem(i, 2)
            put_sum(Gb.at[pr, x, cc, z, yy], [Gb[pr, x, cc, z, yy]] + [gz[pr, k, cc, yy] for k in range(3)])
            return carry
        lax.fori_loop(0, 4, add, 0)
        cps, own_ = G_own(pr)
        for cp in cps:
            cp.start()
        own_.start()
    def G_done(pr):
        cps, own_ = G_own(pr)
        own_.wait()
        for cp in cps:
            cp.wait()
        D_ = gq.shape[1] // 3
        for g in range(4):
            for q in range(3):
                at = q * D_ + g * W + pr * 2 * hd
                gq[:, at:at + 2 * hd] = go[pr, g, :, q * 2 * hd:(q + 1) * 2 * hd].astype(f32)

    PLAN = {
        1: ((Piece.second, f1[1]),),
        2: ((Piece.second, f2[0]),),
        5: ((Piece.second, f2[1]), (Piece.third, f1[1]),),
        6: ((Piece.second, f1[0]),),
        7: ((Piece.third, f2[0]),),
        8: ((Piece.second, f3),),
        11: ((Piece.third, f2[1]), (Piece.third, f3),),
        13: ((G_second, 0),),
        15: ((Piece.third, f1[0]),),
        17: ((G_second, 1),),
        19: ((G_third, 0),),
        21: ((G_third, 1), (G_done, 0),),
        22: ((Piece.finish, f2[0]),),
        24: ((Piece.finish, f3), (G_done, 1),),
        25: ((Piece.finish, f1[0]), (Piece.finish, f1[1]), (Piece.finish, f2[1]),),
    }

    def slot(i):
        for f, a in PLAN.get(i, ()):
            f(a)

    def attention(k_s, v_s, dk_s, dv_s):
        loc.wait()
        def head(h, carry):
            hr = pl.ds(h * hd, hd)
            @pl.when(h == 2)
            def _():
                ld_n.wait()
                G_first(0)
            k_s[...] = qkvT[pl.ds(W + h * hd, hd), :].T
            v_s[...] = qkvT[pl.ds(2 * W + h * hd, hd), :].T
            dk_s[...] = jnp.zeros_like(dk_s)
            dv_s[...] = jnp.zeros_like(dv_s)
            def group(k, carry):
                step = h * 4 + k
                @pl.when((step > 0) & (step < 4))
                def _():
                    rcopy(dob.at[0], do_s.at[0], sd.at[k - 1], rd.at[k - 1], sib).wait()
                for i in range(16):
                    if i in PLAN:
                        @pl.when(step == i)
                        def _():
                            slot(i)
                cc = jnp.where((k == 1) | (k == 3), 1 - c, c)
                yy = jnp.where(k >= 2, 1 - y, y)
                g = cc * 2 + yy
                qcols = pl.ds(g * QB, QB)
                qt = qkvT[hr, qcols]
                dt = do_s[g, hr, :]
                delta = jnp.sum(dt.astype(f32) * oT[hr, qcols], axis=0, keepdims=True)
                ls = lse[pl.ds(h, 1), qcols]
                def first(i):
                    ks = slice(i * KB, (i + 1) * KB)
                    return dot_nn(k_s[ks, :], qt), dot_nn(v_s[ks, :], dt)
                dq = None
                cur = first(0)
                for i in range(nk):
                    nxt = first(i + 1) if i + 1 < nk else None
                    s, dp = cur
                    ks = slice(i * KB, (i + 1) * KB)
                    p = jnp.exp2(s * cs - ls)
                    ds = (p * (dp - delta)).astype(bf16)
                    prt = dot_nn(qkvT[pl.ds(W + h * hd, hd), ks], ds)
                    dq = prt if dq is None else dq + prt
                    dk_s[:, ks] += dot_nt(qt, ds)
                    dv_s[:, ks] += dot_nt(dt, p.astype(bf16))
                    cur = nxt
                dq_s[hr, qcols] = (dq * sc).astype(bf16)
                return carry
            lax.fori_loop(0, 4, group, 0)
            dq_s[pl.ds(W + h * hd, hd), :] = (dk_s[...] * sc).astype(bf16)
            dq_s[pl.ds(2 * W + h * hd, hd), :] = dv_s[...].astype(bf16)
            return carry
        lax.fori_loop(0, heads, head, 0)

    pl.run_scoped(attention, pltpu.VMEM((N, hd), bf16), pltpu.VMEM((N, hd), bf16),
                  pltpu.VMEM((hd, N), f32), pltpu.VMEM((hd, N), f32))

    def after(tok_s, mg_s, dn, lsem):
        R = tok_s.shape[1]
        B = R // 2
        loads = [pltpu.make_async_copy(a, b, lsem.at[i]) for i, (a, b) in enumerate(((own, tok_s), (mgrad, mg_s)))]
        for cp in loads:
            cp.start()
        ld_w.wait()
        def proj(g, b):
            return dot_nn(dq_s[:, pl.ds(pl.multiple_of(g * QB + b * B, B), B)].T, w_s[...])
        g_sy, g_s, g_oy = (1 - c) * 2 + 1 - y, (1 - c) * 2 + y, c * 2 + 1 - y
        def rows_of(b):
            return b // 2, pl.ds((b % 2) * B, B)
        def to_sib(a, b):
            j, rw = rows_of(b)
            return rcopy(ds_s.at[a, j, rw], dr_c.at[a, j, rw], sdc.at[a * 4 + b], qdc.at[a * 4 + b], sib)
        def to_y(b):
            j, rw = rows_of(b)
            return rcopy(dy_s.at[j, rw], dr_y.at[j, rw], sdy.at[b], qdy.at[b], yp)
        for b in range(4):
            j, rw = rows_of(b)
            ds_s[0, j, rw, :] = proj(g_sy, b).astype(bf16)
            to_sib(0, b).start()
        for b in range(4):
            j, rw = rows_of(b)
            mine = proj(g_oy, b)
            to_sib(0, b).wait()
            dy_s[j, rw, :] = (mine + dr_c[0, j, rw, :].astype(f32)).astype(bf16)
            to_y(b).start()
        slot(16)
        G_first(1)
        for b in range(4):
            j, rw = rows_of(b)
            ds_s[1, j, rw, :] = proj(g_s, b).astype(bf16)
            to_sib(1, b).start()
        for b in range(4):
            j, rw = rows_of(b)
            dn[j, rw, :] = proj(hg, b)
        ones = jnp.ones((8, N), bf16)
        vs[...] = sums0[...]
        for row, q in ((12, 0), (13, 2)):
            tot = dot_nt(ones, dq_s[q * W:(q + 1) * W, :])
            vs[row:row + 1, :] = jnp.zeros((1, vs.shape[1]), f32)
            vs[row:row + 1, pl.ds(pl.multiple_of(hg * W, W), W)] = tot[0:1]
        slot(17)
        gain = rows[2:3, :]
        shift = rows[15:16, :]
        acc = [jnp.zeros((1, dn.shape[2]), f32) for _ in range(3)]
        for cp in loads:
            cp.wait()
        def home_copy(b):
            j, rw = rows_of(b)
            i = lax.rem(z, 2)
            zt = 2 * c + j
            return zt, rcopy(ig.at[j, rw], hm.at[i, rw], sh.at[b], qh.at[i, b % 2], dev(x, lax.div(z, 2), zt, y)), \
                pltpu.make_async_copy(ig.at[j, rw], hm.at[i, rw], lh.at[b % 2])
        for b in range(4):
            j, rw = rows_of(b)
            to_sib(1, b).wait()
            to_y(b).wait()
            u = dn[j, rw, :] + dr_c[1, j, rw, :].astype(f32) + dr_y[j, rw, :].astype(f32)
            v = tok_s[j, rw, :].astype(f32) + shift
            cen = v - jnp.mean(v, axis=-1, keepdims=True)
            r = lax.rsqrt(jnp.mean(cen * cen, axis=-1, keepdims=True) + EPS)
            xh = cen * r
            e = u * gain
            res = mg_s[j, rw, :] + r * (e - jnp.mean(e, axis=-1, keepdims=True) - xh * jnp.mean(e * xh, axis=-1, keepdims=True))
            ig[j, rw, :] = res.astype(bf16)
            for n, val in enumerate((u * xh, u, res)):
                acc[n] = acc[n] + jnp.sum(val, axis=0, keepdims=True)
            zt, cp, lc = home_copy(b)
            @pl.when(zt != z)
            def _():
                cp.start()
            @pl.when(zt == z)
            def _():
                lc.start()
            slot(18 + b)
        vs[8:9, :] = acc[0]
        vs[9:10, :] = acc[1]
        vs[10:11, :] = acc[2] * rows[14:15, :]
        vs[11:12, :] = acc[2]
        for k, d in enumerate((sib, yp, xp)):
            cp = rcopy(vs, vr.at[k], sv.at[k], qv.at[k], d)
            cp.start()
            slot(22 + k)
            cp.wait()
            vs[...] = vs[...] + vr[k]
        zv = [rcopy(vs, vr.at[3 + k], sv.at[3 + k], qv.at[3 + k], zp[k]) for k in range(3)]
        for cp in zv:
            cp.start()
        slot(25)
        for i in range(2):
            src = 2 * c + i
            for hb in range(2):
                rw = pl.ds(hb * B, B)
                @pl.when(src != z)
                def _():
                    rcopy(ig.at[0, rw], hm.at[i, rw], sh.at[0], qh.at[i, hb], sib).wait_recv()
                @pl.when(src == z)
                def _():
                    pltpu.make_async_copy(ig.at[0, rw], hm.at[i, rw], lh.at[hb]).wait()
                pass
        for cp in zv:
            cp.wait()
        sums[...] = vs[...] + vr[3] + vr[4] + vr[5]
        slot(26)
        for b in range(4):
            zt, cp, lc = home_copy(b)
            @pl.when(zt != z)
            def _():
                cp.wait_send()

    R = own.shape[1]
    D = own.shape[2]
    pl.run_scoped(after, pltpu.VMEM((2, R, D), bf16), pltpu.VMEM((2, R, D), f32), pltpu.VMEM((2, R, D), f32), pltpu.SemaphoreType.DMA((2,)))


def backward_kernel(dob, qkvT, oT, lse, a1, h1, a2, h2, a3, normed, wT, own, rows, mgrad, sums0, heads, hd):
    W3, N = qkvT.shape
    W = heads * hd
    _, R, D = own.shape
    S = pltpu.SemaphoreType.DMA
    V = pltpu.VMEM
    vm = pl.BlockSpec(memory_space=pltpu.VMEM)
    hbm = pl.BlockSpec(memory_space=pl.ANY)
    b1, b2, b3 = a1.shape[2:], a2.shape[2:], a3.shape[3:]
    def bufs(b, yfirst):
        k = (2, 4) if yfirst else (4, 2)
        return [V(k + b, bf16), V(k + b, bf16), V((4,) + b, bf16), V((3,) + b, bf16)]
    rq = D // 32
    return pl.pallas_call(
        functools.partial(tail_kernel, hd, heads),
        in_specs=[hbm, vm, vm, vm, hbm, hbm, hbm, hbm, hbm, hbm, hbm, hbm, vm, hbm, vm],
        out_specs=[vm] * 4 + [hbm, vm],
        out_shape=[
            jax.ShapeDtypeStruct(b1, f32), jax.ShapeDtypeStruct(b2, f32), jax.ShapeDtypeStruct(b3, f32),
            jax.ShapeDtypeStruct((rq, 3 * D), f32), jax.ShapeDtypeStruct((2, R, D), bf16), jax.ShapeDtypeStruct((16, D), f32),
        ],
        scratch_shapes=[V((4, W, N // 4), bf16), V((W3, N), bf16)] + bufs(b1, True) + bufs(b2, False) + bufs(b3, False) + [
            V((8, R, D), bf16), V((W3, D), bf16),
            V((2, 2, 2, 4, 2, rq, W3 // 2), bf16), V((2, 2, 4, 2, rq, W3 // 2), bf16), V((2, 3, 2, 2, rq, W3 // 2), bf16), V((2, 4, rq, W3 // 2), bf16),
            V((2, 2, R, D), bf16), V((2, 2, R, D), bf16), V((2, R, D), bf16), V((2, R, D), bf16), V((2, R, D), bf16),
            V((16, D), f32), V((6, 16, D), f32),
            S((3,)), S((3,)), S, S((10,)), S((10,)), S((10,)), S((10,)), S((5,)), S((5,)), S((5,)),
            S((2,)), S((2,)), S((2, 3)), S((2, 3)), S((2, 3)), S((2, 3)), S((8,)), S((8,)), S((4,)), S((4,)),
            S((4,)), S((2, 2)), S((2,)), S((6,)), S((6,)), S((2,)), S((2,)),
        ],
        compiler_params=pltpu.CompilerParams(collective_id=1, has_side_effects=True, vmem_limit_bytes=60 << 20),
        name="backward",
    )(dob, qkvT, oT, lse, a1, h1, a2, h2, a3, normed, wT, own, rows, mgrad, sums0)


def result_kernel(rows, fc, o1, o2, o3, gq, hm, bo, sums, r1, r2, r3, rq, rh, rb, *rest):
    for a, b in ((o1, r1), (o2, r2), (o3, r3), (gq, rq), (bo, rb)):
        b[...] = a[...]
    rh[...] = hm[...].astype(f32)
    x, c, z, y = place()
    index = (x * 2 + c) * 8 + z * 2 + y
    per = 128 // rows
    block = sums[:, pl.ds(pl.multiple_of(lax.div(index, per) * 128, 128), 128)]
    mine = pltpu.roll(block, lax.rem(per - lax.rem(index, per), per) * rows, 1)
    for ref, row in zip(rest, (8, 9, 12, 13, 0, 1, 2, None, 3, 10, 11)):
        if row is None:
            per_row = sums.shape[1] // fc
            at = pl.ds(pl.multiple_of(lax.rem(index, per_row) * fc, fc), fc)
            part = sums[0:8, at]
            val = part[4:5]
            for i in range(1, 4):
                val = jnp.where(lax.div(index, per_row) == i, part[4 + i:5 + i], val)
            ref[...] = val
        else:
            ref[...] = mine[row:row + 1, 0:rows]


def results(o1, o2, o3, gq, hm, bo, sums, rows, fc):
    vm = pl.BlockSpec(memory_space=pltpu.VMEM)
    sd = jax.ShapeDtypeStruct
    widths = [rows] * 7 + [fc] + [rows] * 3
    return pl.pallas_call(
        functools.partial(result_kernel, rows, fc),
        in_specs=[vm] * 7,
        out_specs=[vm] * 17,
        out_shape=[sd(a.shape, f32) for a in (o1, o2, o3, gq, hm)] + [sd(bo.shape, bf16)] + [sd((1, w), f32) for w in widths],
        compiler_params=pltpu.CompilerParams(vmem_limit_bytes=60 << 20),
        name="results",
    )(o1, o2, o3, gq, hm, bo, sums)


HEADS = 16


epsilon = EPS


def norm_rows_s(values, gain, shift):
    center = values - jnp.mean(values, axis=-1, keepdims=True)
    spread = jnp.mean(center * center, axis=-1, keepdims=True)
    return center * lax.rsqrt(spread + epsilon) * gain + shift


def gelu_exact_s(values):
    return jax.nn.gelu(values, approximate=False)


def product(left, right):
    return jnp.dot(left, right, preferred_element_type=jnp.float32)


def product_tleft(left, right):
    return lax.dot_general(
        left, right, (((0,), (0,)), ((), ())), preferred_element_type=jnp.float32
    )


def product_tright(left, right):
    return lax.dot_general(
        left, right, (((1,), (1,)), ((), ())), preferred_element_type=jnp.float32
    )


def split_heads(values):
    return values.reshape(values.shape[0], HEADS, values.shape[1] // HEADS)


def attend(operands):
    queries, keys_all, values_all = operands
    scale = (queries.shape[1] // HEADS) ** (-0.5)
    scores = (
        jnp.einsum(
            "qhd,khd->hqk",
            split_heads(queries),
            split_heads(keys_all),
            preferred_element_type=jnp.float32,
        )
        * scale
    )
    highest = jnp.max(scores, axis=-1, keepdims=True)
    exps = jnp.exp(scores - highest)
    totals = jnp.sum(exps, axis=-1, keepdims=True)
    probs_low = (exps / totals).astype(jnp.bfloat16)
    blended = jnp.einsum(
        "hqk,khd->qhd", probs_low, split_heads(values_all), preferred_element_type=jnp.float32
    ).reshape(queries.shape)
    return (blended, (highest + jnp.log(totals))[:, :, 0])


def recompute_probs(queries, keys_all, values_all, grads_in, log_totals):
    scale = (queries.shape[1] // HEADS) ** (-0.5)
    scores = (
        jnp.einsum(
            "qhd,khd->hqk",
            split_heads(queries),
            split_heads(keys_all),
            preferred_element_type=jnp.float32,
        )
        * scale
    )
    probs = jnp.exp(scores - log_totals[:, :, None])
    prob_grads = jnp.einsum(
        "qhd,khd->hqk",
        split_heads(grads_in),
        split_heads(values_all),
        preferred_element_type=jnp.float32,
    )
    return (probs, prob_grads, scale)


def key_side_grads(score_grads, probs, queries, grads_in, row_count):
    key_grads = jnp.einsum(
        "hqk,qhd->khd", score_grads, split_heads(queries), preferred_element_type=jnp.float32
    )
    value_grads = jnp.einsum(
        "hqk,qhd->khd",
        probs.astype(jnp.bfloat16),
        split_heads(grads_in),
        preferred_element_type=jnp.float32,
    )
    width = queries.shape[1]
    return (key_grads.reshape(row_count, width), value_grads.reshape(row_count, width))


def query_side(with_keys, operands):
    queries, keys_all, values_all, grads_in, log_totals = operands
    probs, prob_grads, scale = recompute_probs(queries, keys_all, values_all, grads_in, log_totals)
    row_delta = jnp.sum(probs * prob_grads, axis=-1)
    score_grads = (probs * (prob_grads - row_delta[:, :, None]) * scale).astype(jnp.bfloat16)
    query_grads = jnp.einsum(
        "hqk,khd->qhd", score_grads, split_heads(keys_all), preferred_element_type=jnp.float32
    ).reshape(queries.shape)
    key_grads, value_grads = key_side_grads(
        score_grads, probs, queries, grads_in, keys_all.shape[0]
    )
    return (query_grads, row_delta, key_grads, value_grads)


def spread_on_device(
    tokens_in,
    lead_hours,
    cotangent,
    w_qkv,
    w_out,
    w_fc1,
    w_fc2,
    ln1_gain,
    ln1_bias,
    q_bias,
    v_bias,
    out_bias,
    ln2_gain,
    ln2_bias,
    fc1_bias,
    fc2_bias,
    lead_weight,
    lead_bias,
):
    gathered = (
        lax.all_gather(w_qkv, ("dp", "seq"), axis=0, tiled=True),
        lax.all_gather(w_out, ("dp", "seq"), axis=0, tiled=True),
        lax.all_gather(w_fc1, ("dp", "seq"), axis=0, tiled=True),
        lax.all_gather(w_fc2, ("dp", "seq"), axis=0, tiled=True),
        lax.all_gather(ln1_gain, ("dp", "seq"), axis=0, tiled=True),
        lax.all_gather(ln1_bias, ("dp", "seq"), axis=0, tiled=True),
        lax.all_gather(q_bias, ("dp", "seq"), axis=0, tiled=True),
        lax.all_gather(v_bias, ("dp", "seq"), axis=0, tiled=True),
        lax.all_gather(out_bias, ("dp", "seq"), axis=0, tiled=True),
        lax.all_gather(ln2_gain, ("dp", "seq"), axis=0, tiled=True),
        lax.all_gather(ln2_bias, ("dp", "seq"), axis=0, tiled=True),
        lax.all_gather(fc1_bias, ("dp", "seq"), axis=0, tiled=True),
        lax.all_gather(fc2_bias, ("dp", "seq"), axis=0, tiled=True),
        lax.all_gather(lead_weight, ("dp", "seq"), axis=0, tiled=True),
        lax.all_gather(lead_bias, ("dp", "seq"), axis=0, tiled=True),
    )
    (
        full_qkv,
        full_out,
        full_fc1,
        full_fc2,
        gain_one,
        shift_one,
        bias_query,
        bias_value,
        bias_out,
        gain_two,
        shift_two,
        bias_fc1,
        bias_fc2,
        lead_scale,
        lead_shift,
    ) = gathered
    items, rows, width = tokens_in.shape
    count = items * rows
    lead_times = lead_hours.astype(jnp.float32) / 100.0
    leading = (
        tokens_in.astype(jnp.float32)
        + lead_times[:, None, None] * lead_scale.astype(jnp.float32)
        + lead_shift.astype(jnp.float32)
    ).reshape(count, width)
    normed, norm_one_back = jax.vjp(
        norm_rows_s, leading, gain_one.astype(jnp.float32), shift_one.astype(jnp.float32)
    )
    normed_low = normed.astype(jnp.bfloat16)
    projected = product(normed_low, full_qkv)
    queries = (projected[:, :width] + bias_query.astype(jnp.float32)).astype(jnp.bfloat16)
    keys_own = projected[:, width : 2 * width].astype(jnp.bfloat16)
    values_own = (projected[:, 2 * width :] + bias_value.astype(jnp.float32)).astype(jnp.bfloat16)
    queries3 = queries.reshape(items, rows, width)
    keys_all, values_all = (
        lax.all_gather(keys_own.reshape(items, rows, width), "seq", axis=1, tiled=True),
        lax.all_gather(values_own.reshape(items, rows, width), "seq", axis=1, tiled=True),
    )
    blended, log_totals = lax.map(attend, (queries3, keys_all, values_all))
    blended_low = blended.reshape(count, width).astype(jnp.bfloat16)
    middle = leading + product(blended_low, full_out) + bias_out.astype(jnp.float32)
    normed_two, norm_two_back = jax.vjp(
        norm_rows_s, middle, gain_two.astype(jnp.float32), shift_two.astype(jnp.float32)
    )
    normed_two_low = normed_two.astype(jnp.bfloat16)
    hidden = product(normed_two_low, full_fc1) + bias_fc1.astype(jnp.float32)
    activated, gelu_back = jax.vjp(gelu_exact_s, hidden)
    activated_low = activated.astype(jnp.bfloat16)
    output = middle + product(activated_low, full_fc2) + bias_fc2.astype(jnp.float32)
    block_output = output.reshape(items, rows, width).astype(jnp.bfloat16)
    back_qkv, back_out, back_fc1, back_fc2 = (
        lax.all_gather(w_qkv, ("dp", "seq"), axis=0, tiled=True),
        lax.all_gather(w_out, ("dp", "seq"), axis=0, tiled=True),
        lax.all_gather(w_fc1, ("dp", "seq"), axis=0, tiled=True),
        lax.all_gather(w_fc2, ("dp", "seq"), axis=0, tiled=True),
    )
    out_grad = cotangent.reshape(count, width)
    upstream = out_grad.astype(jnp.float32)
    grad_fc2 = product_tleft(activated_low, out_grad)
    grad_fc2_bias = jnp.sum(upstream, axis=0)
    hidden_grad = gelu_back(product_tright(out_grad, back_fc2))[0].astype(jnp.bfloat16)
    grad_fc1 = product_tleft(normed_two_low, hidden_grad)
    grad_fc1_bias = jnp.sum(hidden_grad.astype(jnp.float32), axis=0)
    middle_part, grad_ln2_gain, grad_ln2_bias = norm_two_back(product_tright(hidden_grad, back_fc1))
    middle_grad = upstream + middle_part
    attn_grad = middle_grad.astype(jnp.bfloat16)
    grad_out = product_tleft(blended_low, attn_grad)
    grad_out_bias = jnp.sum(attn_grad.astype(jnp.float32), axis=0)
    blended_grad = (
        product_tright(attn_grad, back_out).astype(jnp.bfloat16).reshape(items, rows, width)
    )
    query_grads, row_delta, key_parts, value_parts = lax.map(
        partial(query_side, True), (queries3, keys_all, values_all, blended_grad, log_totals)
    )
    key_grads, value_grads = (
        lax.psum_scatter(
            key_parts.astype(jnp.bfloat16), "seq", scatter_dimension=1, tiled=True
        ).astype(jnp.float32),
        lax.psum_scatter(
            value_parts.astype(jnp.bfloat16), "seq", scatter_dimension=1, tiled=True
        ).astype(jnp.float32),
    )
    query_low = query_grads.reshape(count, width).astype(jnp.bfloat16)
    key_low = key_grads.reshape(count, width).astype(jnp.bfloat16)
    value_low = value_grads.reshape(count, width).astype(jnp.bfloat16)
    qkv_grad = jnp.concatenate([query_low, key_low, value_low], axis=1)
    grad_qkv = product_tleft(normed_low, qkv_grad)
    grad_q_bias = jnp.sum(query_low.astype(jnp.float32), axis=0)
    grad_v_bias = jnp.sum(value_low.astype(jnp.float32), axis=0)
    leading_part, grad_ln1_gain, grad_ln1_bias = norm_one_back(product_tright(qkv_grad, back_qkv))
    input_grad = (middle_grad + leading_part).reshape(items, rows, width)
    grad_lead_weight = jnp.sum(jnp.sum(input_grad, axis=1) * lead_times[:, None], axis=0)
    grad_lead_bias = jnp.sum(input_grad, axis=(0, 1))
    summed = (
        lax.psum_scatter(grad_qkv, ("dp", "seq"), scatter_dimension=0, tiled=True),
        lax.psum_scatter(grad_out, ("dp", "seq"), scatter_dimension=0, tiled=True),
        lax.psum_scatter(grad_fc1, ("dp", "seq"), scatter_dimension=0, tiled=True),
        lax.psum_scatter(grad_fc2, ("dp", "seq"), scatter_dimension=0, tiled=True),
        lax.psum_scatter(grad_ln1_gain, ("dp", "seq"), scatter_dimension=0, tiled=True),
        lax.psum_scatter(grad_ln1_bias, ("dp", "seq"), scatter_dimension=0, tiled=True),
        lax.psum_scatter(grad_q_bias, ("dp", "seq"), scatter_dimension=0, tiled=True),
        lax.psum_scatter(grad_v_bias, ("dp", "seq"), scatter_dimension=0, tiled=True),
        lax.psum_scatter(grad_out_bias, ("dp", "seq"), scatter_dimension=0, tiled=True),
        lax.psum_scatter(grad_ln2_gain, ("dp", "seq"), scatter_dimension=0, tiled=True),
        lax.psum_scatter(grad_ln2_bias, ("dp", "seq"), scatter_dimension=0, tiled=True),
        lax.psum_scatter(grad_fc1_bias, ("dp", "seq"), scatter_dimension=0, tiled=True),
        lax.psum_scatter(grad_fc2_bias, ("dp", "seq"), scatter_dimension=0, tiled=True),
        lax.psum_scatter(grad_lead_weight, ("dp", "seq"), scatter_dimension=0, tiled=True),
        lax.psum_scatter(grad_lead_bias, ("dp", "seq"), scatter_dimension=0, tiled=True),
    )
    return (block_output, input_grad) + tuple(summed)


def on_device(mesh_shape, tokens_in, lead_hours, cotangent, w_qkv, w_out, w_fc1, w_fc2, ln1_gain, ln1_bias, q_bias, v_bias,
              out_bias, ln2_gain, ln2_bias, fc1_bias, fc2_bias, lead_weight, lead_bias):
    _, R, D = tokens_in.shape
    FF = w_fc1.shape[1]
    hd = D // HEADS
    heads = HEADS // 4
    W = heads * hd
    rows = w_qkv.shape[0]
    vectors = (lead_weight, lead_bias, ln1_gain, ln1_bias, q_bias, v_bias, out_bias, ln2_gain, ln2_bias, fc2_bias, fc1_bias,
               lead_hours.astype(bf16))
    small = sum(lax.pad(v[None].astype(f32), f32(0), ((k, 31 - k, 0), (0, 128 - v.shape[0], 0))) for k, v in enumerate(vectors)).astype(bf16)
    normed, qkvT, oT, lse, own, vec, wT, a1, h1, a2, h2, a3, dob, mgrad, block_output, sums0 = forward_kernel(
        tokens_in, cotangent, w_qkv, small, w_fc1, w_fc2, w_out, heads, hd)[:16]
    o1, o2, o3, gq, hm, sums = backward_kernel(
        dob, qkvT, oT, lse, a1, h1, a2, h2, a3.reshape(2, 4, 2, rows, D), normed, wT,
        own, vec, mgrad, sums0, heads, hd)
    grad_fc1, grad_fc2, grad_out, grad_qkv, home, block_output, *small = results(
        o1, o2, o3, gq, hm, block_output, sums, rows, fc1_bias.shape[0])
    return (block_output, home, grad_qkv, grad_out, grad_fc1, grad_fc2) + tuple(v.reshape(-1) for v in small)


def choose(mesh_shape, *args):
    items, rows = args[0].shape[0], args[3].shape[0]
    planes = mesh_shape["seq"] // 2
    if items == 2 and planes == 2 * items and mesh_shape["dp"] == 4 and rows % 16 == 0 and 4 * args[0].shape[1] == args[0].shape[2]:
        return on_device(mesh_shape, *args)
    return spread_on_device(*args)


def solution(mesh):
    big, rows, vec = P("dp", "seq", None), P(("dp", "seq"), None), P(("dp", "seq"))
    in_specs = (big, P("dp"), big) + (rows,) * 4 + (vec,) * 11
    out_specs = (big, big) + (rows,) * 4 + (vec,) * 11
    body = functools.partial(choose, dict(mesh.shape))
    return jax.shard_map(body, mesh=mesh, in_specs=in_specs, out_specs=out_specs, check_vma=False)
```

```python
import functools
from functools import partial
import jax, jax.numpy as jnp
from jax import lax
from jax.experimental import pallas as pl
from jax.experimental.pallas import tpu as pltpu
from jax.sharding import PartitionSpec as P

MESH = pl.DeviceIdType.MESH
f32, bf16 = jnp.float32, jnp.bfloat16
LOG2E = 1.4426950408889634
EPS = 1e-06


def dot_nn(a, b):
    return lax.dot_general(a, b, (((1,), (0,)), ((), ())), preferred_element_type=f32)


def dot_nt(a, b):
    return lax.dot_general(a, b, (((1,), (1,)), ((), ())), preferred_element_type=f32)


def rcopy(src, dst, ssem, rsem, dev):
    return pltpu.make_async_remote_copy(src_ref=src, dst_ref=dst, send_sem=ssem, recv_sem=rsem, device_id=dev, device_id_type=MESH)


def place():
    dp, seq = lax.axis_index("dp"), lax.axis_index("seq")
    return lax.div(dp, 2), lax.rem(dp, 2), lax.div(seq, 2), lax.rem(seq, 2)


def dev(x, c, z, y):
    return (x * 2 + c, z * 2 + y)


def greet(partners):
    bar = pltpu.get_barrier_semaphore()
    for p in partners:
        pl.semaphore_signal(bar, inc=1, device_id=p, device_id_type=MESH)
    pl.semaphore_wait(bar, len(partners))


def fwd_kernel(hd, heads, tok, cot, wq, small, fa, fb, fc, normed, qkv_out, o_out, lse, own_out, vec, w_out_, a1, h1, a2, h2, a3, dob_out, mg_out, bo, sums,
               ga, gb, gc, qkvT, oT, wT, own, dob, mgrad, T, Ws, fb1, bt, up, r1, r2, r3, st, rt, lt, sy, ry, sc, rc, scy, rcy, sa, ra, la, sz, rz, sx, rx, so, ro, lo,
               ln, su, ru, lu, gss, grs, gsz, grz, gs1, gr1, gs2, gr2, gsc, grc, sf1, rf1, sf2, rf2, sf3, rf3, la1, la2, la3,
               sh1, qh1, sh2, qh2, sbo, qbo, lbo, lq):
    x, c, z, y = place()
    hg = c * 2 + y
    W = heads * hd
    D = T.shape[2]
    R = T.shape[1]
    N = qkvT.shape[1]
    zoff = [lax.rem(z + k, 4) for k in (1, 2, 3)]
    sums[...] = jnp.zeros_like(sums)
    greet([dev(x, c, zz, y) for zz in zoff] + [dev(x, 1 - c, zz, y) for zz in zoff]
          + [dev(x, 1 - c, z, y), dev(x, c, z, 1 - y), dev(x, 1 - c, z, 1 - y), dev(1 - x, c, z, y)])
    sib, yp, diag, xp = dev(x, 1 - c, z, y), dev(x, c, z, 1 - y), dev(x, 1 - c, z, 1 - y), dev(1 - x, c, z, y)
    pos = (lax.div(z, 2) * 2 + y) * 2 + lax.rem(z, 2)
    tcp = []
    for i in range(2):
        zt = 2 * c + i
        cp = rcopy(tok.at[i], T.at[pos], st.at[i], rt.at[lax.rem(z, 2)], dev(x, lax.div(z, 2), zt, y))
        loc = pltpu.make_async_copy(tok.at[i], T.at[pos], lt)
        @pl.when(zt != z)
        def _():
            cp.start()
        @pl.when(zt == z)
        def _():
            loc.start()
        tcp.append((zt, cp, loc))
    xz = x * 4 + z
    def slices(g):
        dst = Ws.at[xz, hg]
        out = [(wq.at[:, pl.ds(pl.multiple_of(q * D + g * W, W), W)], dst.at[:, q * W:(q + 1) * W]) for q in range(3)]
        return out + [(small, dst.at[:, 3 * W:3 * W + 128])]
    wa = [pltpu.make_async_copy(a, b, la.at[n]) for n, (a, b) in enumerate(slices(hg))]
    for k, (d, g) in enumerate(((yp, c * 2 + 1 - y), (sib, (1 - c) * 2 + y), (diag, (1 - c) * 2 + 1 - y))):
        wa += [rcopy(a, b, sa.at[k, n], ra.at[k, n], d) for n, (a, b) in enumerate(slices(g))]
    for cp in wa:
        cp.start()
    for cp in wa:
        cp.wait()
    def zz_of(u):
        return z if u == 0 else (z - u if u <= 3 else z + (u - 3))

    def ok(u):
        return True if u == 0 else (z >= u if u <= 3 else z + (u - 3) <= 3)

    def guard(cond, f):
        if cond is True:
            f()
        else:
            pl.when(cond)(f)

    def w_z(u, down):
        v = Ws.at[x * 4 + zz_of(u)]
        k = (u if u <= 3 else u - 3) + (3 if down else 0)
        return rcopy(v, v, sz.at[k], rz.at[k], dev(x, c, z - 1 if down else z + 1, y))

    def w_arr(u):
        v = Ws.at[x * 4 + zz_of(u)]
        return rcopy(v, v, sz.at[u - 1], rz.at[u - 1], sib)

    def w_x(u):
        v = Ws.at[x * 4 + zz_of(u)]
        return rcopy(v, v, sx.at[u], rx.at[u], xp)

    def w_recv(d):
        for u in (d, d + 3):
            def go(u=u):
                w_arr(u).wait_recv()
                if d < 3:
                    guard((z > 0) if u > 3 else (z < 3), lambda: w_z(u, u > 3).start())
                w_x(u).start()
            guard(ok(u), go)

    guard(z < 3, lambda: w_z(0, False).start())
    guard(z > 0, lambda: w_z(0, True).start())
    w_x(0).start()
    ca = 1 - c
    gat = ((fa, ga, False), (fb, gb, True), (fc, gc, False))
    before_z = (False, True, True)
    known = set()

    def g_start(p):
        f, g, _ = gat[p]
        return rcopy(f, g.at[x, c, z, y], gss.at[p], grs.at[p], sib)

    def z_block(p, u):
        g, xfirst = gat[p][1:]
        if not before_z[p]:
            return g.at[x, ca, zz_of(u), y]
        return g.at[:, ca, zz_of(u), y] if xfirst else g.at[x, ca, zz_of(u)]

    def g_z(p, u, down):
        v = z_block(p, u)
        d = u if u <= 3 else u - 3
        k = d + (3 if down else 0)
        return rcopy(v, v, gsz.at[p, k], grz.at[p, k], dev(x, c, z - 1 if down else z + 1, y))

    def g_zarr(p, u):
        v = z_block(p, u)
        return rcopy(v, v, gsz.at[p, u - 1], grz.at[p, u - 1], sib)

    def g_one(p, u):
        g, xfirst = gat[p][1:]
        v = g.at[x, ca, zz_of(u), y]
        return rcopy(v, v, gs1.at[p, u], gr1.at[p, u], xp if xfirst else yp)

    def g_two(p, u):
        g, xfirst = gat[p][1:]
        v = g.at[:, ca, zz_of(u), y] if xfirst else g.at[x, ca, zz_of(u)]
        return rcopy(v, v, gs2.at[p, u], gr2.at[p, u], yp if xfirst else xp)

    def g_core(p, u):
        v = gat[p][1].at[:, ca, zz_of(u)]
        return rcopy(v, v, gsc.at[p, u], grc.at[p, u], sib)

    def ag_own(p):
        g_start(p).wait()
        g_one(p, 0).start()

    def one_own(p):
        if p not in known:
            known.add(p)
            g_one(p, 0).wait()

    def ag_z0(p, d):
        if before_z[p]:
            one_own(p)
        guard(z < 3, lambda: g_z(p, 0, False).start())
        guard(z > 0, lambda: g_z(p, 0, True).start())

    def ag_recv(p, d):
        for u in (d, d + 3):
            def go(u=u):
                g_zarr(p, u).wait_recv()
                if d < 3:
                    guard((z > 0) if u > 3 else (z < 3), lambda: g_z(p, u, u > 3).start())
                (g_two if before_z[p] else g_one)(p, u).start()
            guard(ok(u), go)

    def units(d):
        return (0,) if d == 0 else (d, d + 3)

    def ag_two(p, d):
        if before_z[p] and d > 0:
            return
        for u in units(d):
            def go(u=u):
                if u == 0:
                    one_own(p)
                else:
                    g_one(p, u).wait()
                g_two(p, u).start()
            guard(ok(u), go)

    def ag_core(p, d):
        for u in units(d):
            def go(u=u):
                g_two(p, u).wait()
                g_core(p, u).start()
            guard(ok(u), go)

    def ag_got(p, half):
        own_half = ((0, True), (1, lax.rem(z, 2) == 1), (4, lax.rem(z, 2) == 0))
        rest = ((1, z == 2), (2, z >= 2), (3, z == 3), (4, z == 1), (5, z <= 1), (6, z == 0))
        for u, cond in (own_half if half == 0 else rest):
            guard(cond, lambda: g_core(p, u).wait())

    def ag_sent(p):
        for u in (0, 1, 2):
            guard((z >= u) & (z < 3), lambda: g_z(p, u, False).wait_send())
            guard((z + u <= 3) & (z > 0), lambda: g_z(p, u + 3 if u else 0, True).wait_send())

    PLAN = {
        0: ((ag_two, 1, 0),),
        2: ((ag_z0, 1, 0), (ag_two, 0, 0),),
        3: ((ag_z0, 0, 0),),
        4: ((ag_two, 2, 0),),
        5: ((ag_recv, 0, 1),),
        7: ((ag_recv, 2, 1), (ag_recv, 1, 1),),
        10: ((ag_two, 1, 1),),
        11: ((ag_recv, 2, 2), (ag_recv, 0, 3),),
        12: ((ag_two, 2, 1),),
        13: ((ag_two, 0, 2),),
        14: ((ag_two, 2, 2),),
        15: ((ag_core, 0, 0),),
        17: ((ag_core, 2, 0),),
        18: ((ag_recv, 2, 3),),
        19: ((ag_two, 0, 3),),
        20: ((ag_recv, 1, 2),),
        22: ((ag_core, 0, 1), (ag_core, 0, 2),),
        23: ((ag_core, 2, 2), (ag_core, 1, 1),),
        24: ((ag_two, 2, 3), (ag_core, 2, 1), (ag_core, 2, 3),),
        25: ((ag_two, 1, 2), (ag_two, 1, 3), (ag_core, 0, 3), (ag_recv, 1, 3),),
        26: ((ag_core, 1, 2),),
        28: ((ag_core, 1, 3),),
        35: ((ag_z0, 2, 0), (ag_two, 0, 1),),
        36: ((ag_core, 1, 0), (ag_recv, 0, 2),),
    }

    COT = 14

    def ag_slot(i):
        for f, p, d in PLAN.get(i, ()):
            f(p, d)

    for p in (2, 0, 1):
        g_start(p).start()
    for p in (2, 0, 1):
        ag_own(p)
    ag_slot(0)
    w_recv(1)
    ag_slot(1)
    ycp, ccp, cycp = [], [], []
    j0 = jnp.where(lax.div(z, 2) == c, lax.rem(z, 2), 0)
    for j in (j0, 1 - j0):
        src_z = 2 * c + j
        p = hg * 2 + j
        @pl.when(src_z != z)
        def _():
            rcopy(tok.at[0], T.at[p], st.at[0], rt.at[j], sib).wait_recv()
        @pl.when(src_z == z)
        def _():
            pltpu.make_async_copy(tok.at[0], T.at[p], lt).wait()
        a = rcopy(T.at[p], T.at[p], sy.at[j], ry.at[j], yp)
        b = rcopy(T.at[p], T.at[p], sc.at[j], rc.at[j], sib)
        a.start()
        b.start()
        ycp.append(a)
        ccp.append(b)
    ag_slot(2)
    w_recv(2)
    ag_slot(3)
    w_recv(3)
    ag_slot(4)
    for n, j in enumerate((j0, 1 - j0)):
        ycp[n].wait()
        p = (c * 2 + 1 - y) * 2 + j
        cp = rcopy(T.at[p], T.at[p], scy.at[j], rcy.at[j], sib)
        cp.start()
        cycp.append(cp)
    ag_slot(5)
    for u in range(7):
        guard(ok(u), lambda: w_x(u).wait())
    for u in (0, 1, 2):
        guard((z >= u) & (z < 3), lambda: w_z(u, False).wait_send())
        guard((z + u <= 3) & (z > 0), lambda: w_z(u + 3 if u else 0, True).wait_send())
    for xx in range(2):
        for zz in range(4):
            for cc in range(2):
                for yy in range(2):
                    r = (xx * 2 + cc) * 8 + zz * 2 + yy
                    blk = Ws[xx * 4 + zz, cc * 2 + yy, 0:16, 3 * W:3 * W + 128].astype(f32)
                    vec[:, r * 32:(r + 1) * 32] = blk[:, 0:32]
                    fb1[:, r * 128:(r + 1) * 128] = blk[8:16, :]
                c0 = (xx * 2 + cc) * 256 + zz * 64
                wT[:, c0:c0 + 64] = Ws[xx * 4 + zz, cc * 2:cc * 2 + 2, :, 0:3 * W].reshape(64, 3 * W).T
    hours = jnp.zeros((1, 1), f32)
    for zz in range(4):
        hz = Ws[x * 4, (zz // 2) * 2, 0:16, 3 * W:3 * W + 128].astype(f32)[11:12, zz % 2:zz % 2 + 1]
        hours = jnp.where(z == zz, hz, hours)
    t = hours / 100.0
    for j in range(2):
        ccp[j].wait()
        cycp[j].wait()
    ag_slot(6)
    shift = t * vec[0:1, :] + vec[1:2, :]
    vec[14:15, :] = jnp.broadcast_to(t, (1, D))
    vec[15:16, :] = shift
    gain, bias = vec[2:3, :], vec[3:4, :]
    qb = vec[:, pl.ds(hg * W, W)].T
    def blk(p, carry):
        for i in range(8):
            if 34 + i in PLAN:
                @pl.when(p == i)
                def _():
                    ag_slot(34 + i)
        v = T[p].astype(f32) + shift
        cen = v - jnp.mean(v, axis=-1, keepdims=True)
        r = lax.rsqrt(jnp.mean(cen * cen, axis=-1, keepdims=True) + EPS)
        nb = (cen * r * gain + bias).astype(bf16)
        T[p] = nb
        pr = dot_nt(wT[...], nb)
        cols = pl.ds(p * R, R)
        qkvT[0:W, cols] = (pr[0:W] + qb[:, 4:5]).astype(bf16)
        qkvT[W:2 * W, cols] = pr[W:2 * W].astype(bf16)
        qkvT[2 * W:3 * W, cols] = (pr[2 * W:] + qb[:, 5:6]).astype(bf16)
        return carry
    own[...] = T[pl.ds(hg * 2, 2)]
    lax.fori_loop(0, T.shape[0], blk, 0)
    keep = pltpu.make_async_copy(T, normed, ln)
    keep.start()
    early = [pltpu.make_async_copy(a, b, lq.at[i]) for i, (a, b) in enumerate(((qkvT, qkv_out), (wT, w_out_), (oT, o_out)))]
    early.append(pltpu.make_async_copy(own, own_out, lq.at[3]))
    early[0].start()
    early[1].start()
    early[3].start()
    ag_slot(7)
    keep.wait()
    def cot_copy(i):
        zt = 2 * c + i
        return zt, rcopy(cot.at[i], up.at[lax.rem(z, 2)], su.at[i], ru.at[lax.rem(z, 2)], dev(x, lax.div(z, 2), zt, y))
    def cot_start():
        for i in range(2):
            zt, cp = cot_copy(i)
            @pl.when(zt != z)
            def _():
                cp.start()
            @pl.when(zt == z)
            def _():
                pltpu.make_async_copy(cot.at[i], up.at[lax.rem(z, 2)], lu).start()
    def cot_wait():
        for j in range(2):
            @pl.when(2 * c + j != z)
            def _():
                rcopy(cot.at[0], up.at[j], su.at[0], ru.at[j], sib).wait_recv()
            @pl.when(2 * c + j == z)
            def _():
                pltpu.make_async_copy(cot.at[0], up.at[j], lu).wait()
            zt, cp = cot_copy(j)
            @pl.when(zt != z)
            def _():
                cp.wait_send()
    def attention(k_s, o_s):
        for h in range(heads):
            k_s[h] = qkvT[W + h * hd:W + (h + 1) * hd, :].T
        QB, KB = 2 * R, 512
        cs = LOG2E * hd ** -0.5
        nk = N // KB
        def group(k, carry):
            cc = jnp.where((k == 1) | (k == 2), 1 - c, c)
            yy = jnp.where(k < 2, 1 - y, y)
            g = cc * 2 + yy
            qcols = pl.ds(g * QB, QB)
            def head(h, carry):
                step = k * heads + h
                for i in range(16):
                    if 8 + i in PLAN or COT == 8 + i:
                        @pl.when(step == i)
                        def _():
                            ag_slot(8 + i)
                            if COT == 8 + i:
                                cot_start()
                qt = qkvT[pl.ds(h * hd, hd), qcols]
                def scores(i):
                    return dot_nn(k_s[h, i * KB:(i + 1) * KB, :], qt)
                m = None
                s = scores(0)
                for i in range(nk):
                    nxt = scores(i + 1) if i + 1 < nk else None
                    cm = jnp.max(s, axis=0, keepdims=True)
                    mn = cm if m is None else jnp.maximum(m, cm)
                    p = jnp.exp2(s * cs - mn * cs)
                    ps = jnp.sum(p, axis=0, keepdims=True)
                    vt = qkvT[pl.ds(2 * W + h * hd, hd), i * KB:(i + 1) * KB]
                    ov = dot_nn(vt, p.astype(bf16))
                    if m is None:
                        l, o = ps, ov
                    else:
                        a = jnp.exp2((m - mn) * cs)
                        l = l * a + ps
                        o = o * a + ov
                    m = mn
                    s = nxt
                o = o / l
                o_s[g, pl.ds(h * hd, hd), :] = o.astype(bf16)
                oT[pl.ds(h * hd, hd), qcols] = o
                lse[pl.ds(h, 1), qcols] = m * cs + jnp.log2(l)
                return carry
            lax.fori_loop(0, heads, head, 0)
            @pl.when(k < 3)
            def _():
                rcopy(o_s.at[g], bt.at[hg], so.at[k], ro.at[k], dev(x, cc, z, yy)).start()
            @pl.when(k == 3)
            def _():
                pltpu.make_async_copy(o_s.at[g], bt.at[hg], lo).start()
            return carry
        lax.fori_loop(0, 4, group, 0)
        for k, d in enumerate((yp, diag, sib)):
            rcopy(o_s.at[0], bt.at[hg], so.at[k], ro.at[k], d).wait()
        pltpu.make_async_copy(o_s.at[0], bt.at[hg], lo).wait()
    pl.run_scoped(attention, pltpu.VMEM((heads, N, hd), bf16), pltpu.VMEM((4, W, 2 * R), bf16))
    for i in range(2):
        zt, cp, loc = tcp[i]
        @pl.when(zt != z)
        def _():
            cp.wait_send()


    early[2].start()
    FF = fb1.shape[1]
    C = 2 * R

    def out_copy(bout, j):
        zt = 2 * c + j
        return zt, rcopy(bout.at[j], bo.at[lax.rem(z, 2)], sbo.at[j], qbo.at[lax.rem(z, 2)], dev(x, lax.div(z, 2), zt, y)), \
            pltpu.make_async_copy(bout.at[j], bo.at[lax.rem(z, 2)], lbo)
    def out_wait(bout):
        for i in range(2):
            zt, cp, lc = out_copy(bout, i)
            @pl.when(2 * c + i != z)
            def _():
                rcopy(bout.at[0], bo.at[i], sbo.at[0], qbo.at[i], sib).wait_recv()
            @pl.when(2 * c + i == z)
            def _():
                pltpu.make_async_copy(bout.at[0], bo.at[i], lbo).wait()
            @pl.when(zt != z)
            def _():
                cp.wait_send()

    def middle_part(Wo, mid_s, n2, n2T, oacc, dacc, f1b, f2b, p1, sb1, k1, p2, sb2, k2, sb3, bout, lw, l1, l2):
        ag_slot(24)
        ag_got(2, 0)
        ag_got(2, 1)
        cpw = pltpu.make_async_copy(gc, Wo, lw)
        cpw.start()
        bT = bt[...].reshape(4 * W, C).T
        cpw.wait()
        w_o = Wo[...].reshape(D, D)
        def norm(v):
            cen = v - jnp.mean(v, axis=-1, keepdims=True)
            return cen, lax.rsqrt(jnp.mean(cen * cen, axis=-1, keepdims=True) + EPS)
        for j in range(2):
            v = own[j].astype(f32) + vec[15:16, :] + dot_nn(bT[j * R:(j + 1) * R], w_o) + vec[6:7, :]
            mid_s[j] = v
            cen, r = norm(v)
            nb = (cen * r * vec[7:8, :] + vec[8:9, :]).astype(bf16)
            n2[j] = nb
            n2T[:, :, j * R:(j + 1) * R] = nb.T.reshape(4, D // 4, R)
        ag_slot(25)
        ag_got(0, 0)
        ag_got(0, 1)
        cot_wait()
        ag_got(1, 0)

        def order(s):
            zp = jnp.where(s < 4, lax.div(z, 2), 1 - lax.div(z, 2))
            xx = jnp.where(lax.rem(lax.div(s, 2), 2) == 0, 1 - x, x)
            cc = lax.rem(s, 2)
            return xx, cc, zp, (xx * 2 + cc) * 2 + zp
        def loads(s):
            xx, cc, zp, j = order(s)
            slot = lax.rem(s, 2)
            return (pltpu.make_async_copy(ga.at[:, :, :, :, :, pl.ds(pl.multiple_of(j * C, C), C)], f1b.at[slot], l1.at[slot]),
                    pltpu.make_async_copy(gb.at[xx, cc, pl.ds(zp * 2, 2)], f2b.at[slot], l2.at[slot]))
        for cp in loads(0):
            cp.start()
        oacc[...] = jnp.zeros_like(oacc)
        dacc[...] = jnp.zeros_like(dacc)
        def sends(s):
            slot = lax.rem(s, 2)
            return (rcopy(sb1.at[slot], r1.at[slot], sf1.at[s], rf1.at[s], sib), rcopy(sb2, r2, sf2.at[s], rf2.at[s], sib))
        def cols_of(s):
            return pl.ds(pl.multiple_of(order(s)[3] * C, C), C)
        def go1(s):
            slot = lax.rem(s, 2)
            out = []
            for q in range(2):
                cs_ = pl.ds(q * C, C)
                out.append(rcopy(k1.at[slot, :, 1 - y, :, cs_], h1.at[q, :, :, cols_of(s)], sh1.at[s, q], qh1.at[s, q], yp))
                out.append(pltpu.make_async_copy(k1.at[slot, :, y, :, cs_], a1.at[q, :, :, cols_of(s)], la1.at[s, q]))
            return out
        def go2(s):
            slot, zp = lax.rem(lax.div(s, 2), 2), order(s)[2]
            i = lax.div(s, 4)
            return (rcopy(k2.at[slot], h2.at[pl.ds(zp * 2, 2)], sh2.at[i], qh2.at[i], xp),
                    pltpu.make_async_copy(k2.at[slot], a2.at[pl.ds(zp * 2, 2)], la2.at[i]))
        def keeps(s):
            return lax.rem(s, 2) == c
        def away(s):
            return lax.rem(lax.div(s, 2), 2) == 0
        def finish(s):
            slot = lax.rem(s, 2)
            sends(s)[0].wait_recv()
            @pl.when(s >= 2)
            def _():
                for n, cp in enumerate(go1(s - 2)):
                    cp.wait() if n % 2 else cp.wait_send()
            k1[slot] = (p1[...].astype(f32) + r1[slot].astype(f32)).astype(bf16)
            for cp in go1(s):
                cp.start()
            @pl.when(keeps(s))
            def _():
                sends(s)[1].wait_recv()
                @pl.when(s >= 4)
                def _():
                    @pl.when(away(s))
                    def _():
                        go2(s - 4)[0].wait_send()
                    @pl.when(jnp.logical_not(away(s)))
                    def _():
                        go2(s - 4)[1].wait()
                k2[lax.rem(lax.div(s, 2), 2)] = (p2[...].astype(f32) + r2[...].astype(f32)).astype(bf16).reshape(k2.shape[1:])
                @pl.when(away(s))
                def _():
                    go2(s)[0].start()
                @pl.when(jnp.logical_not(away(s)))
                def _():
                    go2(s)[1].start()
        def chunk(s, carry):
            slot = lax.rem(s, 2)
            xx, cc, zp, j = order(s)
            for cp in loads(s):
                cp.wait()
            for i in range(8):
                if 26 + i in PLAN or i == 3:
                    @pl.when(s == i)
                    def _():
                        ag_slot(26 + i)
                        if i == 3:
                            ag_got(1, 1)
            @pl.when(s < 7)
            def _():
                for cp in loads(s + 1):
                    cp.start()
            f1c = f1b[slot].reshape(D, C)
            f2c = f2b[slot].reshape(C, D)
            u2 = up[...].reshape(C, D)
            h = dot_nn(n2[...].reshape(C, D), f1c) + fb1[2:3, pl.ds(pl.multiple_of(j * C, C), C)]
            da = dot_nt(u2, f2c)
            ph = 0.5 + 0.5 * lax.erf(h * 0.7071067811865476)
            act = (h * ph).astype(bf16)
            hgr = (da * (ph + h * (jnp.exp(-0.5 * h * h) * 0.3989422804014327))).astype(bf16)
            oacc[...] += dot_nn(act, f2c).reshape(2, R, D)
            sums[pl.ds(4 + lax.div(j, 2), 1), pl.ds(pl.multiple_of(lax.rem(j, 2) * C, C), C)] = jnp.sum(hgr.astype(f32), axis=0, keepdims=True)
            dacc[...] += dot_nt(hgr, f1c).reshape(2, R, D)
            @pl.when(s > 0)
            def _():
                finish(s - 1)
            @pl.when(s >= 2)
            def _():
                sends(s - 2)[0].wait_send()
            @pl.when((s >= 2) & jnp.logical_not(keeps(s)))
            def _():
                sends(s - 2)[1].wait_send()
            for q in range(2):
                sb1[slot, :, :, :, q * C:(q + 1) * C] = dot_nn(n2T[q * 2 + 1 - c], hgr).astype(bf16).reshape(4, 2, R // 8, C)
            sends(s)[0].start()
            g2 = dot_nn(act.T, u2).astype(bf16)
            @pl.when(keeps(s))
            def _():
                p2[...] = g2
            @pl.when(jnp.logical_not(keeps(s)))
            def _():
                sb2[...] = g2
                sends(s)[1].start()
            for q in range(2):
                p1[:, :, :, q * C:(q + 1) * C] = dot_nn(n2T[q * 2 + c], hgr).astype(bf16).reshape(4, 2, R // 8, C)
            return carry
        lax.fori_loop(0, 8, chunk, 0)
        for j in range(2):
            bout[j] = (mid_s[j] + oacc[j] + vec[9:10, :]).astype(bf16)
            zt, cp, lc = out_copy(bout, j)
            @pl.when(zt != z)
            def _():
                cp.start()
            @pl.when(zt == z)
            def _():
                lc.start()
        last = jnp.int32(7)
        finish(last)

        tot = [jnp.zeros((1, D), f32) for _ in range(4)]
        ags = []
        for j in range(2):
            v = mid_s[j]
            cen, r = norm(v)
            xh = cen * r
            u = dacc[j]
            e = u * vec[7:8, :]
            g = up[j].astype(f32) + r * (e - jnp.mean(e, axis=-1, keepdims=True) - xh * jnp.mean(e * xh, axis=-1, keepdims=True))
            mgrad[j] = g
            ag = g.astype(bf16)
            ags.append(ag)
            for n, val in enumerate((ag.astype(f32), u * xh, u, up[j].astype(f32))):
                tot[n] = tot[n] + jnp.sum(val, axis=0, keepdims=True)
        for n in range(4):
            sums[n:n + 1, :] = tot[n]
        ag = jnp.concatenate(ags, axis=0)
        for q in range(2):
            sb3[q] = dot_nn(bt[q * 2 + 1 - c], ag).astype(bf16)
            rcopy(sb3.at[q], r3.at[q], sf3.at[q], rf3.at[q], sib).start()
        for q in range(4):
            dob[q] = dot_nt(Wo[q // 2, q % 2].reshape(D // 4, D), ag).astype(bf16)
        late = [pltpu.make_async_copy(dob, dob_out, lq.at[4]), pltpu.make_async_copy(mgrad, mg_out, lq.at[5])]
        for cp in late:
            cp.start()
        for q in range(2):
            rcopy(sb3.at[q], r3.at[q], sf3.at[q], rf3.at[q], sib).wait()
            r3[q] = (r3[q].astype(f32) + dot_nn(bt[q * 2 + c], ag)).astype(bf16)
        cp3 = pltpu.make_async_copy(r3, a3, la3)
        cp3.start()
        for s in (6, 7):
            sends(s)[0].wait_send()
            @pl.when(c != s % 2)
            def _():
                sends(s)[1].wait_send()
            for n, cp in enumerate(go1(jnp.int32(s))):
                cp.wait() if n % 2 else cp.wait_send()
        for s in range(8):
            for cp in go1(jnp.int32(s))[::2]:
                cp.wait_recv()
        go2(4 + c)[0].wait_send()
        go2(6 + c)[1].wait()
        for i in range(2):
            go2(i * 4 + c)[0].wait_recv()
        cp3.wait()
        for cp in early + late:
            cp.wait()
        out_wait(bout)
        for p in range(3):
            ag_sent(p)

    SD = pltpu.SemaphoreType.DMA
    V = pltpu.VMEM
    blk1 = (4, 2, R // 8, 2 * C)
    pl.run_scoped(middle_part, V(gc.shape, bf16), V((2, R, D), f32), V((2, R, D), bf16), V((4, D // 4, C), bf16), V((2, R, D), f32),
                  V((2, R, D), f32), V((2,) + ga.shape[:5] + (C,), bf16), V((2, 2) + gb.shape[3:], bf16),
                  V(blk1, bf16), V((2,) + blk1, bf16), V((2,) + blk1, bf16), V((C, D), bf16), V((C, D), bf16), V((2, 2) + gb.shape[3:], bf16),
                  V((2, D // 4, D), bf16), V((2, R, D), bf16), SD, SD((2,)), SD((2,)))


def forward_kernel(tok, cot, wq, small, fa, fb, fc, heads, hd):
    n_it, R, D = tok.shape
    FF = fa.shape[1]
    W = heads * hd
    N = 8 * R
    C = 2 * R
    S = pltpu.SemaphoreType.DMA
    V = pltpu.VMEM
    vm = pl.BlockSpec(memory_space=pltpu.VMEM)
    hbm = pl.BlockSpec(memory_space=pl.ANY)
    sd = jax.ShapeDtypeStruct
    full = lambda a: sd((2, 2, 4, 2) + a.shape, bf16)
    return pl.pallas_call(
        functools.partial(fwd_kernel, hd, heads),
        in_specs=[hbm] * 7,
        out_specs=[hbm] * 3 + [vm, hbm, vm] + [hbm] * 9 + [vm] + [hbm] * 3,
        out_shape=[
            sd((8, R, D), bf16), sd((3 * W, N), bf16), sd((W, N), f32), sd((heads, N), f32), sd((2, R, D), bf16), sd((16, D), f32),
            sd((3 * W, D), bf16), sd((2, 4) + fa.shape, bf16), sd((2, 4) + fa.shape, bf16), sd((4, 2) + fb.shape, bf16),
            sd((4, 2) + fb.shape, bf16), sd((2, D // 4, D), bf16), sd((4, W, C), bf16),
            sd((2, R, D), f32), sd((2, R, D), bf16), sd((16, D), f32), full(fa), full(fb), full(fc),
        ],
        scratch_shapes=[
            V((3 * W, N), bf16), V((W, N), f32), V((3 * W, D), bf16), V((2, R, D), bf16), V((4, W, C), bf16), V((2, R, D), f32),
            V((8, R, D), bf16), V((8, 4, 32, 3 * W + 128), bf16), V((8, FF), f32), V((4, W, C), bf16), V((2, R, D), bf16),
            V((2, 4, 2, R // 8, 2 * C), bf16), V((C, D), bf16), V((2, D // 4, D), bf16),
            S((2,)), S((2,)), S, S((2,)), S((2,)), S((2,)), S((2,)), S((2,)), S((2,)),
            S((3, 4)), S((3, 4)), S((4,)), S((6,)), S((6,)), S((7,)), S((7,)), S((3,)), S((3,)), S, S,
            S((2,)), S((2,)), S, S((3,)), S((3,)), S((3, 6)), S((3, 6)), S((3, 7)), S((3, 7)), S((3, 7)), S((3, 7)), S((3, 7)), S((3, 7)),
            S((8,)), S((8,)), S((8,)), S((8,)), S((2,)), S((2,)), S((8, 2)), S((2,)), S,
            S((8, 2)), S((8, 2)), S((2,)), S((2,)), S((2,)), S((2,)), S, S((6,)),
        ],
        compiler_params=pltpu.CompilerParams(collective_id=0, has_side_effects=True, vmem_limit_bytes=60 << 20),
        name="forward",
    )(tok, cot, wq, small, fa, fb, fc)


def put_sum(dst, pieces):
    total = pieces[0].astype(f32)
    for p in pieces[1:]:
        total = total + p.astype(f32)
    dst[...] = total.astype(dst.dtype)


def tail_kernel(hd, heads, dob, qkv_in, o_in, lse, a1, h1, a2, h2, a3, normed, wT, own, rows, mgrad, sums0,
                o1, o2, o3, gq, hm, sums,
                qkvT, oT, do_s, dq_s, k1, r11, r12, r13, k2, r21, r22, r23, k3, r31, r32, r33,
                nm, w_s, Gb, gx, gz, go, ds_s, dr_c, dy_s, dr_y, ig, vs, vr,
                sd, rd, ld, s1, q1, s2, q2, s3, q3, lk, sg, qg, sgz, qgz, sga, qga, sdc, qdc, sdy, qdy, sh, qh, lh, sv, qv, ll, lnm, lqo):
    x, c, z, y = place()
    hg = c * 2 + y
    W = heads * hd
    N = qkv_in.shape[1]
    zoff = [lax.rem(z + k, 4) for k in (1, 2, 3)]
    sib, yp, diag, xp = dev(x, 1 - c, z, y), dev(x, c, z, 1 - y), dev(x, 1 - c, z, 1 - y), dev(1 - x, c, z, y)
    zp = [dev(x, c, zz, y) for zz in zoff]
    ins = [pltpu.make_async_copy(a, b, lqo.at[i]) for i, (a, b) in enumerate(((qkv_in, qkvT), (o_in, oT)))]
    for cp in ins:
        cp.start()
    greet(zp + [dev(x, 1 - c, zz, y) for zz in zoff] + [sib, yp, diag, xp])
    peers = ((sib, (1 - c) * 2 + y), (yp, c * 2 + 1 - y), (diag, (1 - c) * 2 + 1 - y))
    for k, (d, g) in enumerate(peers):
        rcopy(dob.at[g], do_s.at[hg], sd.at[k], rd.at[k], d).start()
    loc = pltpu.make_async_copy(dob.at[hg], do_s.at[hg], ld)
    loc.start()

    def part(ref, h, n):
        return ref if n is None else ref.at[..., pl.ds(h * n, n), :]
    n1, n2 = k1.shape[2] // 2, k2.shape[2] // 2

    class Piece:
        def __init__(self, i, h, n, a, first, k, r1, r2, r3, out, s, q, lsem, yfirst):
            self.h = None if first is None else part(first, h, n)
            self.a, self.k, self.r1, self.r2, self.r3, self.out = [part(v, h, n) for v in (a, k, r1, r2, r3, out)]
            self.s, self.q, self.lsem, self.yfirst, self.b = s, q, lsem, yfirst, h * 5
            self.i = i
        def copies(self):
            b, s, q = self.b, self.s, self.q
            if self.yfirst:
                second = rcopy(self.k.at[1 - x], self.r2, s.at[b + 1], q.at[b + 1], xp)
                mine = lambda zz: self.k.at[x, zz]
            else:
                second = rcopy(self.k.at[:, 1 - y], self.r2, s.at[b + 1], q.at[b + 1], yp)
                mine = lambda zz: self.k.at[zz, y]
            if self.h is None:
                first = rcopy(self.a.at[1 - x], self.r1, s.at[b], q.at[b], xp)
                kept = self.a.at[x]
            else:
                first = pltpu.make_async_copy(self.h, self.r1, s.at[b])
                kept = self.a
            zs = [rcopy(mine(zoff[j]), self.r3.at[j], s.at[b + 2 + j], q.at[b + 2 + j], zp[j]) for j in range(3)]
            return first, second, zs, pltpu.make_async_copy(kept, self.k, self.lsem.at[self.i]), mine
        def start(self):
            first, _, _, keep, _ = self.copies()
            keep.start()
            first.start()
        def second(self):
            first, second, _, keep, _ = self.copies()
            keep.wait()
            first.wait()
            n0, n1_ = self.k.shape[0], self.k.shape[1]
            def add(j, carry):
                p, q_ = lax.div(j, n1_), lax.rem(j, n1_)
                self.k[p, q_] = self.k[p, q_] + self.r1[p, q_]
                return carry
            lax.fori_loop(0, n0 * n1_, add, 0)
            second.start()
        def third(self):
            _, second, zs, _, mine = self.copies()
            second.wait()
            def add(zz, carry):
                mine(zz)[...] = mine(zz)[...] + self.r2[zz]
                return carry
            lax.fori_loop(0, 4, add, 0)
            for cp in zs:
                cp.start()
        def finish(self):
            _, _, zs, _, mine = self.copies()
            for cp in zs:
                cp.wait()
            put_sum(self.out, [mine(z)[...]] + [self.r3[j] for j in range(3)])

    f1 = [Piece(h, h, n1, a1, h1, k1, r11, r12, r13, o1, s1, q1, lk, True) for h in range(2)]
    f2 = [Piece(2 + h, h, n2, a2, h2, k2, r21, r22, r23, o2, s2, q2, lk, False) for h in range(2)]
    f3 = Piece(4, 0, None, a3, None, k3, r31, r32, r33, o3, s3, q3, lk, False)
    for piece in (f2[0], f1[0], f2[1], f1[1], f3):
        piece.start()

    QB, KB = N // 4, 512
    cs = LOG2E * hd ** -0.5
    sc = hd ** -0.5
    nk = N // KB

    ld_n = pltpu.make_async_copy(normed, nm, lnm.at[0])
    ld_w = pltpu.make_async_copy(wT, w_s, lnm.at[1])
    ld_n.start()
    ld_w.start()

    def G_first(pr):
        rows_ = [dq_s[q * W + pr * 2 * hd:q * W + (pr + 1) * 2 * hd, :] for q in range(3)]
        g = dot_nn(jnp.concatenate(rows_, axis=0), nm[...].reshape(N, nm.shape[2])).astype(bf16).T
        Gb[pr] = g.reshape(Gb.shape[1:])
        G_x(pr).start()
    def G_x(pr):
        return rcopy(Gb.at[pr, 1 - x], gx.at[pr], sg.at[pr], qg.at[pr], xp)
    def G_z(pr):
        return [rcopy(Gb.at[pr, x, :, zoff[j]], gz.at[pr, j], sgz.at[pr, j], qgz.at[pr, j], zp[j]) for j in range(3)]
    def G_second(pr):
        G_x(pr).wait()
        def add(i, carry):
            cc, zz = lax.div(i, 4), lax.rem(i, 4)
            Gb[pr, x, cc, zz] = Gb[pr, x, cc, zz] + gx[pr, cc, zz]
            return carry
        lax.fori_loop(0, 8, add, 0)
        for cp in G_z(pr):
            cp.start()
    def G_own(pr):
        cps = [rcopy(Gb.at[pr, x, cc, z, yy], go.at[pr, hg], sga.at[pr, k], qga.at[pr, k], d)
               for k, (d, cc, yy) in enumerate(((sib, 1 - c, y), (yp, c, 1 - y), (diag, 1 - c, 1 - y)))]
        return cps, pltpu.make_async_copy(Gb.at[pr, x, c, z, y], go.at[pr, hg], ll.at[pr])
    def G_third(pr):
        for cp in G_z(pr):
            cp.wait()
        def add(i, carry):
            cc, yy = lax.div(i, 2), lax.rem(i, 2)
            put_sum(Gb.at[pr, x, cc, z, yy], [Gb[pr, x, cc, z, yy]] + [gz[pr, k, cc, yy] for k in range(3)])
            return carry
        lax.fori_loop(0, 4, add, 0)
        cps, own_ = G_own(pr)
        for cp in cps:
            cp.start()
        own_.start()
    def G_done(pr):
        cps, own_ = G_own(pr)
        own_.wait()
        for cp in cps:
            cp.wait()
        D_ = gq.shape[1] // 3
        for g in range(4):
            for q in range(3):
                at = q * D_ + g * W + pr * 2 * hd
                gq[:, at:at + 2 * hd] = go[pr, g, :, q * 2 * hd:(q + 1) * 2 * hd].astype(f32)

    PLAN = {
        1: ((Piece.second, f1[1]),),
        2: ((Piece.second, f2[0]),),
        5: ((Piece.second, f2[1]), (Piece.third, f1[1]),),
        6: ((Piece.second, f1[0]),),
        7: ((Piece.third, f2[0]),),
        8: ((Piece.second, f3),),
        11: ((Piece.third, f2[1]), (Piece.third, f3),),
        13: ((G_second, 0),),
        15: ((Piece.third, f1[0]),),
        17: ((G_second, 1),),
        19: ((G_third, 0),),
        21: ((G_third, 1), (G_done, 0),),
        22: ((Piece.finish, f2[0]),),
        24: ((Piece.finish, f3), (G_done, 1),),
        25: ((Piece.finish, f1[0]), (Piece.finish, f1[1]), (Piece.finish, f2[1]),),
    }

    def slot(i):
        for f, a in PLAN.get(i, ()):
            f(a)

    def attention(k_s, v_s, dk_s, dv_s):
        loc.wait()
        for cp in ins:
            cp.wait()
        def head(h, carry):
            hr = pl.ds(h * hd, hd)
            @pl.when(h == 2)
            def _():
                ld_n.wait()
                G_first(0)
            k_s[...] = qkvT[pl.ds(W + h * hd, hd), :].T
            v_s[...] = qkvT[pl.ds(2 * W + h * hd, hd), :].T
            dk_s[...] = jnp.zeros_like(dk_s)
            dv_s[...] = jnp.zeros_like(dv_s)
            def group(k, carry):
                step = h * 4 + k
                @pl.when((step > 0) & (step < 4))
                def _():
                    rcopy(dob.at[0], do_s.at[0], sd.at[k - 1], rd.at[k - 1], sib).wait()
                for i in range(16):
                    if i in PLAN:
                        @pl.when(step == i)
                        def _():
                            slot(i)
                cc = jnp.where((k == 1) | (k == 3), 1 - c, c)
                yy = jnp.where(k >= 2, 1 - y, y)
                g = cc * 2 + yy
                qcols = pl.ds(g * QB, QB)
                qt = qkvT[hr, qcols]
                dt = do_s[g, hr, :]
                delta = jnp.sum(dt.astype(f32) * oT[hr, qcols], axis=0, keepdims=True)
                ls = lse[pl.ds(h, 1), qcols]
                def first(i):
                    ks = slice(i * KB, (i + 1) * KB)
                    return dot_nn(k_s[ks, :], qt), dot_nn(v_s[ks, :], dt)
                dq = None
                cur = first(0)
                for i in range(nk):
                    nxt = first(i + 1) if i + 1 < nk else None
                    s, dp = cur
                    ks = slice(i * KB, (i + 1) * KB)
                    p = jnp.exp2(s * cs - ls)
                    ds = (p * (dp - delta)).astype(bf16)
                    prt = dot_nn(qkvT[pl.ds(W + h * hd, hd), ks], ds)
                    dq = prt if dq is None else dq + prt
                    dk_s[:, ks] += dot_nt(qt, ds)
                    dv_s[:, ks] += dot_nt(dt, p.astype(bf16))
                    cur = nxt
                dq_s[hr, qcols] = (dq * sc).astype(bf16)
                return carry
            lax.fori_loop(0, 4, group, 0)
            dq_s[pl.ds(W + h * hd, hd), :] = (dk_s[...] * sc).astype(bf16)
            dq_s[pl.ds(2 * W + h * hd, hd), :] = dv_s[...].astype(bf16)
            return carry
        lax.fori_loop(0, heads, head, 0)

    pl.run_scoped(attention, pltpu.VMEM((N, hd), bf16), pltpu.VMEM((N, hd), bf16),
                  pltpu.VMEM((hd, N), f32), pltpu.VMEM((hd, N), f32))

    def after(tok_s, mg_s, dn, lsem):
        R = tok_s.shape[1]
        B = R // 2
        loads = [pltpu.make_async_copy(a, b, lsem.at[i]) for i, (a, b) in enumerate(((own, tok_s), (mgrad, mg_s)))]
        for cp in loads:
            cp.start()
        ld_w.wait()
        def proj(g, b):
            return dot_nn(dq_s[:, pl.ds(pl.multiple_of(g * QB + b * B, B), B)].T, w_s[...])
        g_sy, g_s, g_oy = (1 - c) * 2 + 1 - y, (1 - c) * 2 + y, c * 2 + 1 - y
        def rows_of(b):
            return b // 2, pl.ds((b % 2) * B, B)
        def to_sib(a, b):
            j, rw = rows_of(b)
            return rcopy(ds_s.at[a, j, rw], dr_c.at[a, j, rw], sdc.at[a * 4 + b], qdc.at[a * 4 + b], sib)
        def to_y(b):
            j, rw = rows_of(b)
            return rcopy(dy_s.at[j, rw], dr_y.at[j, rw], sdy.at[b], qdy.at[b], yp)
        for b in range(4):
            j, rw = rows_of(b)
            ds_s[0, j, rw, :] = proj(g_sy, b).astype(bf16)
            to_sib(0, b).start()
        for b in range(4):
            j, rw = rows_of(b)
            mine = proj(g_oy, b)
            to_sib(0, b).wait()
            dy_s[j, rw, :] = (mine + dr_c[0, j, rw, :].astype(f32)).astype(bf16)
            to_y(b).start()
        slot(16)
        G_first(1)
        for b in range(4):
            j, rw = rows_of(b)
            ds_s[1, j, rw, :] = proj(g_s, b).astype(bf16)
            to_sib(1, b).start()
        for b in range(4):
            j, rw = rows_of(b)
            dn[j, rw, :] = proj(hg, b)
        ones = jnp.ones((8, N), bf16)
        vs[...] = sums0[...]
        for row, q in ((12, 0), (13, 2)):
            tot = dot_nt(ones, dq_s[q * W:(q + 1) * W, :])
            vs[row:row + 1, :] = jnp.zeros((1, vs.shape[1]), f32)
            vs[row:row + 1, pl.ds(pl.multiple_of(hg * W, W), W)] = tot[0:1]
        slot(17)
        gain = rows[2:3, :]
        shift = rows[15:16, :]
        acc = [jnp.zeros((1, dn.shape[2]), f32) for _ in range(3)]
        for cp in loads:
            cp.wait()
        def home_copy(b):
            j, rw = rows_of(b)
            i = lax.rem(z, 2)
            zt = 2 * c + j
            return zt, rcopy(ig.at[j, rw], hm.at[i, rw], sh.at[b], qh.at[i, b % 2], dev(x, lax.div(z, 2), zt, y)), \
                pltpu.make_async_copy(ig.at[j, rw], hm.at[i, rw], lh.at[b % 2])
        for b in range(4):
            j, rw = rows_of(b)
            to_sib(1, b).wait()
            to_y(b).wait()
            u = dn[j, rw, :] + dr_c[1, j, rw, :].astype(f32) + dr_y[j, rw, :].astype(f32)
            v = tok_s[j, rw, :].astype(f32) + shift
            cen = v - jnp.mean(v, axis=-1, keepdims=True)
            r = lax.rsqrt(jnp.mean(cen * cen, axis=-1, keepdims=True) + EPS)
            xh = cen * r
            e = u * gain
            res = mg_s[j, rw, :] + r * (e - jnp.mean(e, axis=-1, keepdims=True) - xh * jnp.mean(e * xh, axis=-1, keepdims=True))
            ig[j, rw, :] = res.astype(bf16)
            for n, val in enumerate((u * xh, u, res)):
                acc[n] = acc[n] + jnp.sum(val, axis=0, keepdims=True)
            zt, cp, lc = home_copy(b)
            @pl.when(zt != z)
            def _():
                cp.start()
            @pl.when(zt == z)
            def _():
                lc.start()
            slot(18 + b)
        vs[8:9, :] = acc[0]
        vs[9:10, :] = acc[1]
        vs[10:11, :] = acc[2] * rows[14:15, :]
        vs[11:12, :] = acc[2]
        for k, d in enumerate((sib, yp, xp)):
            cp = rcopy(vs, vr.at[k], sv.at[k], qv.at[k], d)
            cp.start()
            slot(22 + k)
            cp.wait()
            vs[...] = vs[...] + vr[k]
        zv = [rcopy(vs, vr.at[3 + k], sv.at[3 + k], qv.at[3 + k], zp[k]) for k in range(3)]
        for cp in zv:
            cp.start()
        slot(25)
        for i in range(2):
            src = 2 * c + i
            for hb in range(2):
                rw = pl.ds(hb * B, B)
                @pl.when(src != z)
                def _():
                    rcopy(ig.at[0, rw], hm.at[i, rw], sh.at[0], qh.at[i, hb], sib).wait_recv()
                @pl.when(src == z)
                def _():
                    pltpu.make_async_copy(ig.at[0, rw], hm.at[i, rw], lh.at[hb]).wait()
                pass
        for cp in zv:
            cp.wait()
        sums[...] = vs[...] + vr[3] + vr[4] + vr[5]
        slot(26)
        for b in range(4):
            zt, cp, lc = home_copy(b)
            @pl.when(zt != z)
            def _():
                cp.wait_send()

    R = own.shape[1]
    D = own.shape[2]
    pl.run_scoped(after, pltpu.VMEM((2, R, D), bf16), pltpu.VMEM((2, R, D), f32), pltpu.VMEM((2, R, D), f32), pltpu.SemaphoreType.DMA((2,)))


def backward_kernel(dob, qkvT, oT, lse, a1, h1, a2, h2, a3, normed, wT, own, rows, mgrad, sums0, heads, hd):
    W3, N = qkvT.shape
    W = heads * hd
    _, R, D = own.shape
    S = pltpu.SemaphoreType.DMA
    V = pltpu.VMEM
    vm = pl.BlockSpec(memory_space=pltpu.VMEM)
    hbm = pl.BlockSpec(memory_space=pl.ANY)
    b1, b2, b3 = a1.shape[2:], a2.shape[2:], a3.shape[3:]
    def bufs(b, yfirst):
        k = (2, 4) if yfirst else (4, 2)
        return [V(k + b, bf16), V(k + b, bf16), V((4,) + b, bf16), V((3,) + b, bf16)]
    rq = D // 32
    return pl.pallas_call(
        functools.partial(tail_kernel, hd, heads),
        in_specs=[hbm, hbm, hbm, vm, hbm, hbm, hbm, hbm, hbm, hbm, hbm, hbm, vm, hbm, vm],
        out_specs=[vm] * 4 + [hbm, vm],
        out_shape=[
            jax.ShapeDtypeStruct(b1, f32), jax.ShapeDtypeStruct(b2, f32), jax.ShapeDtypeStruct(b3, f32),
            jax.ShapeDtypeStruct((rq, 3 * D), f32), jax.ShapeDtypeStruct((2, R, D), bf16), jax.ShapeDtypeStruct((16, D), f32),
        ],
        scratch_shapes=[V((W3, N), bf16), V((W, N), f32), V((4, W, N // 4), bf16), V((W3, N), bf16)] + bufs(b1, True) + bufs(b2, False) + bufs(b3, False) + [
            V((8, R, D), bf16), V((W3, D), bf16),
            V((2, 2, 2, 4, 2, rq, W3 // 2), bf16), V((2, 2, 4, 2, rq, W3 // 2), bf16), V((2, 3, 2, 2, rq, W3 // 2), bf16), V((2, 4, rq, W3 // 2), bf16),
            V((2, 2, R, D), bf16), V((2, 2, R, D), bf16), V((2, R, D), bf16), V((2, R, D), bf16), V((2, R, D), bf16),
            V((16, D), f32), V((6, 16, D), f32),
            S((3,)), S((3,)), S, S((10,)), S((10,)), S((10,)), S((10,)), S((5,)), S((5,)), S((5,)),
            S((2,)), S((2,)), S((2, 3)), S((2, 3)), S((2, 3)), S((2, 3)), S((8,)), S((8,)), S((4,)), S((4,)),
            S((4,)), S((2, 2)), S((2,)), S((6,)), S((6,)), S((2,)), S((2,)), S((2,)),
        ],
        compiler_params=pltpu.CompilerParams(collective_id=1, has_side_effects=True, vmem_limit_bytes=60 << 20),
        name="backward",
    )(dob, qkvT, oT, lse, a1, h1, a2, h2, a3, normed, wT, own, rows, mgrad, sums0)


def result_kernel(rows, fc, o1, o2, o3, gq, hm, bo, sums, r1, r2, r3, rq, rh, rb, *rest):
    for a, b in ((o1, r1), (o2, r2), (o3, r3), (gq, rq), (bo, rb)):
        b[...] = a[...]
    rh[...] = hm[...].astype(f32)
    x, c, z, y = place()
    index = (x * 2 + c) * 8 + z * 2 + y
    per = 128 // rows
    block = sums[:, pl.ds(pl.multiple_of(lax.div(index, per) * 128, 128), 128)]
    mine = pltpu.roll(block, lax.rem(per - lax.rem(index, per), per) * rows, 1)
    for ref, row in zip(rest, (8, 9, 12, 13, 0, 1, 2, None, 3, 10, 11)):
        if row is None:
            per_row = sums.shape[1] // fc
            at = pl.ds(pl.multiple_of(lax.rem(index, per_row) * fc, fc), fc)
            part = sums[0:8, at]
            val = part[4:5]
            for i in range(1, 4):
                val = jnp.where(lax.div(index, per_row) == i, part[4 + i:5 + i], val)
            ref[...] = val
        else:
            ref[...] = mine[row:row + 1, 0:rows]


def results(o1, o2, o3, gq, hm, bo, sums, rows, fc):
    vm = pl.BlockSpec(memory_space=pltpu.VMEM)
    sd = jax.ShapeDtypeStruct
    widths = [rows] * 7 + [fc] + [rows] * 3
    return pl.pallas_call(
        functools.partial(result_kernel, rows, fc),
        in_specs=[vm] * 7,
        out_specs=[vm] * 17,
        out_shape=[sd(a.shape, f32) for a in (o1, o2, o3, gq, hm)] + [sd(bo.shape, bf16)] + [sd((1, w), f32) for w in widths],
        compiler_params=pltpu.CompilerParams(vmem_limit_bytes=60 << 20),
        name="results",
    )(o1, o2, o3, gq, hm, bo, sums)


HEADS = 16


epsilon = EPS


def norm_rows_s(values, gain, shift):
    center = values - jnp.mean(values, axis=-1, keepdims=True)
    spread = jnp.mean(center * center, axis=-1, keepdims=True)
    return center * lax.rsqrt(spread + epsilon) * gain + shift


def gelu_exact_s(values):
    return jax.nn.gelu(values, approximate=False)


def product(left, right):
    return jnp.dot(left, right, preferred_element_type=jnp.float32)


def product_tleft(left, right):
    return lax.dot_general(
        left, right, (((0,), (0,)), ((), ())), preferred_element_type=jnp.float32
    )


def product_tright(left, right):
    return lax.dot_general(
        left, right, (((1,), (1,)), ((), ())), preferred_element_type=jnp.float32
    )


def split_heads(values):
    return values.reshape(values.shape[0], HEADS, values.shape[1] // HEADS)


def attend(operands):
    queries, keys_all, values_all = operands
    scale = (queries.shape[1] // HEADS) ** (-0.5)
    scores = (
        jnp.einsum(
            "qhd,khd->hqk",
            split_heads(queries),
            split_heads(keys_all),
            preferred_element_type=jnp.float32,
        )
        * scale
    )
    highest = jnp.max(scores, axis=-1, keepdims=True)
    exps = jnp.exp(scores - highest)
    totals = jnp.sum(exps, axis=-1, keepdims=True)
    probs_low = (exps / totals).astype(jnp.bfloat16)
    blended = jnp.einsum(
        "hqk,khd->qhd", probs_low, split_heads(values_all), preferred_element_type=jnp.float32
    ).reshape(queries.shape)
    return (blended, (highest + jnp.log(totals))[:, :, 0])


def recompute_probs(queries, keys_all, values_all, grads_in, log_totals):
    scale = (queries.shape[1] // HEADS) ** (-0.5)
    scores = (
        jnp.einsum(
            "qhd,khd->hqk",
            split_heads(queries),
            split_heads(keys_all),
            preferred_element_type=jnp.float32,
        )
        * scale
    )
    probs = jnp.exp(scores - log_totals[:, :, None])
    prob_grads = jnp.einsum(
        "qhd,khd->hqk",
        split_heads(grads_in),
        split_heads(values_all),
        preferred_element_type=jnp.float32,
    )
    return (probs, prob_grads, scale)


def key_side_grads(score_grads, probs, queries, grads_in, row_count):
    key_grads = jnp.einsum(
        "hqk,qhd->khd", score_grads, split_heads(queries), preferred_element_type=jnp.float32
    )
    value_grads = jnp.einsum(
        "hqk,qhd->khd",
        probs.astype(jnp.bfloat16),
        split_heads(grads_in),
        preferred_element_type=jnp.float32,
    )
    width = queries.shape[1]
    return (key_grads.reshape(row_count, width), value_grads.reshape(row_count, width))


def query_side(with_keys, operands):
    queries, keys_all, values_all, grads_in, log_totals = operands
    probs, prob_grads, scale = recompute_probs(queries, keys_all, values_all, grads_in, log_totals)
    row_delta = jnp.sum(probs * prob_grads, axis=-1)
    score_grads = (probs * (prob_grads - row_delta[:, :, None]) * scale).astype(jnp.bfloat16)
    query_grads = jnp.einsum(
        "hqk,khd->qhd", score_grads, split_heads(keys_all), preferred_element_type=jnp.float32
    ).reshape(queries.shape)
    key_grads, value_grads = key_side_grads(
        score_grads, probs, queries, grads_in, keys_all.shape[0]
    )
    return (query_grads, row_delta, key_grads, value_grads)


def spread_on_device(
    tokens_in,
    lead_hours,
    cotangent,
    w_qkv,
    w_out,
    w_fc1,
    w_fc2,
    ln1_gain,
    ln1_bias,
    q_bias,
    v_bias,
    out_bias,
    ln2_gain,
    ln2_bias,
    fc1_bias,
    fc2_bias,
    lead_weight,
    lead_bias,
):
    gathered = (
        lax.all_gather(w_qkv, ("dp", "seq"), axis=0, tiled=True),
        lax.all_gather(w_out, ("dp", "seq"), axis=0, tiled=True),
        lax.all_gather(w_fc1, ("dp", "seq"), axis=0, tiled=True),
        lax.all_gather(w_fc2, ("dp", "seq"), axis=0, tiled=True),
        lax.all_gather(ln1_gain, ("dp", "seq"), axis=0, tiled=True),
        lax.all_gather(ln1_bias, ("dp", "seq"), axis=0, tiled=True),
        lax.all_gather(q_bias, ("dp", "seq"), axis=0, tiled=True),
        lax.all_gather(v_bias, ("dp", "seq"), axis=0, tiled=True),
        lax.all_gather(out_bias, ("dp", "seq"), axis=0, tiled=True),
        lax.all_gather(ln2_gain, ("dp", "seq"), axis=0, tiled=True),
        lax.all_gather(ln2_bias, ("dp", "seq"), axis=0, tiled=True),
        lax.all_gather(fc1_bias, ("dp", "seq"), axis=0, tiled=True),
        lax.all_gather(fc2_bias, ("dp", "seq"), axis=0, tiled=True),
        lax.all_gather(lead_weight, ("dp", "seq"), axis=0, tiled=True),
        lax.all_gather(lead_bias, ("dp", "seq"), axis=0, tiled=True),
    )
    (
        full_qkv,
        full_out,
        full_fc1,
        full_fc2,
        gain_one,
        shift_one,
        bias_query,
        bias_value,
        bias_out,
        gain_two,
        shift_two,
        bias_fc1,
        bias_fc2,
        lead_scale,
        lead_shift,
    ) = gathered
    items, rows, width = tokens_in.shape
    count = items * rows
    lead_times = lead_hours.astype(jnp.float32) / 100.0
    leading = (
        tokens_in.astype(jnp.float32)
        + lead_times[:, None, None] * lead_scale.astype(jnp.float32)
        + lead_shift.astype(jnp.float32)
    ).reshape(count, width)
    normed, norm_one_back = jax.vjp(
        norm_rows_s, leading, gain_one.astype(jnp.float32), shift_one.astype(jnp.float32)
    )
    normed_low = normed.astype(jnp.bfloat16)
    projected = product(normed_low, full_qkv)
    queries = (projected[:, :width] + bias_query.astype(jnp.float32)).astype(jnp.bfloat16)
    keys_own = projected[:, width : 2 * width].astype(jnp.bfloat16)
    values_own = (projected[:, 2 * width :] + bias_value.astype(jnp.float32)).astype(jnp.bfloat16)
    queries3 = queries.reshape(items, rows, width)
    keys_all, values_all = (
        lax.all_gather(keys_own.reshape(items, rows, width), "seq", axis=1, tiled=True),
        lax.all_gather(values_own.reshape(items, rows, width), "seq", axis=1, tiled=True),
    )
    blended, log_totals = lax.map(attend, (queries3, keys_all, values_all))
    blended_low = blended.reshape(count, width).astype(jnp.bfloat16)
    middle = leading + product(blended_low, full_out) + bias_out.astype(jnp.float32)
    normed_two, norm_two_back = jax.vjp(
        norm_rows_s, middle, gain_two.astype(jnp.float32), shift_two.astype(jnp.float32)
    )
    normed_two_low = normed_two.astype(jnp.bfloat16)
    hidden = product(normed_two_low, full_fc1) + bias_fc1.astype(jnp.float32)
    activated, gelu_back = jax.vjp(gelu_exact_s, hidden)
    activated_low = activated.astype(jnp.bfloat16)
    output = middle + product(activated_low, full_fc2) + bias_fc2.astype(jnp.float32)
    block_output = output.reshape(items, rows, width).astype(jnp.bfloat16)
    back_qkv, back_out, back_fc1, back_fc2 = (
        lax.all_gather(w_qkv, ("dp", "seq"), axis=0, tiled=True),
        lax.all_gather(w_out, ("dp", "seq"), axis=0, tiled=True),
        lax.all_gather(w_fc1, ("dp", "seq"), axis=0, tiled=True),
        lax.all_gather(w_fc2, ("dp", "seq"), axis=0, tiled=True),
    )
    out_grad = cotangent.reshape(count, width)
    upstream = out_grad.astype(jnp.float32)
    grad_fc2 = product_tleft(activated_low, out_grad)
    grad_fc2_bias = jnp.sum(upstream, axis=0)
    hidden_grad = gelu_back(product_tright(out_grad, back_fc2))[0].astype(jnp.bfloat16)
    grad_fc1 = product_tleft(normed_two_low, hidden_grad)
    grad_fc1_bias = jnp.sum(hidden_grad.astype(jnp.float32), axis=0)
    middle_part, grad_ln2_gain, grad_ln2_bias = norm_two_back(product_tright(hidden_grad, back_fc1))
    middle_grad = upstream + middle_part
    attn_grad = middle_grad.astype(jnp.bfloat16)
    grad_out = product_tleft(blended_low, attn_grad)
    grad_out_bias = jnp.sum(attn_grad.astype(jnp.float32), axis=0)
    blended_grad = (
        product_tright(attn_grad, back_out).astype(jnp.bfloat16).reshape(items, rows, width)
    )
    query_grads, row_delta, key_parts, value_parts = lax.map(
        partial(query_side, True), (queries3, keys_all, values_all, blended_grad, log_totals)
    )
    key_grads, value_grads = (
        lax.psum_scatter(
            key_parts.astype(jnp.bfloat16), "seq", scatter_dimension=1, tiled=True
        ).astype(jnp.float32),
        lax.psum_scatter(
            value_parts.astype(jnp.bfloat16), "seq", scatter_dimension=1, tiled=True
        ).astype(jnp.float32),
    )
    query_low = query_grads.reshape(count, width).astype(jnp.bfloat16)
    key_low = key_grads.reshape(count, width).astype(jnp.bfloat16)
    value_low = value_grads.reshape(count, width).astype(jnp.bfloat16)
    qkv_grad = jnp.concatenate([query_low, key_low, value_low], axis=1)
    grad_qkv = product_tleft(normed_low, qkv_grad)
    grad_q_bias = jnp.sum(query_low.astype(jnp.float32), axis=0)
    grad_v_bias = jnp.sum(value_low.astype(jnp.float32), axis=0)
    leading_part, grad_ln1_gain, grad_ln1_bias = norm_one_back(product_tright(qkv_grad, back_qkv))
    input_grad = (middle_grad + leading_part).reshape(items, rows, width)
    grad_lead_weight = jnp.sum(jnp.sum(input_grad, axis=1) * lead_times[:, None], axis=0)
    grad_lead_bias = jnp.sum(input_grad, axis=(0, 1))
    summed = (
        lax.psum_scatter(grad_qkv, ("dp", "seq"), scatter_dimension=0, tiled=True),
        lax.psum_scatter(grad_out, ("dp", "seq"), scatter_dimension=0, tiled=True),
        lax.psum_scatter(grad_fc1, ("dp", "seq"), scatter_dimension=0, tiled=True),
        lax.psum_scatter(grad_fc2, ("dp", "seq"), scatter_dimension=0, tiled=True),
        lax.psum_scatter(grad_ln1_gain, ("dp", "seq"), scatter_dimension=0, tiled=True),
        lax.psum_scatter(grad_ln1_bias, ("dp", "seq"), scatter_dimension=0, tiled=True),
        lax.psum_scatter(grad_q_bias, ("dp", "seq"), scatter_dimension=0, tiled=True),
        lax.psum_scatter(grad_v_bias, ("dp", "seq"), scatter_dimension=0, tiled=True),
        lax.psum_scatter(grad_out_bias, ("dp", "seq"), scatter_dimension=0, tiled=True),
        lax.psum_scatter(grad_ln2_gain, ("dp", "seq"), scatter_dimension=0, tiled=True),
        lax.psum_scatter(grad_ln2_bias, ("dp", "seq"), scatter_dimension=0, tiled=True),
        lax.psum_scatter(grad_fc1_bias, ("dp", "seq"), scatter_dimension=0, tiled=True),
        lax.psum_scatter(grad_fc2_bias, ("dp", "seq"), scatter_dimension=0, tiled=True),
        lax.psum_scatter(grad_lead_weight, ("dp", "seq"), scatter_dimension=0, tiled=True),
        lax.psum_scatter(grad_lead_bias, ("dp", "seq"), scatter_dimension=0, tiled=True),
    )
    return (block_output, input_grad) + tuple(summed)


def on_device(mesh_shape, tokens_in, lead_hours, cotangent, w_qkv, w_out, w_fc1, w_fc2, ln1_gain, ln1_bias, q_bias, v_bias,
              out_bias, ln2_gain, ln2_bias, fc1_bias, fc2_bias, lead_weight, lead_bias):
    _, R, D = tokens_in.shape
    FF = w_fc1.shape[1]
    hd = D // HEADS
    heads = HEADS // 4
    W = heads * hd
    rows = w_qkv.shape[0]
    vectors = (lead_weight, lead_bias, ln1_gain, ln1_bias, q_bias, v_bias, out_bias, ln2_gain, ln2_bias, fc2_bias, fc1_bias,
               lead_hours.astype(bf16))
    small = sum(lax.pad(v[None].astype(f32), f32(0), ((k, 31 - k, 0), (0, 128 - v.shape[0], 0))) for k, v in enumerate(vectors)).astype(bf16)
    normed, qkvT, oT, lse, own, vec, wT, a1, h1, a2, h2, a3, dob, mgrad, block_output, sums0 = forward_kernel(
        tokens_in, cotangent, w_qkv, small, w_fc1, w_fc2, w_out, heads, hd)[:16]
    o1, o2, o3, gq, hm, sums = backward_kernel(
        dob, qkvT, oT, lse, a1, h1, a2, h2, a3.reshape(2, 4, 2, rows, D), normed, wT,
        own, vec, mgrad, sums0, heads, hd)
    grad_fc1, grad_fc2, grad_out, grad_qkv, home, block_output, *small = results(
        o1, o2, o3, gq, hm, block_output, sums, rows, fc1_bias.shape[0])
    return (block_output, home, grad_qkv, grad_out, grad_fc1, grad_fc2) + tuple(v.reshape(-1) for v in small)


def choose(mesh_shape, *args):
    items, rows = args[0].shape[0], args[3].shape[0]
    planes = mesh_shape["seq"] // 2
    if items == 2 and planes == 2 * items and mesh_shape["dp"] == 4 and rows % 16 == 0 and 4 * args[0].shape[1] == args[0].shape[2]:
        return on_device(mesh_shape, *args)
    return spread_on_device(*args)


def solution(mesh):
    big, rows, vec = P("dp", "seq", None), P(("dp", "seq"), None), P(("dp", "seq"))
    in_specs = (big, P("dp"), big) + (rows,) * 4 + (vec,) * 11
    out_specs = (big, big) + (rows,) * 4 + (vec,) * 11
    body = functools.partial(choose, dict(mesh.shape))
    return jax.shard_map(body, mesh=mesh, in_specs=in_specs, out_specs=out_specs, check_vma=False)
```

```python
import functools
from functools import partial
import jax, jax.numpy as jnp
from jax import lax
from jax.experimental import pallas as pl
from jax.experimental.pallas import tpu as pltpu
from jax.sharding import PartitionSpec as P

MESH = pl.DeviceIdType.MESH
f32, bf16 = jnp.float32, jnp.bfloat16
LOG2E = 1.4426950408889634
EPS = 1e-06


def dot_nn(a, b):
    return lax.dot_general(a, b, (((1,), (0,)), ((), ())), preferred_element_type=f32)


def dot_nt(a, b):
    return lax.dot_general(a, b, (((1,), (1,)), ((), ())), preferred_element_type=f32)


def rcopy(src, dst, ssem, rsem, dev):
    return pltpu.make_async_remote_copy(src_ref=src, dst_ref=dst, send_sem=ssem, recv_sem=rsem, device_id=dev, device_id_type=MESH)


def place():
    dp, seq = lax.axis_index("dp"), lax.axis_index("seq")
    return lax.div(dp, 2), lax.rem(dp, 2), lax.div(seq, 2), lax.rem(seq, 2)


def dev(x, c, z, y):
    return (x * 2 + c, z * 2 + y)


def greet(partners):
    bar = pltpu.get_barrier_semaphore()
    for p in partners:
        pl.semaphore_signal(bar, inc=1, device_id=p, device_id_type=MESH)
    pl.semaphore_wait(bar, len(partners))


def fwd_kernel(hd, heads, tok, cot, wq, small, fa, fb, fc, normed, qkv_out, o_out, lse, own_out, vec, w_out_, a1, h1, a2, h2, a3, dob_out, mg_out, bo, bout_b, sums,
               ga, gb, gc, qkvT, oT, wT, own, dob, mgrad, T, Ws, fb1, bt, up, r1, r2, r3, st, rt, lt, sy, ry, sc, rc, scy, rcy, sa, ra, la, sz, rz, sx, rx, so, ro, lo,
               ln, su, ru, lu, gss, grs, gsz, grz, gs1, gr1, gs2, gr2, gsc, grc, sf1, rf1, sf2, rf2, sf3, rf3, la1, la2, la3,
               sh1, qh1, sh2, qh2, sbo, qbo, lbo, lq):
    x, c, z, y = place()
    hg = c * 2 + y
    W = heads * hd
    D = T.shape[2]
    R = T.shape[1]
    N = qkvT.shape[1]
    zoff = [lax.rem(z + k, 4) for k in (1, 2, 3)]
    sums[...] = jnp.zeros_like(sums)
    greet([dev(x, c, zz, y) for zz in zoff] + [dev(x, 1 - c, zz, y) for zz in zoff]
          + [dev(x, 1 - c, z, y), dev(x, c, z, 1 - y), dev(x, 1 - c, z, 1 - y), dev(1 - x, c, z, y)])
    sib, yp, diag, xp = dev(x, 1 - c, z, y), dev(x, c, z, 1 - y), dev(x, 1 - c, z, 1 - y), dev(1 - x, c, z, y)
    pos = (lax.div(z, 2) * 2 + y) * 2 + lax.rem(z, 2)
    tcp = []
    for i in range(2):
        zt = 2 * c + i
        cp = rcopy(tok.at[i], T.at[pos], st.at[i], rt.at[lax.rem(z, 2)], dev(x, lax.div(z, 2), zt, y))
        loc = pltpu.make_async_copy(tok.at[i], T.at[pos], lt)
        @pl.when(zt != z)
        def _():
            cp.start()
        @pl.when(zt == z)
        def _():
            loc.start()
        tcp.append((zt, cp, loc))
    xz = x * 4 + z
    def slices(g):
        dst = Ws.at[xz, hg]
        out = [(wq.at[:, pl.ds(pl.multiple_of(q * D + g * W, W), W)], dst.at[:, q * W:(q + 1) * W]) for q in range(3)]
        return out + [(small, dst.at[:, 3 * W:3 * W + 128])]
    wa = [pltpu.make_async_copy(a, b, la.at[n]) for n, (a, b) in enumerate(slices(hg))]
    for k, (d, g) in enumerate(((yp, c * 2 + 1 - y), (sib, (1 - c) * 2 + y), (diag, (1 - c) * 2 + 1 - y))):
        wa += [rcopy(a, b, sa.at[k, n], ra.at[k, n], d) for n, (a, b) in enumerate(slices(g))]
    for cp in wa:
        cp.start()
    for cp in wa:
        cp.wait()
    def zz_of(u):
        return z if u == 0 else (z - u if u <= 3 else z + (u - 3))

    def ok(u):
        return True if u == 0 else (z >= u if u <= 3 else z + (u - 3) <= 3)

    def guard(cond, f):
        if cond is True:
            f()
        else:
            pl.when(cond)(f)

    def w_z(u, down):
        v = Ws.at[x * 4 + zz_of(u)]
        k = (u if u <= 3 else u - 3) + (3 if down else 0)
        return rcopy(v, v, sz.at[k], rz.at[k], dev(x, c, z - 1 if down else z + 1, y))

    def w_arr(u):
        v = Ws.at[x * 4 + zz_of(u)]
        return rcopy(v, v, sz.at[u - 1], rz.at[u - 1], sib)

    def w_x(u):
        v = Ws.at[x * 4 + zz_of(u)]
        return rcopy(v, v, sx.at[u], rx.at[u], xp)

    def w_recv(d):
        for u in (d, d + 3):
            def go(u=u):
                w_arr(u).wait_recv()
                if d < 3:
                    guard((z > 0) if u > 3 else (z < 3), lambda: w_z(u, u > 3).start())
                w_x(u).start()
            guard(ok(u), go)

    guard(z < 3, lambda: w_z(0, False).start())
    guard(z > 0, lambda: w_z(0, True).start())
    w_x(0).start()
    ca = 1 - c
    gat = ((fa, ga, False), (fb, gb, True), (fc, gc, False))
    before_z = (False, True, True)
    known = set()

    def g_start(p):
        f, g, _ = gat[p]
        return rcopy(f, g.at[x, c, z, y], gss.at[p], grs.at[p], sib)

    def z_block(p, u):
        g, xfirst = gat[p][1:]
        if not before_z[p]:
            return g.at[x, ca, zz_of(u), y]
        return g.at[:, ca, zz_of(u), y] if xfirst else g.at[x, ca, zz_of(u)]

    def g_z(p, u, down):
        v = z_block(p, u)
        d = u if u <= 3 else u - 3
        k = d + (3 if down else 0)
        return rcopy(v, v, gsz.at[p, k], grz.at[p, k], dev(x, c, z - 1 if down else z + 1, y))

    def g_zarr(p, u):
        v = z_block(p, u)
        return rcopy(v, v, gsz.at[p, u - 1], grz.at[p, u - 1], sib)

    def g_one(p, u):
        g, xfirst = gat[p][1:]
        v = g.at[x, ca, zz_of(u), y]
        return rcopy(v, v, gs1.at[p, u], gr1.at[p, u], xp if xfirst else yp)

    def g_two(p, u):
        g, xfirst = gat[p][1:]
        v = g.at[:, ca, zz_of(u), y] if xfirst else g.at[x, ca, zz_of(u)]
        return rcopy(v, v, gs2.at[p, u], gr2.at[p, u], yp if xfirst else xp)

    def g_core(p, u):
        v = gat[p][1].at[:, ca, zz_of(u)]
        return rcopy(v, v, gsc.at[p, u], grc.at[p, u], sib)

    def ag_own(p):
        g_start(p).wait()
        g_one(p, 0).start()

    def one_own(p):
        if p not in known:
            known.add(p)
            g_one(p, 0).wait()

    def ag_z0(p, d):
        if before_z[p]:
            one_own(p)
        guard(z < 3, lambda: g_z(p, 0, False).start())
        guard(z > 0, lambda: g_z(p, 0, True).start())

    def ag_recv(p, d):
        for u in (d, d + 3):
            def go(u=u):
                g_zarr(p, u).wait_recv()
                if d < 3:
                    guard((z > 0) if u > 3 else (z < 3), lambda: g_z(p, u, u > 3).start())
                (g_two if before_z[p] else g_one)(p, u).start()
            guard(ok(u), go)

    def units(d):
        return (0,) if d == 0 else (d, d + 3)

    def ag_two(p, d):
        if before_z[p] and d > 0:
            return
        for u in units(d):
            def go(u=u):
                if u == 0:
                    one_own(p)
                else:
                    g_one(p, u).wait()
                g_two(p, u).start()
            guard(ok(u), go)

    def ag_core(p, d):
        for u in units(d):
            def go(u=u):
                g_two(p, u).wait()
                g_core(p, u).start()
            guard(ok(u), go)

    def ag_got(p, half):
        own_half = ((0, True), (1, lax.rem(z, 2) == 1), (4, lax.rem(z, 2) == 0))
        rest = ((1, z == 2), (2, z >= 2), (3, z == 3), (4, z == 1), (5, z <= 1), (6, z == 0))
        for u, cond in (own_half if half == 0 else rest):
            guard(cond, lambda: g_core(p, u).wait())

    def ag_sent(p):
        for u in (0, 1, 2):
            guard((z >= u) & (z < 3), lambda: g_z(p, u, False).wait_send())
            guard((z + u <= 3) & (z > 0), lambda: g_z(p, u + 3 if u else 0, True).wait_send())

    PLAN = {
        0: ((ag_two, 1, 0),),
        2: ((ag_z0, 1, 0), (ag_two, 0, 0),),
        3: ((ag_z0, 0, 0),),
        4: ((ag_two, 2, 0),),
        5: ((ag_recv, 0, 1),),
        7: ((ag_recv, 2, 1), (ag_recv, 1, 1),),
        10: ((ag_two, 1, 1),),
        11: ((ag_recv, 2, 2), (ag_recv, 0, 3),),
        12: ((ag_two, 2, 1),),
        13: ((ag_two, 0, 2),),
        14: ((ag_two, 2, 2),),
        15: ((ag_core, 0, 0),),
        17: ((ag_core, 2, 0),),
        18: ((ag_recv, 2, 3),),
        19: ((ag_two, 0, 3),),
        20: ((ag_recv, 1, 2),),
        22: ((ag_core, 0, 1), (ag_core, 0, 2),),
        23: ((ag_core, 2, 2), (ag_core, 1, 1),),
        24: ((ag_two, 2, 3), (ag_core, 2, 1), (ag_core, 2, 3),),
        25: ((ag_two, 1, 2), (ag_two, 1, 3), (ag_core, 0, 3), (ag_recv, 1, 3),),
        26: ((ag_core, 1, 2),),
        28: ((ag_core, 1, 3),),
        35: ((ag_z0, 2, 0), (ag_two, 0, 1),),
        36: ((ag_core, 1, 0), (ag_recv, 0, 2),),
    }

    COT = 14

    def ag_slot(i):
        for f, p, d in PLAN.get(i, ()):
            f(p, d)

    for p in (2, 0, 1):
        g_start(p).start()
    for p in (2, 0, 1):
        ag_own(p)
    ag_slot(0)
    w_recv(1)
    ag_slot(1)
    ycp, ccp, cycp = [], [], []
    j0 = jnp.where(lax.div(z, 2) == c, lax.rem(z, 2), 0)
    for j in (j0, 1 - j0):
        src_z = 2 * c + j
        p = hg * 2 + j
        @pl.when(src_z != z)
        def _():
            rcopy(tok.at[0], T.at[p], st.at[0], rt.at[j], sib).wait_recv()
        @pl.when(src_z == z)
        def _():
            pltpu.make_async_copy(tok.at[0], T.at[p], lt).wait()
        a = rcopy(T.at[p], T.at[p], sy.at[j], ry.at[j], yp)
        b = rcopy(T.at[p], T.at[p], sc.at[j], rc.at[j], sib)
        a.start()
        b.start()
        ycp.append(a)
        ccp.append(b)
    ag_slot(2)
    w_recv(2)
    ag_slot(3)
    w_recv(3)
    ag_slot(4)
    for n, j in enumerate((j0, 1 - j0)):
        ycp[n].wait()
        p = (c * 2 + 1 - y) * 2 + j
        cp = rcopy(T.at[p], T.at[p], scy.at[j], rcy.at[j], sib)
        cp.start()
        cycp.append(cp)
    ag_slot(5)
    for u in range(7):
        guard(ok(u), lambda: w_x(u).wait())
    for u in (0, 1, 2):
        guard((z >= u) & (z < 3), lambda: w_z(u, False).wait_send())
        guard((z + u <= 3) & (z > 0), lambda: w_z(u + 3 if u else 0, True).wait_send())
    for xx in range(2):
        for zz in range(4):
            for cc in range(2):
                for yy in range(2):
                    r = (xx * 2 + cc) * 8 + zz * 2 + yy
                    blk = Ws[xx * 4 + zz, cc * 2 + yy, 0:16, 3 * W:3 * W + 128].astype(f32)
                    vec[:, r * 32:(r + 1) * 32] = blk[:, 0:32]
                    fb1[:, r * 128:(r + 1) * 128] = blk[8:16, :]
                c0 = (xx * 2 + cc) * 256 + zz * 64
                wT[:, c0:c0 + 64] = Ws[xx * 4 + zz, cc * 2:cc * 2 + 2, :, 0:3 * W].reshape(64, 3 * W).T
    hours = jnp.zeros((1, 1), f32)
    for zz in range(4):
        hz = Ws[x * 4, (zz // 2) * 2, 0:16, 3 * W:3 * W + 128].astype(f32)[11:12, zz % 2:zz % 2 + 1]
        hours = jnp.where(z == zz, hz, hours)
    t = hours / 100.0
    for j in range(2):
        ccp[j].wait()
        cycp[j].wait()
    ag_slot(6)
    shift = t * vec[0:1, :] + vec[1:2, :]
    vec[14:15, :] = jnp.broadcast_to(t, (1, D))
    vec[15:16, :] = shift
    gain, bias = vec[2:3, :], vec[3:4, :]
    qb = vec[:, pl.ds(hg * W, W)].T
    def blk(p, carry):
        for i in range(8):
            if 34 + i in PLAN:
                @pl.when(p == i)
                def _():
                    ag_slot(34 + i)
        v = T[p].astype(f32) + shift
        cen = v - jnp.mean(v, axis=-1, keepdims=True)
        r = lax.rsqrt(jnp.mean(cen * cen, axis=-1, keepdims=True) + EPS)
        nb = (cen * r * gain + bias).astype(bf16)
        T[p] = nb
        pr = dot_nt(wT[...], nb)
        cols = pl.ds(p * R, R)
        qkvT[0:W, cols] = (pr[0:W] + qb[:, 4:5]).astype(bf16)
        qkvT[W:2 * W, cols] = pr[W:2 * W].astype(bf16)
        qkvT[2 * W:3 * W, cols] = (pr[2 * W:] + qb[:, 5:6]).astype(bf16)
        return carry
    own[...] = T[pl.ds(hg * 2, 2)]
    lax.fori_loop(0, T.shape[0], blk, 0)
    keep = pltpu.make_async_copy(T, normed, ln)
    keep.start()
    early = [pltpu.make_async_copy(a, b, lq.at[i]) for i, (a, b) in enumerate(((qkvT, qkv_out), (wT, w_out_), (oT, o_out)))]
    early.append(pltpu.make_async_copy(own, own_out, lq.at[3]))
    early[0].start()
    early[1].start()
    early[3].start()
    ag_slot(7)
    keep.wait()
    def cot_copy(i):
        zt = 2 * c + i
        return zt, rcopy(cot.at[i], up.at[lax.rem(z, 2)], su.at[i], ru.at[lax.rem(z, 2)], dev(x, lax.div(z, 2), zt, y))
    def cot_start():
        for i in range(2):
            zt, cp = cot_copy(i)
            @pl.when(zt != z)
            def _():
                cp.start()
            @pl.when(zt == z)
            def _():
                pltpu.make_async_copy(cot.at[i], up.at[lax.rem(z, 2)], lu).start()
    def cot_wait():
        for j in range(2):
            @pl.when(2 * c + j != z)
            def _():
                rcopy(cot.at[0], up.at[j], su.at[0], ru.at[j], sib).wait_recv()
            @pl.when(2 * c + j == z)
            def _():
                pltpu.make_async_copy(cot.at[0], up.at[j], lu).wait()
            zt, cp = cot_copy(j)
            @pl.when(zt != z)
            def _():
                cp.wait_send()
    def attention(k_s, o_s):
        for h in range(heads):
            k_s[h] = qkvT[W + h * hd:W + (h + 1) * hd, :].T
        QB, KB = 2 * R, 512
        cs = LOG2E * hd ** -0.5
        nk = N // KB
        def group(k, carry):
            cc = jnp.where((k == 1) | (k == 2), 1 - c, c)
            yy = jnp.where(k < 2, 1 - y, y)
            g = cc * 2 + yy
            qcols = pl.ds(g * QB, QB)
            def head(h, carry):
                step = k * heads + h
                for i in range(16):
                    if 8 + i in PLAN or COT == 8 + i:
                        @pl.when(step == i)
                        def _():
                            ag_slot(8 + i)
                            if COT == 8 + i:
                                cot_start()
                qt = qkvT[pl.ds(h * hd, hd), qcols]
                def scores(i):
                    return dot_nn(k_s[h, i * KB:(i + 1) * KB, :], qt)
                m = None
                s = scores(0)
                for i in range(nk):
                    nxt = scores(i + 1) if i + 1 < nk else None
                    cm = jnp.max(s, axis=0, keepdims=True)
                    mn = cm if m is None else jnp.maximum(m, cm)
                    p = jnp.exp2(s * cs - mn * cs)
                    ps = jnp.sum(p, axis=0, keepdims=True)
                    vt = qkvT[pl.ds(2 * W + h * hd, hd), i * KB:(i + 1) * KB]
                    ov = dot_nn(vt, p.astype(bf16))
                    if m is None:
                        l, o = ps, ov
                    else:
                        a = jnp.exp2((m - mn) * cs)
                        l = l * a + ps
                        o = o * a + ov
                    m = mn
                    s = nxt
                o = o / l
                o_s[g, pl.ds(h * hd, hd), :] = o.astype(bf16)
                oT[pl.ds(h * hd, hd), qcols] = o
                lse[pl.ds(h, 1), qcols] = m * cs + jnp.log2(l)
                return carry
            lax.fori_loop(0, heads, head, 0)
            @pl.when(k < 3)
            def _():
                rcopy(o_s.at[g], bt.at[hg], so.at[k], ro.at[k], dev(x, cc, z, yy)).start()
            @pl.when(k == 3)
            def _():
                pltpu.make_async_copy(o_s.at[g], bt.at[hg], lo).start()
            return carry
        lax.fori_loop(0, 4, group, 0)
        for k, d in enumerate((yp, diag, sib)):
            rcopy(o_s.at[0], bt.at[hg], so.at[k], ro.at[k], d).wait()
        pltpu.make_async_copy(o_s.at[0], bt.at[hg], lo).wait()
    pl.run_scoped(attention, pltpu.VMEM((heads, N, hd), bf16), pltpu.VMEM((4, W, 2 * R), bf16))
    for i in range(2):
        zt, cp, loc = tcp[i]
        @pl.when(zt != z)
        def _():
            cp.wait_send()


    early[2].start()
    FF = fb1.shape[1]
    C = 2 * R

    H = R // 2
    def out_copy(bout, j):
        zt = 2 * c + j
        src, dst = bout.at[j, pl.ds(0, H)], bo.at[lax.rem(z, 2)]
        return zt, rcopy(src, dst, sbo.at[j], qbo.at[lax.rem(z, 2)], dev(x, lax.div(z, 2), zt, y)), pltpu.make_async_copy(src, dst, lbo)
    def out_wait(bout):
        src = bout.at[0, pl.ds(0, H)]
        for i in range(2):
            zt, cp, lc = out_copy(bout, i)
            @pl.when(2 * c + i != z)
            def _():
                rcopy(src, bo.at[i], sbo.at[0], qbo.at[i], sib).wait_recv()
            @pl.when(2 * c + i == z)
            def _():
                pltpu.make_async_copy(src, bo.at[i], lbo).wait()
            @pl.when(zt != z)
            def _():
                cp.wait_send()

    def middle_part(Wo, mid_s, n2, n2T, oacc, dacc, f1b, f2b, p1, sb1, k1, p2, sb2, k2, sb3, bout, lw, l1, l2):
        ag_slot(24)
        ag_got(2, 0)
        ag_got(2, 1)
        cpw = pltpu.make_async_copy(gc, Wo, lw)
        cpw.start()
        bT = bt[...].reshape(4 * W, C).T
        cpw.wait()
        w_o = Wo[...].reshape(D, D)
        def norm(v):
            cen = v - jnp.mean(v, axis=-1, keepdims=True)
            return cen, lax.rsqrt(jnp.mean(cen * cen, axis=-1, keepdims=True) + EPS)
        for j in range(2):
            v = own[j].astype(f32) + vec[15:16, :] + dot_nn(bT[j * R:(j + 1) * R], w_o) + vec[6:7, :]
            mid_s[j] = v
            cen, r = norm(v)
            nb = (cen * r * vec[7:8, :] + vec[8:9, :]).astype(bf16)
            n2[j] = nb
            n2T[:, :, j * R:(j + 1) * R] = nb.T.reshape(4, D // 4, R)
        ag_slot(25)
        ag_got(0, 0)
        ag_got(0, 1)
        cot_wait()
        ag_got(1, 0)

        def order(s):
            zp = jnp.where(s < 4, lax.div(z, 2), 1 - lax.div(z, 2))
            xx = jnp.where(lax.rem(lax.div(s, 2), 2) == 0, 1 - x, x)
            cc = lax.rem(s, 2)
            return xx, cc, zp, (xx * 2 + cc) * 2 + zp
        def loads(s):
            xx, cc, zp, j = order(s)
            slot = lax.rem(s, 2)
            return (pltpu.make_async_copy(ga.at[:, :, :, :, :, pl.ds(pl.multiple_of(j * C, C), C)], f1b.at[slot], l1.at[slot]),
                    pltpu.make_async_copy(gb.at[xx, cc, pl.ds(zp * 2, 2)], f2b.at[slot], l2.at[slot]))
        for cp in loads(0):
            cp.start()
        oacc[...] = jnp.zeros_like(oacc)
        dacc[...] = jnp.zeros_like(dacc)
        def sends(s):
            slot = lax.rem(s, 2)
            return (rcopy(sb1.at[slot], r1.at[slot], sf1.at[s], rf1.at[s], sib), rcopy(sb2, r2, sf2.at[s], rf2.at[s], sib))
        def cols_of(s):
            return pl.ds(pl.multiple_of(order(s)[3] * C, C), C)
        def go1(s):
            slot = lax.rem(s, 2)
            out = []
            for q in range(2):
                cs_ = pl.ds(q * C, C)
                out.append(rcopy(k1.at[slot, :, 1 - y, :, cs_], h1.at[q, :, :, cols_of(s)], sh1.at[s, q], qh1.at[s, q], yp))
                out.append(pltpu.make_async_copy(k1.at[slot, :, y, :, cs_], a1.at[q, :, :, cols_of(s)], la1.at[s, q]))
            return out
        def go2(s):
            slot, zp = lax.rem(lax.div(s, 2), 2), order(s)[2]
            i = lax.div(s, 4)
            return (rcopy(k2.at[slot], h2.at[pl.ds(zp * 2, 2)], sh2.at[i], qh2.at[i], xp),
                    pltpu.make_async_copy(k2.at[slot], a2.at[pl.ds(zp * 2, 2)], la2.at[i]))
        def keeps(s):
            return lax.rem(s, 2) == c
        def away(s):
            return lax.rem(lax.div(s, 2), 2) == 0
        def finish(s):
            slot = lax.rem(s, 2)
            sends(s)[0].wait_recv()
            @pl.when(s >= 2)
            def _():
                for n, cp in enumerate(go1(s - 2)):
                    cp.wait() if n % 2 else cp.wait_send()
            k1[slot] = (p1[...].astype(f32) + r1[slot].astype(f32)).astype(bf16)
            for cp in go1(s):
                cp.start()
            @pl.when(keeps(s))
            def _():
                sends(s)[1].wait_recv()
                @pl.when(s >= 4)
                def _():
                    @pl.when(away(s))
                    def _():
                        go2(s - 4)[0].wait_send()
                    @pl.when(jnp.logical_not(away(s)))
                    def _():
                        go2(s - 4)[1].wait()
                k2[lax.rem(lax.div(s, 2), 2)] = (p2[...].astype(f32) + r2[...].astype(f32)).astype(bf16).reshape(k2.shape[1:])
                @pl.when(away(s))
                def _():
                    go2(s)[0].start()
                @pl.when(jnp.logical_not(away(s)))
                def _():
                    go2(s)[1].start()
        def chunk(s, carry):
            slot = lax.rem(s, 2)
            xx, cc, zp, j = order(s)
            for cp in loads(s):
                cp.wait()
            for i in range(8):
                if 26 + i in PLAN or i == 3:
                    @pl.when(s == i)
                    def _():
                        ag_slot(26 + i)
                        if i == 3:
                            ag_got(1, 1)
            @pl.when(s < 7)
            def _():
                for cp in loads(s + 1):
                    cp.start()
            f1c = f1b[slot].reshape(D, C)
            f2c = f2b[slot].reshape(C, D)
            u2 = up[...].reshape(C, D)
            h = dot_nn(n2[...].reshape(C, D), f1c) + fb1[2:3, pl.ds(pl.multiple_of(j * C, C), C)]
            da = dot_nt(u2, f2c)
            ph = 0.5 + 0.5 * lax.erf(h * 0.7071067811865476)
            act = (h * ph).astype(bf16)
            hgr = (da * (ph + h * (jnp.exp(-0.5 * h * h) * 0.3989422804014327))).astype(bf16)
            oacc[...] += dot_nn(act, f2c).reshape(2, R, D)
            sums[pl.ds(4 + lax.div(j, 2), 1), pl.ds(pl.multiple_of(lax.rem(j, 2) * C, C), C)] = jnp.sum(hgr.astype(f32), axis=0, keepdims=True)
            dacc[...] += dot_nt(hgr, f1c).reshape(2, R, D)
            @pl.when(s > 0)
            def _():
                finish(s - 1)
            @pl.when(s >= 2)
            def _():
                sends(s - 2)[0].wait_send()
            @pl.when((s >= 2) & jnp.logical_not(keeps(s)))
            def _():
                sends(s - 2)[1].wait_send()
            for q in range(2):
                sb1[slot, :, :, :, q * C:(q + 1) * C] = dot_nn(n2T[q * 2 + 1 - c], hgr).astype(bf16).reshape(4, 2, R // 8, C)
            sends(s)[0].start()
            g2 = dot_nn(act.T, u2).astype(bf16)
            @pl.when(keeps(s))
            def _():
                p2[...] = g2
            @pl.when(jnp.logical_not(keeps(s)))
            def _():
                sb2[...] = g2
                sends(s)[1].start()
            for q in range(2):
                p1[:, :, :, q * C:(q + 1) * C] = dot_nn(n2T[q * 2 + c], hgr).astype(bf16).reshape(4, 2, R // 8, C)
            return carry
        lax.fori_loop(0, 8, chunk, 0)
        for j in range(2):
            bout[j] = (mid_s[j] + oacc[j] + vec[9:10, :]).astype(bf16)
            zt, cp, lc = out_copy(bout, j)
            @pl.when(zt != z)
            def _():
                cp.start()
            @pl.when(zt == z)
            def _():
                lc.start()
        second = pltpu.make_async_copy(bout.at[:, pl.ds(H, H)], bout_b, lq.at[6])
        second.start()
        last = jnp.int32(7)
        finish(last)

        tot = [jnp.zeros((1, D), f32) for _ in range(4)]
        ags = []
        for j in range(2):
            v = mid_s[j]
            cen, r = norm(v)
            xh = cen * r
            u = dacc[j]
            e = u * vec[7:8, :]
            g = up[j].astype(f32) + r * (e - jnp.mean(e, axis=-1, keepdims=True) - xh * jnp.mean(e * xh, axis=-1, keepdims=True))
            mgrad[j] = g
            ag = g.astype(bf16)
            ags.append(ag)
            for n, val in enumerate((ag.astype(f32), u * xh, u, up[j].astype(f32))):
                tot[n] = tot[n] + jnp.sum(val, axis=0, keepdims=True)
        for n in range(4):
            sums[n:n + 1, :] = tot[n]
        ag = jnp.concatenate(ags, axis=0)
        for q in range(2):
            sb3[q] = dot_nn(bt[q * 2 + 1 - c], ag).astype(bf16)
            rcopy(sb3.at[q], r3.at[q], sf3.at[q], rf3.at[q], sib).start()
        for q in range(4):
            dob[q] = dot_nt(Wo[q // 2, q % 2].reshape(D // 4, D), ag).astype(bf16)
        late = [pltpu.make_async_copy(dob, dob_out, lq.at[4]), pltpu.make_async_copy(mgrad, mg_out, lq.at[5])]
        for cp in late:
            cp.start()
        for q in range(2):
            rcopy(sb3.at[q], r3.at[q], sf3.at[q], rf3.at[q], sib).wait()
            r3[q] = (r3[q].astype(f32) + dot_nn(bt[q * 2 + c], ag)).astype(bf16)
        cp3 = pltpu.make_async_copy(r3, a3, la3)
        cp3.start()
        for s in (6, 7):
            sends(s)[0].wait_send()
            @pl.when(c != s % 2)
            def _():
                sends(s)[1].wait_send()
            for n, cp in enumerate(go1(jnp.int32(s))):
                cp.wait() if n % 2 else cp.wait_send()
        for s in range(8):
            for cp in go1(jnp.int32(s))[::2]:
                cp.wait_recv()
        go2(4 + c)[0].wait_send()
        go2(6 + c)[1].wait()
        for i in range(2):
            go2(i * 4 + c)[0].wait_recv()
        cp3.wait()
        for cp in early + late + [second]:
            cp.wait()
        out_wait(bout)
        for p in range(3):
            ag_sent(p)

    SD = pltpu.SemaphoreType.DMA
    V = pltpu.VMEM
    blk1 = (4, 2, R // 8, 2 * C)
    pl.run_scoped(middle_part, V(gc.shape, bf16), V((2, R, D), f32), V((2, R, D), bf16), V((4, D // 4, C), bf16), V((2, R, D), f32),
                  V((2, R, D), f32), V((2,) + ga.shape[:5] + (C,), bf16), V((2, 2) + gb.shape[3:], bf16),
                  V(blk1, bf16), V((2,) + blk1, bf16), V((2,) + blk1, bf16), V((C, D), bf16), V((C, D), bf16), V((2, 2) + gb.shape[3:], bf16),
                  V((2, D // 4, D), bf16), V((2, R, D), bf16), SD, SD((2,)), SD((2,)))


def forward_kernel(tok, cot, wq, small, fa, fb, fc, heads, hd):
    n_it, R, D = tok.shape
    FF = fa.shape[1]
    W = heads * hd
    N = 8 * R
    C = 2 * R
    S = pltpu.SemaphoreType.DMA
    V = pltpu.VMEM
    vm = pl.BlockSpec(memory_space=pltpu.VMEM)
    hbm = pl.BlockSpec(memory_space=pl.ANY)
    sd = jax.ShapeDtypeStruct
    full = lambda a: sd((2, 2, 4, 2) + a.shape, bf16)
    return pl.pallas_call(
        functools.partial(fwd_kernel, hd, heads),
        in_specs=[hbm] * 7,
        out_specs=[hbm] * 3 + [vm, hbm, vm] + [hbm] * 10 + [vm] + [hbm] * 3,
        out_shape=[
            sd((8, R, D), bf16), sd((3 * W, N), bf16), sd((W, N), f32), sd((heads, N), f32), sd((2, R, D), bf16), sd((16, D), f32),
            sd((3 * W, D), bf16), sd((2, 4) + fa.shape, bf16), sd((2, 4) + fa.shape, bf16), sd((4, 2) + fb.shape, bf16),
            sd((4, 2) + fb.shape, bf16), sd((2, D // 4, D), bf16), sd((4, W, C), bf16),
            sd((2, R, D), f32), sd((2, R // 2, D), bf16), sd((2, R // 2, D), bf16), sd((16, D), f32), full(fa), full(fb), full(fc),
        ],
        scratch_shapes=[
            V((3 * W, N), bf16), V((W, N), f32), V((3 * W, D), bf16), V((2, R, D), bf16), V((4, W, C), bf16), V((2, R, D), f32),
            V((8, R, D), bf16), V((8, 4, 32, 3 * W + 128), bf16), V((8, FF), f32), V((4, W, C), bf16), V((2, R, D), bf16),
            V((2, 4, 2, R // 8, 2 * C), bf16), V((C, D), bf16), V((2, D // 4, D), bf16),
            S((2,)), S((2,)), S, S((2,)), S((2,)), S((2,)), S((2,)), S((2,)), S((2,)),
            S((3, 4)), S((3, 4)), S((4,)), S((6,)), S((6,)), S((7,)), S((7,)), S((3,)), S((3,)), S, S,
            S((2,)), S((2,)), S, S((3,)), S((3,)), S((3, 6)), S((3, 6)), S((3, 7)), S((3, 7)), S((3, 7)), S((3, 7)), S((3, 7)), S((3, 7)),
            S((8,)), S((8,)), S((8,)), S((8,)), S((2,)), S((2,)), S((8, 2)), S((2,)), S,
            S((8, 2)), S((8, 2)), S((2,)), S((2,)), S((2,)), S((2,)), S, S((7,)),
        ],
        compiler_params=pltpu.CompilerParams(collective_id=0, has_side_effects=True, vmem_limit_bytes=60 << 20),
        name="forward",
    )(tok, cot, wq, small, fa, fb, fc)


def put_sum(dst, pieces):
    total = pieces[0].astype(f32)
    for p in pieces[1:]:
        total = total + p.astype(f32)
    dst[...] = total.astype(dst.dtype)


def tail_kernel(hd, heads, dob, qkv_in, o_in, lse, a1, h1, a2, h2, a3, normed, wT, own, rows, mgrad, sums0, bout_b,
                o1, o2, o3, gq, hm, sums, bo_b,
                qkvT, oT, out_vm, do_s, dq_s, k1, r11, r12, r13, k2, r21, r22, r23, k3, r31, r32, r33,
                nm, w_s, Gb, gx, gz, go, ds_s, dr_c, dy_s, dr_y, ig, vs, vr,
                sd, rd, ld, s1, q1, s2, q2, s3, q3, lk, sg, qg, sgz, qgz, sga, qga, sdc, qdc, sdy, qdy, sh, qh, lh, sv, qv, ll, lnm, lqo, sbo, qbo, lbo):
    x, c, z, y = place()
    hg = c * 2 + y
    W = heads * hd
    N = qkv_in.shape[1]
    zoff = [lax.rem(z + k, 4) for k in (1, 2, 3)]
    sib, yp, diag, xp = dev(x, 1 - c, z, y), dev(x, c, z, 1 - y), dev(x, 1 - c, z, 1 - y), dev(1 - x, c, z, y)
    zp = [dev(x, c, zz, y) for zz in zoff]
    ins = [pltpu.make_async_copy(a, b, lqo.at[i]) for i, (a, b) in enumerate(((qkv_in, qkvT), (o_in, oT)))]
    for cp in ins:
        cp.start()
    greet(zp + [dev(x, 1 - c, zz, y) for zz in zoff] + [sib, yp, diag, xp])
    peers = ((sib, (1 - c) * 2 + y), (yp, c * 2 + 1 - y), (diag, (1 - c) * 2 + 1 - y))
    for k, (d, g) in enumerate(peers):
        rcopy(dob.at[g], do_s.at[hg], sd.at[k], rd.at[k], d).start()
    loc = pltpu.make_async_copy(dob.at[hg], do_s.at[hg], ld)
    loc.start()

    def out_copy(j):
        zt = 2 * c + j
        src, dst = bout_b.at[j], bo_b.at[lax.rem(z, 2)]
        return zt, rcopy(src, dst, sbo.at[j], qbo.at[lax.rem(z, 2)], dev(x, lax.div(z, 2), zt, y))
    def out_local(j):
        v = out_vm.at[j]
        return pltpu.make_async_copy(bout_b.at[j], v, lbo.at[0]), pltpu.make_async_copy(v, bo_b.at[lax.rem(z, 2)], lbo.at[1])
    for j in range(2):
        zt, cp = out_copy(j)
        @pl.when(zt != z)
        def _():
            cp.start()
        @pl.when(zt == z)
        def _():
            out_local(j)[0].start()
    def out_wait():
        for i in range(2):
            zt, cp = out_copy(i)
            @pl.when(2 * c + i != z)
            def _():
                rcopy(bout_b.at[0], bo_b.at[i], sbo.at[0], qbo.at[i], sib).wait_recv()
            @pl.when(2 * c + i == z)
            def _():
                first, then = out_local(i)
                first.wait()
                then.start()
                then.wait()
            @pl.when(zt != z)
            def _():
                cp.wait_send()

    def part(ref, h, n):
        return ref if n is None else ref.at[..., pl.ds(h * n, n), :]
    n1, n2 = k1.shape[2] // 2, k2.shape[2] // 2

    class Piece:
        def __init__(self, i, h, n, a, first, k, r1, r2, r3, out, s, q, lsem, yfirst):
            self.h = None if first is None else part(first, h, n)
            self.a, self.k, self.r1, self.r2, self.r3, self.out = [part(v, h, n) for v in (a, k, r1, r2, r3, out)]
            self.s, self.q, self.lsem, self.yfirst, self.b = s, q, lsem, yfirst, h * 5
            self.i = i
        def copies(self):
            b, s, q = self.b, self.s, self.q
            if self.yfirst:
                second = rcopy(self.k.at[1 - x], self.r2, s.at[b + 1], q.at[b + 1], xp)
                mine = lambda zz: self.k.at[x, zz]
            else:
                second = rcopy(self.k.at[:, 1 - y], self.r2, s.at[b + 1], q.at[b + 1], yp)
                mine = lambda zz: self.k.at[zz, y]
            if self.h is None:
                first = rcopy(self.a.at[1 - x], self.r1, s.at[b], q.at[b], xp)
                kept = self.a.at[x]
            else:
                first = pltpu.make_async_copy(self.h, self.r1, s.at[b])
                kept = self.a
            zs = [rcopy(mine(zoff[j]), self.r3.at[j], s.at[b + 2 + j], q.at[b + 2 + j], zp[j]) for j in range(3)]
            return first, second, zs, pltpu.make_async_copy(kept, self.k, self.lsem.at[self.i]), mine
        def start(self):
            first, _, _, keep, _ = self.copies()
            keep.start()
            first.start()
        def second(self):
            first, second, _, keep, _ = self.copies()
            keep.wait()
            first.wait()
            n0, n1_ = self.k.shape[0], self.k.shape[1]
            def add(j, carry):
                p, q_ = lax.div(j, n1_), lax.rem(j, n1_)
                self.k[p, q_] = self.k[p, q_] + self.r1[p, q_]
                return carry
            lax.fori_loop(0, n0 * n1_, add, 0)
            second.start()
        def third(self):
            _, second, zs, _, mine = self.copies()
            second.wait()
            def add(zz, carry):
                mine(zz)[...] = mine(zz)[...] + self.r2[zz]
                return carry
            lax.fori_loop(0, 4, add, 0)
            for cp in zs:
                cp.start()
        def finish(self):
            _, _, zs, _, mine = self.copies()
            for cp in zs:
                cp.wait()
            put_sum(self.out, [mine(z)[...]] + [self.r3[j] for j in range(3)])

    f1 = [Piece(h, h, n1, a1, h1, k1, r11, r12, r13, o1, s1, q1, lk, True) for h in range(2)]
    f2 = [Piece(2 + h, h, n2, a2, h2, k2, r21, r22, r23, o2, s2, q2, lk, False) for h in range(2)]
    f3 = Piece(4, 0, None, a3, None, k3, r31, r32, r33, o3, s3, q3, lk, False)
    for piece in (f2[0], f1[0], f2[1], f1[1], f3):
        piece.start()

    QB, KB = N // 4, 512
    cs = LOG2E * hd ** -0.5
    sc = hd ** -0.5
    nk = N // KB

    ld_n = pltpu.make_async_copy(normed, nm, lnm.at[0])
    ld_w = pltpu.make_async_copy(wT, w_s, lnm.at[1])
    ld_n.start()
    ld_w.start()

    def G_first(pr):
        rows_ = [dq_s[q * W + pr * 2 * hd:q * W + (pr + 1) * 2 * hd, :] for q in range(3)]
        g = dot_nn(jnp.concatenate(rows_, axis=0), nm[...].reshape(N, nm.shape[2])).astype(bf16).T
        Gb[pr] = g.reshape(Gb.shape[1:])
        G_x(pr).start()
    def G_x(pr):
        return rcopy(Gb.at[pr, 1 - x], gx.at[pr], sg.at[pr], qg.at[pr], xp)
    def G_z(pr):
        return [rcopy(Gb.at[pr, x, :, zoff[j]], gz.at[pr, j], sgz.at[pr, j], qgz.at[pr, j], zp[j]) for j in range(3)]
    def G_second(pr):
        G_x(pr).wait()
        def add(i, carry):
            cc, zz = lax.div(i, 4), lax.rem(i, 4)
            Gb[pr, x, cc, zz] = Gb[pr, x, cc, zz] + gx[pr, cc, zz]
            return carry
        lax.fori_loop(0, 8, add, 0)
        for cp in G_z(pr):
            cp.start()
    def G_own(pr):
        cps = [rcopy(Gb.at[pr, x, cc, z, yy], go.at[pr, hg], sga.at[pr, k], qga.at[pr, k], d)
               for k, (d, cc, yy) in enumerate(((sib, 1 - c, y), (yp, c, 1 - y), (diag, 1 - c, 1 - y)))]
        return cps, pltpu.make_async_copy(Gb.at[pr, x, c, z, y], go.at[pr, hg], ll.at[pr])
    def G_third(pr):
        for cp in G_z(pr):
            cp.wait()
        def add(i, carry):
            cc, yy = lax.div(i, 2), lax.rem(i, 2)
            put_sum(Gb.at[pr, x, cc, z, yy], [Gb[pr, x, cc, z, yy]] + [gz[pr, k, cc, yy] for k in range(3)])
            return carry
        lax.fori_loop(0, 4, add, 0)
        cps, own_ = G_own(pr)
        for cp in cps:
            cp.start()
        own_.start()
    def G_done(pr):
        cps, own_ = G_own(pr)
        own_.wait()
        for cp in cps:
            cp.wait()
        D_ = gq.shape[1] // 3
        for g in range(4):
            for q in range(3):
                at = q * D_ + g * W + pr * 2 * hd
                gq[:, at:at + 2 * hd] = go[pr, g, :, q * 2 * hd:(q + 1) * 2 * hd].astype(f32)

    PLAN = {
        1: ((Piece.second, f1[1]),),
        2: ((Piece.second, f2[0]),),
        5: ((Piece.second, f2[1]), (Piece.third, f1[1]),),
        6: ((Piece.second, f1[0]),),
        7: ((Piece.third, f2[0]),),
        8: ((Piece.second, f3),),
        11: ((Piece.third, f2[1]), (Piece.third, f3),),
        13: ((G_second, 0),),
        15: ((Piece.third, f1[0]),),
        17: ((G_second, 1),),
        19: ((G_third, 0),),
        21: ((G_third, 1), (G_done, 0),),
        22: ((Piece.finish, f2[0]),),
        24: ((Piece.finish, f3), (G_done, 1),),
        25: ((Piece.finish, f1[0]), (Piece.finish, f1[1]), (Piece.finish, f2[1]),),
    }

    def slot(i):
        for f, a in PLAN.get(i, ()):
            f(a)

    def attention(k_s, v_s, dk_s, dv_s):
        loc.wait()
        for cp in ins:
            cp.wait()
        def head(h, carry):
            hr = pl.ds(h * hd, hd)
            @pl.when(h == 2)
            def _():
                ld_n.wait()
                G_first(0)
            k_s[...] = qkvT[pl.ds(W + h * hd, hd), :].T
            v_s[...] = qkvT[pl.ds(2 * W + h * hd, hd), :].T
            dk_s[...] = jnp.zeros_like(dk_s)
            dv_s[...] = jnp.zeros_like(dv_s)
            def group(k, carry):
                step = h * 4 + k
                @pl.when((step > 0) & (step < 4))
                def _():
                    rcopy(dob.at[0], do_s.at[0], sd.at[k - 1], rd.at[k - 1], sib).wait()
                for i in range(16):
                    if i in PLAN:
                        @pl.when(step == i)
                        def _():
                            slot(i)
                cc = jnp.where((k == 1) | (k == 3), 1 - c, c)
                yy = jnp.where(k >= 2, 1 - y, y)
                g = cc * 2 + yy
                qcols = pl.ds(g * QB, QB)
                qt = qkvT[hr, qcols]
                dt = do_s[g, hr, :]
                delta = jnp.sum(dt.astype(f32) * oT[hr, qcols], axis=0, keepdims=True)
                ls = lse[pl.ds(h, 1), qcols]
                def first(i):
                    ks = slice(i * KB, (i + 1) * KB)
                    return dot_nn(k_s[ks, :], qt), dot_nn(v_s[ks, :], dt)
                dq = None
                cur = first(0)
                for i in range(nk):
                    nxt = first(i + 1) if i + 1 < nk else None
                    s, dp = cur
                    ks = slice(i * KB, (i + 1) * KB)
                    p = jnp.exp2(s * cs - ls)
                    ds = (p * (dp - delta)).astype(bf16)
                    prt = dot_nn(qkvT[pl.ds(W + h * hd, hd), ks], ds)
                    dq = prt if dq is None else dq + prt
                    dk_s[:, ks] += dot_nt(qt, ds)
                    dv_s[:, ks] += dot_nt(dt, p.astype(bf16))
                    cur = nxt
                dq_s[hr, qcols] = (dq * sc).astype(bf16)
                return carry
            lax.fori_loop(0, 4, group, 0)
            dq_s[pl.ds(W + h * hd, hd), :] = (dk_s[...] * sc).astype(bf16)
            dq_s[pl.ds(2 * W + h * hd, hd), :] = dv_s[...].astype(bf16)
            return carry
        lax.fori_loop(0, heads, head, 0)

    pl.run_scoped(attention, pltpu.VMEM((N, hd), bf16), pltpu.VMEM((N, hd), bf16),
                  pltpu.VMEM((hd, N), f32), pltpu.VMEM((hd, N), f32))

    def after(tok_s, mg_s, dn, lsem):
        R = tok_s.shape[1]
        B = R // 2
        loads = [pltpu.make_async_copy(a, b, lsem.at[i]) for i, (a, b) in enumerate(((own, tok_s), (mgrad, mg_s)))]
        for cp in loads:
            cp.start()
        ld_w.wait()
        def proj(g, j):
            return dot_nn(dq_s[:, pl.ds(pl.multiple_of(g * QB + j * R, R), R)].T, w_s[...])
        g_sy, g_s, g_oy = (1 - c) * 2 + 1 - y, (1 - c) * 2 + y, c * 2 + 1 - y
        def rows_of(b):
            return b // 2, pl.ds((b % 2) * B, B)
        def to_sib(a, b):
            j, rw = rows_of(b)
            return rcopy(ds_s.at[a, j, rw], dr_c.at[a, j, rw], sdc.at[a * 4 + b], qdc.at[a * 4 + b], sib)
        def to_y(b):
            j, rw = rows_of(b)
            return rcopy(dy_s.at[j, rw], dr_y.at[j, rw], sdy.at[b], qdy.at[b], yp)
        for j in range(2):
            ds_s[0, j] = proj(g_sy, j).astype(bf16)
            to_sib(0, 2 * j).start()
            to_sib(0, 2 * j + 1).start()
        for j in range(2):
            mine = proj(g_oy, j)
            for b in (2 * j, 2 * j + 1):
                rw = rows_of(b)[1]
                to_sib(0, b).wait()
                dy_s[j, rw, :] = (mine[(b % 2) * B:(b % 2 + 1) * B] + dr_c[0, j, rw, :].astype(f32)).astype(bf16)
                to_y(b).start()
        slot(16)
        G_first(1)
        for j in range(2):
            ds_s[1, j] = proj(g_s, j).astype(bf16)
            to_sib(1, 2 * j).start()
            to_sib(1, 2 * j + 1).start()
        for j in range(2):
            dn[j] = proj(hg, j)
        ones = jnp.ones((8, N), bf16)
        vs[...] = sums0[...]
        for row, q in ((12, 0), (13, 2)):
            tot = dot_nt(ones, dq_s[q * W:(q + 1) * W, :])
            vs[row:row + 1, :] = jnp.zeros((1, vs.shape[1]), f32)
            vs[row:row + 1, pl.ds(pl.multiple_of(hg * W, W), W)] = tot[0:1]
        slot(17)
        gain = rows[2:3, :]
        shift = rows[15:16, :]
        acc = [jnp.zeros((1, dn.shape[2]), f32) for _ in range(3)]
        for cp in loads:
            cp.wait()
        def home_copy(b):
            j, rw = rows_of(b)
            i = lax.rem(z, 2)
            zt = 2 * c + j
            return zt, rcopy(ig.at[j, rw], hm.at[i, rw], sh.at[b], qh.at[i, b % 2], dev(x, lax.div(z, 2), zt, y)), \
                pltpu.make_async_copy(ig.at[j, rw], hm.at[i, rw], lh.at[b % 2])
        for b in range(4):
            j, rw = rows_of(b)
            to_sib(1, b).wait()
            to_y(b).wait()
            u = dn[j, rw, :] + dr_c[1, j, rw, :].astype(f32) + dr_y[j, rw, :].astype(f32)
            v = tok_s[j, rw, :].astype(f32) + shift
            cen = v - jnp.mean(v, axis=-1, keepdims=True)
            r = lax.rsqrt(jnp.mean(cen * cen, axis=-1, keepdims=True) + EPS)
            xh = cen * r
            e = u * gain
            res = mg_s[j, rw, :] + r * (e - jnp.mean(e, axis=-1, keepdims=True) - xh * jnp.mean(e * xh, axis=-1, keepdims=True))
            ig[j, rw, :] = res.astype(bf16)
            for n, val in enumerate((u * xh, u, res)):
                acc[n] = acc[n] + jnp.sum(val, axis=0, keepdims=True)
            zt, cp, lc = home_copy(b)
            @pl.when(zt != z)
            def _():
                cp.start()
            @pl.when(zt == z)
            def _():
                lc.start()
            slot(18 + b)
        vs[8:9, :] = acc[0]
        vs[9:10, :] = acc[1]
        vs[10:11, :] = acc[2] * rows[14:15, :]
        vs[11:12, :] = acc[2]
        for k, d in enumerate((sib, yp, xp)):
            cp = rcopy(vs, vr.at[k], sv.at[k], qv.at[k], d)
            cp.start()
            slot(22 + k)
            cp.wait()
            vs[...] = vs[...] + vr[k]
        zv = [rcopy(vs, vr.at[3 + k], sv.at[3 + k], qv.at[3 + k], zp[k]) for k in range(3)]
        for cp in zv:
            cp.start()
        slot(25)
        for i in range(2):
            src = 2 * c + i
            for hb in range(2):
                rw = pl.ds(hb * B, B)
                @pl.when(src != z)
                def _():
                    rcopy(ig.at[0, rw], hm.at[i, rw], sh.at[0], qh.at[i, hb], sib).wait_recv()
                @pl.when(src == z)
                def _():
                    pltpu.make_async_copy(ig.at[0, rw], hm.at[i, rw], lh.at[hb]).wait()
                pass
        for cp in zv:
            cp.wait()
        sums[...] = vs[...] + vr[3] + vr[4] + vr[5]
        slot(26)
        out_wait()
        for b in range(4):
            zt, cp, lc = home_copy(b)
            @pl.when(zt != z)
            def _():
                cp.wait_send()

    R = own.shape[1]
    D = own.shape[2]
    pl.run_scoped(after, pltpu.VMEM((2, R, D), bf16), pltpu.VMEM((2, R, D), f32), pltpu.VMEM((2, R, D), f32), pltpu.SemaphoreType.DMA((2,)))


def backward_kernel(dob, qkvT, oT, lse, a1, h1, a2, h2, a3, normed, wT, own, rows, mgrad, sums0, bout_b, heads, hd):
    W3, N = qkvT.shape
    W = heads * hd
    _, R, D = own.shape
    S = pltpu.SemaphoreType.DMA
    V = pltpu.VMEM
    vm = pl.BlockSpec(memory_space=pltpu.VMEM)
    hbm = pl.BlockSpec(memory_space=pl.ANY)
    b1, b2, b3 = a1.shape[2:], a2.shape[2:], a3.shape[3:]
    def bufs(b, yfirst):
        k = (2, 4) if yfirst else (4, 2)
        return [V(k + b, bf16), V(k + b, bf16), V((4,) + b, bf16), V((3,) + b, bf16)]
    rq = D // 32
    return pl.pallas_call(
        functools.partial(tail_kernel, hd, heads),
        in_specs=[hbm, hbm, hbm, vm, hbm, hbm, hbm, hbm, hbm, hbm, hbm, hbm, vm, hbm, vm, hbm],
        out_specs=[vm] * 4 + [hbm, vm, hbm],
        out_shape=[
            jax.ShapeDtypeStruct(b1, f32), jax.ShapeDtypeStruct(b2, f32), jax.ShapeDtypeStruct(b3, f32),
            jax.ShapeDtypeStruct((rq, 3 * D), f32), jax.ShapeDtypeStruct((2, R, D), bf16), jax.ShapeDtypeStruct((16, D), f32),
            jax.ShapeDtypeStruct((2, R // 2, D), bf16),
        ],
        scratch_shapes=[V((W3, N), bf16), V((W, N), f32), V((2, R // 2, D), bf16), V((4, W, N // 4), bf16), V((W3, N), bf16)] + bufs(b1, True) + bufs(b2, False) + bufs(b3, False) + [
            V((8, R, D), bf16), V((W3, D), bf16),
            V((2, 2, 2, 4, 2, rq, W3 // 2), bf16), V((2, 2, 4, 2, rq, W3 // 2), bf16), V((2, 3, 2, 2, rq, W3 // 2), bf16), V((2, 4, rq, W3 // 2), bf16),
            V((2, 2, R, D), bf16), V((2, 2, R, D), bf16), V((2, R, D), bf16), V((2, R, D), bf16), V((2, R, D), bf16),
            V((16, D), f32), V((6, 16, D), f32),
            S((3,)), S((3,)), S, S((10,)), S((10,)), S((10,)), S((10,)), S((5,)), S((5,)), S((5,)),
            S((2,)), S((2,)), S((2, 3)), S((2, 3)), S((2, 3)), S((2, 3)), S((8,)), S((8,)), S((4,)), S((4,)),
            S((4,)), S((2, 2)), S((2,)), S((6,)), S((6,)), S((2,)), S((2,)), S((2,)), S((2,)), S((2,)), S((2,)),
        ],
        compiler_params=pltpu.CompilerParams(collective_id=1, has_side_effects=True, vmem_limit_bytes=60 << 20),
        name="backward",
    )(dob, qkvT, oT, lse, a1, h1, a2, h2, a3, normed, wT, own, rows, mgrad, sums0, bout_b)


def result_kernel(rows, fc, o1, o2, o3, gq, hm, bo_a, bo_b, sums, r1, r2, r3, rq, rh, rb, *rest):
    for a, b in ((o1, r1), (o2, r2), (o3, r3), (gq, rq)):
        b[...] = a[...]
    half = bo_a.shape[1]
    rb[:, 0:half, :] = bo_a[...]
    rb[:, half:, :] = bo_b[...]
    rh[...] = hm[...].astype(f32)
    x, c, z, y = place()
    index = (x * 2 + c) * 8 + z * 2 + y
    per = 128 // rows
    block = sums[:, pl.ds(pl.multiple_of(lax.div(index, per) * 128, 128), 128)]
    mine = pltpu.roll(block, lax.rem(per - lax.rem(index, per), per) * rows, 1)
    for ref, row in zip(rest, (8, 9, 12, 13, 0, 1, 2, None, 3, 10, 11)):
        if row is None:
            per_row = sums.shape[1] // fc
            at = pl.ds(pl.multiple_of(lax.rem(index, per_row) * fc, fc), fc)
            part = sums[0:8, at]
            val = part[4:5]
            for i in range(1, 4):
                val = jnp.where(lax.div(index, per_row) == i, part[4 + i:5 + i], val)
            ref[...] = val
        else:
            ref[...] = mine[row:row + 1, 0:rows]


def results(o1, o2, o3, gq, hm, bo_a, bo_b, sums, rows, fc):
    vm = pl.BlockSpec(memory_space=pltpu.VMEM)
    sd = jax.ShapeDtypeStruct
    widths = [rows] * 7 + [fc] + [rows] * 3
    return pl.pallas_call(
        functools.partial(result_kernel, rows, fc),
        in_specs=[vm] * 8,
        out_specs=[vm] * 17,
        out_shape=[sd(a.shape, f32) for a in (o1, o2, o3, gq, hm)] + [sd(hm.shape, bf16)] + [sd((1, w), f32) for w in widths],
        compiler_params=pltpu.CompilerParams(vmem_limit_bytes=60 << 20),
        name="results",
    )(o1, o2, o3, gq, hm, bo_a, bo_b, sums)


HEADS = 16


epsilon = EPS


def norm_rows_s(values, gain, shift):
    center = values - jnp.mean(values, axis=-1, keepdims=True)
    spread = jnp.mean(center * center, axis=-1, keepdims=True)
    return center * lax.rsqrt(spread + epsilon) * gain + shift


def gelu_exact_s(values):
    return jax.nn.gelu(values, approximate=False)


def product(left, right):
    return jnp.dot(left, right, preferred_element_type=jnp.float32)


def product_tleft(left, right):
    return lax.dot_general(
        left, right, (((0,), (0,)), ((), ())), preferred_element_type=jnp.float32
    )


def product_tright(left, right):
    return lax.dot_general(
        left, right, (((1,), (1,)), ((), ())), preferred_element_type=jnp.float32
    )


def split_heads(values):
    return values.reshape(values.shape[0], HEADS, values.shape[1] // HEADS)


def attend(operands):
    queries, keys_all, values_all = operands
    scale = (queries.shape[1] // HEADS) ** (-0.5)
    scores = (
        jnp.einsum(
            "qhd,khd->hqk",
            split_heads(queries),
            split_heads(keys_all),
            preferred_element_type=jnp.float32,
        )
        * scale
    )
    highest = jnp.max(scores, axis=-1, keepdims=True)
    exps = jnp.exp(scores - highest)
    totals = jnp.sum(exps, axis=-1, keepdims=True)
    probs_low = (exps / totals).astype(jnp.bfloat16)
    blended = jnp.einsum(
        "hqk,khd->qhd", probs_low, split_heads(values_all), preferred_element_type=jnp.float32
    ).reshape(queries.shape)
    return (blended, (highest + jnp.log(totals))[:, :, 0])


def recompute_probs(queries, keys_all, values_all, grads_in, log_totals):
    scale = (queries.shape[1] // HEADS) ** (-0.5)
    scores = (
        jnp.einsum(
            "qhd,khd->hqk",
            split_heads(queries),
            split_heads(keys_all),
            preferred_element_type=jnp.float32,
        )
        * scale
    )
    probs = jnp.exp(scores - log_totals[:, :, None])
    prob_grads = jnp.einsum(
        "qhd,khd->hqk",
        split_heads(grads_in),
        split_heads(values_all),
        preferred_element_type=jnp.float32,
    )
    return (probs, prob_grads, scale)


def key_side_grads(score_grads, probs, queries, grads_in, row_count):
    key_grads = jnp.einsum(
        "hqk,qhd->khd", score_grads, split_heads(queries), preferred_element_type=jnp.float32
    )
    value_grads = jnp.einsum(
        "hqk,qhd->khd",
        probs.astype(jnp.bfloat16),
        split_heads(grads_in),
        preferred_element_type=jnp.float32,
    )
    width = queries.shape[1]
    return (key_grads.reshape(row_count, width), value_grads.reshape(row_count, width))


def query_side(with_keys, operands):
    queries, keys_all, values_all, grads_in, log_totals = operands
    probs, prob_grads, scale = recompute_probs(queries, keys_all, values_all, grads_in, log_totals)
    row_delta = jnp.sum(probs * prob_grads, axis=-1)
    score_grads = (probs * (prob_grads - row_delta[:, :, None]) * scale).astype(jnp.bfloat16)
    query_grads = jnp.einsum(
        "hqk,khd->qhd", score_grads, split_heads(keys_all), preferred_element_type=jnp.float32
    ).reshape(queries.shape)
    key_grads, value_grads = key_side_grads(
        score_grads, probs, queries, grads_in, keys_all.shape[0]
    )
    return (query_grads, row_delta, key_grads, value_grads)


def spread_on_device(
    tokens_in,
    lead_hours,
    cotangent,
    w_qkv,
    w_out,
    w_fc1,
    w_fc2,
    ln1_gain,
    ln1_bias,
    q_bias,
    v_bias,
    out_bias,
    ln2_gain,
    ln2_bias,
    fc1_bias,
    fc2_bias,
    lead_weight,
    lead_bias,
):
    gathered = (
        lax.all_gather(w_qkv, ("dp", "seq"), axis=0, tiled=True),
        lax.all_gather(w_out, ("dp", "seq"), axis=0, tiled=True),
        lax.all_gather(w_fc1, ("dp", "seq"), axis=0, tiled=True),
        lax.all_gather(w_fc2, ("dp", "seq"), axis=0, tiled=True),
        lax.all_gather(ln1_gain, ("dp", "seq"), axis=0, tiled=True),
        lax.all_gather(ln1_bias, ("dp", "seq"), axis=0, tiled=True),
        lax.all_gather(q_bias, ("dp", "seq"), axis=0, tiled=True),
        lax.all_gather(v_bias, ("dp", "seq"), axis=0, tiled=True),
        lax.all_gather(out_bias, ("dp", "seq"), axis=0, tiled=True),
        lax.all_gather(ln2_gain, ("dp", "seq"), axis=0, tiled=True),
        lax.all_gather(ln2_bias, ("dp", "seq"), axis=0, tiled=True),
        lax.all_gather(fc1_bias, ("dp", "seq"), axis=0, tiled=True),
        lax.all_gather(fc2_bias, ("dp", "seq"), axis=0, tiled=True),
        lax.all_gather(lead_weight, ("dp", "seq"), axis=0, tiled=True),
        lax.all_gather(lead_bias, ("dp", "seq"), axis=0, tiled=True),
    )
    (
        full_qkv,
        full_out,
        full_fc1,
        full_fc2,
        gain_one,
        shift_one,
        bias_query,
        bias_value,
        bias_out,
        gain_two,
        shift_two,
        bias_fc1,
        bias_fc2,
        lead_scale,
        lead_shift,
    ) = gathered
    items, rows, width = tokens_in.shape
    count = items * rows
    lead_times = lead_hours.astype(jnp.float32) / 100.0
    leading = (
        tokens_in.astype(jnp.float32)
        + lead_times[:, None, None] * lead_scale.astype(jnp.float32)
        + lead_shift.astype(jnp.float32)
    ).reshape(count, width)
    normed, norm_one_back = jax.vjp(
        norm_rows_s, leading, gain_one.astype(jnp.float32), shift_one.astype(jnp.float32)
    )
    normed_low = normed.astype(jnp.bfloat16)
    projected = product(normed_low, full_qkv)
    queries = (projected[:, :width] + bias_query.astype(jnp.float32)).astype(jnp.bfloat16)
    keys_own = projected[:, width : 2 * width].astype(jnp.bfloat16)
    values_own = (projected[:, 2 * width :] + bias_value.astype(jnp.float32)).astype(jnp.bfloat16)
    queries3 = queries.reshape(items, rows, width)
    keys_all, values_all = (
        lax.all_gather(keys_own.reshape(items, rows, width), "seq", axis=1, tiled=True),
        lax.all_gather(values_own.reshape(items, rows, width), "seq", axis=1, tiled=True),
    )
    blended, log_totals = lax.map(attend, (queries3, keys_all, values_all))
    blended_low = blended.reshape(count, width).astype(jnp.bfloat16)
    middle = leading + product(blended_low, full_out) + bias_out.astype(jnp.float32)
    normed_two, norm_two_back = jax.vjp(
        norm_rows_s, middle, gain_two.astype(jnp.float32), shift_two.astype(jnp.float32)
    )
    normed_two_low = normed_two.astype(jnp.bfloat16)
    hidden = product(normed_two_low, full_fc1) + bias_fc1.astype(jnp.float32)
    activated, gelu_back = jax.vjp(gelu_exact_s, hidden)
    activated_low = activated.astype(jnp.bfloat16)
    output = middle + product(activated_low, full_fc2) + bias_fc2.astype(jnp.float32)
    block_output = output.reshape(items, rows, width).astype(jnp.bfloat16)
    back_qkv, back_out, back_fc1, back_fc2 = (
        lax.all_gather(w_qkv, ("dp", "seq"), axis=0, tiled=True),
        lax.all_gather(w_out, ("dp", "seq"), axis=0, tiled=True),
        lax.all_gather(w_fc1, ("dp", "seq"), axis=0, tiled=True),
        lax.all_gather(w_fc2, ("dp", "seq"), axis=0, tiled=True),
    )
    out_grad = cotangent.reshape(count, width)
    upstream = out_grad.astype(jnp.float32)
    grad_fc2 = product_tleft(activated_low, out_grad)
    grad_fc2_bias = jnp.sum(upstream, axis=0)
    hidden_grad = gelu_back(product_tright(out_grad, back_fc2))[0].astype(jnp.bfloat16)
    grad_fc1 = product_tleft(normed_two_low, hidden_grad)
    grad_fc1_bias = jnp.sum(hidden_grad.astype(jnp.float32), axis=0)
    middle_part, grad_ln2_gain, grad_ln2_bias = norm_two_back(product_tright(hidden_grad, back_fc1))
    middle_grad = upstream + middle_part
    attn_grad = middle_grad.astype(jnp.bfloat16)
    grad_out = product_tleft(blended_low, attn_grad)
    grad_out_bias = jnp.sum(attn_grad.astype(jnp.float32), axis=0)
    blended_grad = (
        product_tright(attn_grad, back_out).astype(jnp.bfloat16).reshape(items, rows, width)
    )
    query_grads, row_delta, key_parts, value_parts = lax.map(
        partial(query_side, True), (queries3, keys_all, values_all, blended_grad, log_totals)
    )
    key_grads, value_grads = (
        lax.psum_scatter(
            key_parts.astype(jnp.bfloat16), "seq", scatter_dimension=1, tiled=True
        ).astype(jnp.float32),
        lax.psum_scatter(
            value_parts.astype(jnp.bfloat16), "seq", scatter_dimension=1, tiled=True
        ).astype(jnp.float32),
    )
    query_low = query_grads.reshape(count, width).astype(jnp.bfloat16)
    key_low = key_grads.reshape(count, width).astype(jnp.bfloat16)
    value_low = value_grads.reshape(count, width).astype(jnp.bfloat16)
    qkv_grad = jnp.concatenate([query_low, key_low, value_low], axis=1)
    grad_qkv = product_tleft(normed_low, qkv_grad)
    grad_q_bias = jnp.sum(query_low.astype(jnp.float32), axis=0)
    grad_v_bias = jnp.sum(value_low.astype(jnp.float32), axis=0)
    leading_part, grad_ln1_gain, grad_ln1_bias = norm_one_back(product_tright(qkv_grad, back_qkv))
    input_grad = (middle_grad + leading_part).reshape(items, rows, width)
    grad_lead_weight = jnp.sum(jnp.sum(input_grad, axis=1) * lead_times[:, None], axis=0)
    grad_lead_bias = jnp.sum(input_grad, axis=(0, 1))
    summed = (
        lax.psum_scatter(grad_qkv, ("dp", "seq"), scatter_dimension=0, tiled=True),
        lax.psum_scatter(grad_out, ("dp", "seq"), scatter_dimension=0, tiled=True),
        lax.psum_scatter(grad_fc1, ("dp", "seq"), scatter_dimension=0, tiled=True),
        lax.psum_scatter(grad_fc2, ("dp", "seq"), scatter_dimension=0, tiled=True),
        lax.psum_scatter(grad_ln1_gain, ("dp", "seq"), scatter_dimension=0, tiled=True),
        lax.psum_scatter(grad_ln1_bias, ("dp", "seq"), scatter_dimension=0, tiled=True),
        lax.psum_scatter(grad_q_bias, ("dp", "seq"), scatter_dimension=0, tiled=True),
        lax.psum_scatter(grad_v_bias, ("dp", "seq"), scatter_dimension=0, tiled=True),
        lax.psum_scatter(grad_out_bias, ("dp", "seq"), scatter_dimension=0, tiled=True),
        lax.psum_scatter(grad_ln2_gain, ("dp", "seq"), scatter_dimension=0, tiled=True),
        lax.psum_scatter(grad_ln2_bias, ("dp", "seq"), scatter_dimension=0, tiled=True),
        lax.psum_scatter(grad_fc1_bias, ("dp", "seq"), scatter_dimension=0, tiled=True),
        lax.psum_scatter(grad_fc2_bias, ("dp", "seq"), scatter_dimension=0, tiled=True),
        lax.psum_scatter(grad_lead_weight, ("dp", "seq"), scatter_dimension=0, tiled=True),
        lax.psum_scatter(grad_lead_bias, ("dp", "seq"), scatter_dimension=0, tiled=True),
    )
    return (block_output, input_grad) + tuple(summed)


def on_device(mesh_shape, tokens_in, lead_hours, cotangent, w_qkv, w_out, w_fc1, w_fc2, ln1_gain, ln1_bias, q_bias, v_bias,
              out_bias, ln2_gain, ln2_bias, fc1_bias, fc2_bias, lead_weight, lead_bias):
    _, R, D = tokens_in.shape
    FF = w_fc1.shape[1]
    hd = D // HEADS
    heads = HEADS // 4
    W = heads * hd
    rows = w_qkv.shape[0]
    vectors = (lead_weight, lead_bias, ln1_gain, ln1_bias, q_bias, v_bias, out_bias, ln2_gain, ln2_bias, fc2_bias, fc1_bias,
               lead_hours.astype(bf16))
    small = sum(lax.pad(v[None].astype(f32), f32(0), ((k, 31 - k, 0), (0, 128 - v.shape[0], 0))) for k, v in enumerate(vectors)).astype(bf16)
    normed, qkvT, oT, lse, own, vec, wT, a1, h1, a2, h2, a3, dob, mgrad, bo_a, bout_b, sums0 = forward_kernel(
        tokens_in, cotangent, w_qkv, small, w_fc1, w_fc2, w_out, heads, hd)[:17]
    o1, o2, o3, gq, hm, sums, bo_b = backward_kernel(
        dob, qkvT, oT, lse, a1, h1, a2, h2, a3.reshape(2, 4, 2, rows, D), normed, wT,
        own, vec, mgrad, sums0, bout_b, heads, hd)
    grad_fc1, grad_fc2, grad_out, grad_qkv, home, block_output, *small = results(
        o1, o2, o3, gq, hm, bo_a, bo_b, sums, rows, fc1_bias.shape[0])
    return (block_output, home, grad_qkv, grad_out, grad_fc1, grad_fc2) + tuple(v.reshape(-1) for v in small)


def choose(mesh_shape, *args):
    items, rows = args[0].shape[0], args[3].shape[0]
    planes = mesh_shape["seq"] // 2
    if items == 2 and planes == 2 * items and mesh_shape["dp"] == 4 and rows % 16 == 0 and 4 * args[0].shape[1] == args[0].shape[2]:
        return on_device(mesh_shape, *args)
    return spread_on_device(*args)


def solution(mesh):
    big, rows, vec = P("dp", "seq", None), P(("dp", "seq"), None), P(("dp", "seq"))
    in_specs = (big, P("dp"), big) + (rows,) * 4 + (vec,) * 11
    out_specs = (big, big) + (rows,) * 4 + (vec,) * 11
    body = functools.partial(choose, dict(mesh.shape))
    return jax.shard_map(body, mesh=mesh, in_specs=in_specs, out_specs=out_specs, check_vma=False)
```
